32 devices in a mesh: section: 2 (over core), dp: 16 (over z, y, x).
Axes of the slice: x: 2, y: 2, z: 4, core: 2. Of those that a mesh axis runs over, the one named last changes fastest.
Arguments:
- ends_in: bfloat16 [2, 2048, 768], P('section', 'dp'), may hold values from -6 to 6
- lengths: int32 [64, 3], P('dp'), may hold values from 1 to 16, 32 in all within a row
- norm_gain: float32 [2, 768], P('section'), may hold values from 0.1 to 1.9
- in_weight: bfloat16 [2, 768, 3072], P('section'), may hold values from -0.21875 to 0.21875
- conv_weight: float32 [2, 4, 1536], P('section'), may hold values from -3 to 3
- conv_bias: float32 [2, 1536], P('section'), may hold values from -3 to 3
- xproj_weight: bfloat16 [2, 1536, 80], P('section'), may hold values from -0.15625 to 0.15625
- dtproj_weight: bfloat16 [2, 48, 1536], P('section'), may hold values from -0.875 to 0.875
- dt_bias: float32 [2, 1536], P('section'), may hold values from -4 to -1
- a_log: float32 [2, 16, 1536], P('section'), may hold values from -1 to 2.77
- d_skip: float32 [2, 1536], P('section'), may hold values from 0.5 to 1.5
- out_weight: bfloat16 [2, 1536, 768], P('section'), may hold values from -0.3125 to 0.3125
Outputs:
- ends: float32 [2, 2048, 768], P('section', 'dp')
- grad_norm_gain: float32 [2, 768], P('section')
- grad_in_weight: float32 [2, 768, 3072], P('section')
- grad_conv_weight: float32 [2, 4, 1536], P('section')
- grad_conv_bias: float32 [2, 1536], P('section')
- grad_xproj_weight: float32 [2, 1536, 80], P('section')
- grad_dtproj_weight: float32 [2, 48, 1536], P('section')
- grad_dt_bias: float32 [2, 1536], P('section')
- grad_a_log: float32 [2, 16, 1536], P('section')
- grad_d_skip: float32 [2, 1536], P('section')
- grad_out_weight: float32 [2, 1536, 768], P('section')
The draws below stay inside these ranges and needn't reach their ends.
Inputs may be any that keep to these rules, and one draw needn't show every extreme that they name: Each row's lengths sum to 32; the longest of each row is exactly 16.
All inputs are finite; a program needn't handle non-finite values.
Results may differ from the reference program's by a relative error of at most 0.02.
Values may be sent and summed in bfloat16 or wider, within the bound.
No kernel may reach another device: no remote copies, remote signals or barrier semaphores. Data moves between devices by JAX's collectives and lax.ppermute only.
A program may use at most 256 MiB of HBM per device.

```python
import math
import jax
import jax.numpy as jnp
import numpy as np
from jax import lax

D = 768
E = 1536
NS = 16
RANK = 48
KC = 4
SEQ_MB = 3
MB_TOK = 32
SEQ_MOST = 16
BLOCKS = 64
TOKENS = 2048


def levels(rng, shape, split, smallest, high):
    factor_of = 1.0
    for position, shards_of in split:
        heights = jax.random.uniform(jax.random.fold_in(jax.random.fold_in(rng, 6), position), (shards_of,), jnp.float32, smallest / len(split), high / len(split))
        factor_of = factor_of * jnp.repeat(jnp.exp(heights), shape[position] // shards_of).reshape((-1,) + (1,) * (len(shape) - 1 - position))
    return factor_of


def profile(amount, total, bound, lean):
    portions = [(1 << 20) // math.isqrt(standing ** lean) + 1 for standing in range(2, amount + 1)]
    spare, given = total - bound - (amount - 1), [1] * (amount - 1)
    while spare > 0:
        movable = [i for i in range(amount - 1) if given[i] < bound]
        mass, remaining = sum([portions[i] for i in movable]), spare
        for i in movable:
            extra = min(bound - given[i], max(1, remaining * portions[i] // mass), spare)
            given[i] = given[i] + extra
            spare = spare - extra
    return np.array([bound] + given)


def ragged_sizes(own_key, amount, total, limit, lean):
    if amount == 2:
        one = jax.random.randint(own_key, (), max(1, total - limit), min(limit, total - 1) + 1)
        return jnp.stack([one, total - one])
    sizes = jnp.asarray(profile(amount, total, limit, lean), jnp.int32)
    couples = (amount - 1) // 2
    giver, sink = sizes[1:1 + 2 * couples:2], sizes[2:2 + 2 * couples:2]
    margin = jnp.minimum(giver - 1, limit - sink)
    moved = jax.random.randint(jax.random.fold_in(own_key, 1), (couples,), 0, 1 << 20) % (margin + 1)
    sizes = sizes.at[1:1 + 2 * couples:2].set(giver - moved).at[2:2 + 2 * couples:2].set(sink + moved)
    return sizes[jax.random.permutation(jax.random.fold_in(own_key, 2), amount)]


def bell_draw(key, shape, scale, bound, pieces=(), kind=jnp.bfloat16):
    entries = scale * jax.random.normal(key, shape, jnp.float32)
    if pieces:
        entries = entries * levels(key, shape, pieces, -0.22, 0.18)
    return jnp.clip(entries, -bound, bound).astype(kind)


def setup_inputs(seed: int = 0) -> dict:
    streams_of = jax.random.split(jax.random.key(seed), 13)
    ends_in = bell_draw(streams_of[0], (2, TOKENS, D), 1.0, 6.0, ((0, 2), (1, 16)))
    lengths = jax.vmap(lambda own: ragged_sizes(own, SEQ_MB, MB_TOK, SEQ_MOST, 0))(jax.random.split(streams_of[1], BLOCKS)).reshape((BLOCKS, SEQ_MB)).astype(jnp.int32)
    norm_gain = jnp.clip(1.0 + 0.18 * jax.random.normal(streams_of[2], (2, D), jnp.float32), 0.1, 1.9)
    in_weight = bell_draw(streams_of[3], (2, D, 2 * E), D ** -0.5, 0.21875, ((0, 2),))
    conv_weight = bell_draw(streams_of[4], (2, KC, E), KC ** -0.5, 3.0, ((0, 2),), jnp.float32)
    conv_bias = bell_draw(streams_of[5], (2, E), 0.5, 3.0, ((0, 2),), jnp.float32)
    xproj_weight = bell_draw(streams_of[6], (2, E, RANK + 2 * NS), E ** -0.5, 0.15625, ((0, 2),))
    dtproj_weight = bell_draw(streams_of[7], (2, RANK, E), RANK ** -0.5, 0.875, ((0, 2),))
    dt_bias = jnp.clip(-4.0 + 3.0 * jax.random.uniform(streams_of[8], (2, E), jnp.float32) ** levels(streams_of[8], (2, E), ((0, 2),), -0.2, 0.2), -4.0, -1.0)
    a_log = jnp.clip(-1.0 + 3.77 * jax.random.uniform(streams_of[9], (2, NS, E), jnp.float32) ** levels(streams_of[9], (2, NS, E), ((0, 2),), -0.2, 0.2), -1.0, 2.77)
    d_skip = jnp.clip(0.5 + 1.0 * jax.random.uniform(streams_of[10], (2, E), jnp.float32) ** levels(streams_of[10], (2, E), ((0, 2),), -0.2, 0.2), 0.5, 1.5)
    out_weight = bell_draw(streams_of[11], (2, E, D), (E // 4) ** -0.5, 0.3125, ((0, 2),))
    return dict(ends_in=ends_in, lengths=lengths, norm_gain=norm_gain, in_weight=in_weight, conv_weight=conv_weight, conv_bias=conv_bias, xproj_weight=xproj_weight, dtproj_weight=dtproj_weight, dt_bias=dt_bias, a_log=a_log, d_skip=d_skip, out_weight=out_weight)


epsilon = 1e-05
highest = lax.Precision.HIGHEST

@jax.custom_vjp
def low(v):
    return lax.optimization_barrier(v.astype(jnp.bfloat16)).astype(jnp.float32)

@jax.custom_vjp
def low_back(v):
    return v

def low_keep(v):
    return (low(v), None)

def low_pass(kept, grad):
    return (grad,)

def back_keep(v):
    return (v, None)

def back_low(kept, grad):
    return (low(grad),)
low.defvjp(low_keep, low_pass)
low_back.defvjp(back_keep, back_low)

def positions(lengths_row, count):
    ends_at = jnp.cumsum(lengths_row).astype(jnp.int32)
    starts = ends_at - lengths_row.astype(jnp.int32)
    index = jnp.arange(count, dtype=jnp.int32)
    before = jnp.where(index[:, None] >= starts[None, :], starts[None, :], jnp.int32(0))
    return (index - lax.optimization_barrier(jnp.max(before, axis=1))).astype(jnp.int32)

def mixer(residual, offset, gain, in_weight, conv_weight, conv_bias, xproj_weight, dtproj_weight, dt_bias, a_log, d_skip, out_weight):
    count = residual.shape[0]
    inner = in_weight.shape[1] // 2
    taps = conv_weight.shape[0]
    states = a_log.shape[0]
    rank = dtproj_weight.shape[0]
    normed = low(residual * lax.rsqrt(lax.optimization_barrier(jnp.mean(residual * residual, axis=1, keepdims=True)) + epsilon) * gain)
    both = low_back(jnp.dot(normed, in_weight, precision=highest))
    inner_x = both[:, :inner]
    gate_z = both[:, inner:]
    convolved = conv_bias + conv_weight[taps - 1] * inner_x
    for k in range(1, taps):
        shifted = jnp.concatenate([jnp.zeros((k, inner), jnp.float32), inner_x[:count - k]], axis=0)
        convolved = convolved + conv_weight[taps - 1 - k] * jnp.where((offset >= k)[:, None], shifted, 0.0)
    activated = low(jax.nn.silu(convolved))
    projected = low_back(jnp.dot(activated, xproj_weight, precision=highest))
    dt_low = low(projected[:, :rank])
    b_coef = projected[:, rank:rank + states]
    c_coef = projected[:, rank + states:]
    step_size = jax.nn.softplus(low_back(jnp.dot(dt_low, dtproj_weight, precision=highest)) + dt_bias)
    decay_rate = -jnp.exp(a_log)
    continued = (offset > 0).astype(jnp.float32)

    def advance(carried, inputs):
        size_t, act_t, b_t, c_t, cont_t = inputs
        carried = jnp.exp(size_t[None, :] * decay_rate) * carried * cont_t + b_t[:, None] * (size_t * act_t)[None, :]
        return (carried, lax.optimization_barrier(jnp.sum(c_t[:, None] * carried, axis=0)))
    start_state = jnp.zeros((states, inner), jnp.float32)
    _, scanned = lax.scan(advance, start_state, (step_size, activated, b_coef, c_coef, continued))
    gated = low((scanned + d_skip * activated) * jax.nn.silu(gate_z))
    return residual + low_back(jnp.dot(gated, out_weight, precision=highest))

def reference(ends_in, lengths, norm_gain, in_weight, conv_weight, conv_bias, xproj_weight, dtproj_weight, dt_bias, a_log, d_skip, out_weight):
    params = tuple((p.astype(jnp.float32) for p in (norm_gain, in_weight, conv_weight, conv_bias, xproj_weight, dtproj_weight, dt_bias, a_log, d_skip, out_weight)))
    blocks = lengths.shape[0]
    count = ends_in.shape[1] // blocks
    width = ends_in.shape[2]
    inputs = ends_in[0].astype(jnp.float32).reshape(blocks, count, width)
    cotangent = ends_in[1].astype(jnp.float32).reshape(blocks, count, width)
    offsets = jax.vmap(lambda row: positions(row, count))(lengths)

    def two_layers(block_in, offset, weights):
        first = mixer(block_in, offset, *[w[0] for w in weights])
        passed = low_back(low(first))
        return mixer(passed, offset, *[w[1] for w in weights])

    def whole(values, weights):
        return lax.map(lambda pair: jax.checkpoint(two_layers)(pair[0], pair[1], weights), (values, offsets))
    outputs, pull = jax.vjp(whole, inputs, params)
    grad_inputs, grads = pull(cotangent)
    ends = jnp.stack([grad_inputs.reshape(-1, width), outputs.reshape(-1, width)])
    return (ends, grads[0], grads[1], grads[2], grads[3], grads[4], grads[5], grads[6], grads[7], grads[8], grads[9])
```

```python
import jax
import jax.numpy as jnp
from jax import lax
from jax.experimental import pallas as pl
from jax.experimental.pallas import tpu as pltpu
from jax.sharding import PartitionSpec as P

EPSILON = 1e-05
LOG2E = 1.4426950408889634
LN2 = 0.6931471805599453
CUT = 1e6
LANES = 128
WIDE = 512
GROUP = 8

bf16, f32 = jnp.bfloat16, jnp.float32


def nn(a, b):
    return jnp.dot(a, b, preferred_element_type=f32)


def nt(a, b):
    return lax.dot_general(a, b, (((1,), (1,)), ((), ())), preferred_element_type=f32)


def tn(a, b):
    return lax.dot_general(a, b, (((0,), (0,)), ((), ())), preferred_element_type=f32)


def sigmoid(v):
    return 1.0 / (1.0 + jnp.exp(-v))


def make_layers_kernel(tokens, width, e, states, taps, rank):
    steps_wide = e // WIDE
    tiles = WIDE // LANES
    low_rows = rank + 2 * states
    AL, CW, CB, DB, DS, GN = 0, states, states + taps, states + taps + 1, states + taps + 2, states + taps + 3
    GX, GD = 0, low_rows
    GA = GD + rank
    GC = GA + states
    GB, GT, GS, GG = GC + taps, GC + taps + 1, GC + taps + 2, GC + taps + 3

    def wide(i, base=0):
        return pl.ds(pl.multiple_of(i * WIDE + base, WIDE), WIDE)

    def tile(i, k):
        return pl.ds(pl.multiple_of(i * WIDE + k * LANES, LANES), LANES)

    def of_state(t):
        return pl.ds(pl.multiple_of(t * states, states), states)

    def grouped(value):
        return value.reshape(tokens // GROUP, GROUP, value.shape[1])

    def flat(value):
        return value.reshape(tokens, value.shape[2])

    def kernel(
        sec, lengths, x_in, cot_in, small,
        in_own, in_recv, xd_own, xd_recv, out_own, out_recv,
        out_o, gin_o, normed_o, both_o, gated_o, outg_o, grads_o,
        in_w, xd_w, out_w, sems, offs,
        resid, norm_r, inner, gate, conv, act, size, step, sig, yscan, uin, low_t, bb, cb, rate, hist,
        dyscan, dact, dsz, dtg, acc_b, acc_c, pg_t, upstream,
    ):
        me = sec[0]
        weights = ((in_own, in_recv, in_w), (xd_own, xd_recv, xd_w), (out_own, out_recv, out_w))
        for l in range(2):
            for k, (own, recv, dst) in enumerate(weights):
                @pl.when(me == l)
                def _(own=own, dst=dst, l=l, k=k):
                    pltpu.make_async_copy(own, dst.at[l], sems.at[l, k]).start()

                @pl.when(me != l)
                def _(recv=recv, dst=dst, l=l, k=k):
                    pltpu.make_async_copy(recv, dst.at[l], sems.at[l, k]).start()

        def arrived(l, k):
            own, _, dst = weights[k]
            pltpu.make_async_copy(own, dst.at[l], sems.at[l, k]).wait()

        micro = lengths.shape[0]
        count = tokens // micro
        row = lax.broadcasted_iota(jnp.int32, (tokens, LANES), 0)
        begin = jnp.zeros_like(row)
        for m in range(micro):
            a = lengths[m, 0] + m * count
            b = a + lengths[m, 1]
            begin = jnp.where(row >= m * count, m * count, begin)
            begin = jnp.where(row >= a, a, begin)
            begin = jnp.where(row >= b, b, begin)
        offs[...] = row - begin

        def keep(k):
            return jnp.concatenate([offs[...]] * tiles, axis=1) >= k

        for l in range(2):
            hist[l, 0:states, :] = jnp.zeros((states, e), f32)
        resid[0] = x_in[...].astype(f32)
        upstream[...] = cot_in[...].astype(f32)

        def forward(l, _):
            x = resid[l]
            r = lax.rsqrt(jnp.mean(x * x, axis=1, keepdims=True) + EPSILON)
            norm_r[l] = jnp.broadcast_to(r, (tokens, LANES))
            normed_o[l] = (x * r * small[l, GN:GN + 1, 0:width]).astype(bf16)
            arrived(l, 0)

            def project(i, _):
                c = wide(i)
                v = nn(normed_o[l], in_w[l, :, c])
                inner[l, :, c] = v
                gate[l, :, c] = nn(normed_o[l], in_w[l, :, wide(i, e)])
                total = small[l, CB:CB + 1, c] + small[l, CW + taps - 1:CW + taps, c] * v
                for k in range(1, taps):
                    before = jnp.where(keep(k), pltpu.roll(v, k, 0), 0.0)
                    total = total + small[l, CW + taps - 1 - k:CW + taps - k, c] * before
                conv[l, :, c] = total
                act[l, :, c] = (total * sigmoid(total)).astype(bf16)
                return 0

            lax.fori_loop(0, steps_wide, project, 0)
            arrived(l, 1)
            a = act[l]
            low = nt(a, xd_w[l, 0:rank, :]).astype(bf16)
            proj_t = nt(xd_w[l, 0:low_rows, :], a)
            low_t[l] = proj_t[0:rank].astype(bf16)
            for t in range(tokens):
                here = slice(t * states, (t + 1) * states)
                bb[l, here, :] = jnp.broadcast_to(proj_t[rank:rank + states, t:t + 1], (states, LANES))
                cb[l, here, :] = jnp.broadcast_to(proj_t[rank + states:, t:t + 1], (states, LANES))
            rate[l] = -jnp.exp(small[l, AL:AL + states, :]) * LOG2E

            def scan(i, _):
                c = wide(i)
                v = nn(low, xd_w[l, low_rows:low_rows + rank, c]) + small[l, DB:DB + 1, c]
                shrunk = jnp.exp(-jnp.abs(v))
                s = jnp.maximum(v, 0.0) + jnp.log1p(shrunk)
                inverse = 1.0 / (1.0 + shrunk)
                sig[l, :, c] = jnp.where(v >= 0, inverse, shrunk * inverse)
                step[l, :, c] = s
                uin[l, :, :, c] = grouped(s * act[l, :, c].astype(f32))
                size[l, :, :, c] = grouped(jnp.where(keep(1), s, CUT))
                rates = [rate[l, :, tile(i, k)] for k in range(tiles)]

                def group(g, h):
                    h = list(h)
                    for j in range(GROUP):
                        t = g * GROUP + j
                        bt, ct = bb[l, of_state(t), :], cb[l, of_state(t), :]
                        for k in range(tiles):
                            f = jnp.exp2(size[l, g, j:j + 1, tile(i, k)] * rates[k])
                            h[k] = f * h[k] + bt * uin[l, g, j:j + 1, tile(i, k)]
                            hist[l, of_state(t + 1), tile(i, k)] = h[k]
                            yscan[l, g, j:j + 1, tile(i, k)] = jnp.sum(ct * h[k], axis=0, keepdims=True)
                    return tuple(h)

                none = tuple(jnp.zeros((states, LANES), f32) for _ in range(tiles))
                lax.fori_loop(0, tokens // GROUP, group, none)
                z = gate[l, :, c]
                p = flat(yscan[l, :, :, c]) + small[l, DS:DS + 1, c] * act[l, :, c].astype(f32)
                gated_o[l, :, c] = (p * (z * sigmoid(z))).astype(bf16)
                return 0

            lax.fori_loop(0, steps_wide, scan, 0)
            arrived(l, 2)
            result = x + nn(gated_o[l], out_w[l])
            out_o[...] = result
            resid[l + 1] = result.astype(bf16).astype(f32)
            return 0

        lax.fori_loop(0, 2, forward, 0)

        def backward(back, _):
            l = 1 - back
            outg_o[l] = upstream[...].astype(bf16)
            acc_b[...] = jnp.zeros_like(acc_b)
            acc_c[...] = jnp.zeros_like(acc_c)

            def scan(i, _):
                c = wide(i)
                from_out = nt(outg_o[l], out_w[l, c, :])
                a = act[l, :, c].astype(f32)
                z = gate[l, :, c]
                s = sigmoid(z)
                p = flat(yscan[l, :, :, c]) + small[l, DS:DS + 1, c] * a
                dp = from_out * (z * s)
                dyscan[:, :, c] = grouped(dp)
                both_o[l, :, wide(i, e)] = (from_out * p * (s * (1.0 + z * (1.0 - s)))).astype(bf16)
                grads_o[l, GS:GS + 1, c] = jnp.sum(dp * a, axis=0, keepdims=True)
                rates = [rate[l, :, tile(i, k)] for k in range(tiles)]

                def group(backwards, carried):
                    carry, now, drate = (list(v) for v in carried)
                    g = tokens // GROUP - 1 - backwards
                    for j in reversed(range(GROUP)):
                        t = g * GROUP + j
                        bt, ct = bb[l, of_state(t), :], cb[l, of_state(t), :]
                        sum_b = sum_c = None
                        for k in range(tiles):
                            sz = size[l, g, j:j + 1, tile(i, k)]
                            dy = dyscan[g, j:j + 1, tile(i, k)]
                            grad = carry[k] + ct * dy
                            part_b = grad * uin[l, g, j:j + 1, tile(i, k)]
                            part_c = now[k] * dy
                            sum_b = part_b if sum_b is None else sum_b + part_b
                            sum_c = part_c if sum_c is None else sum_c + part_c
                            dact[g, j:j + 1, tile(i, k)] = jnp.sum(bt * grad, axis=0, keepdims=True)
                            carry[k] = jnp.exp2(sz * rates[k]) * grad
                            now[k] = hist[l, of_state(t), tile(i, k)]
                            w = carry[k] * now[k]
                            dsz[g, j:j + 1, tile(i, k)] = jnp.sum(w * rates[k], axis=0, keepdims=True)
                            drate[k] = drate[k] + sz * w
                        acc_b[of_state(t), :] += sum_b
                        acc_c[of_state(t), :] += sum_c
                    return tuple(carry), tuple(now), tuple(drate)

                none = tuple(jnp.zeros((states, LANES), f32) for _ in range(tiles))
                final = tuple(hist[l, of_state(tokens), tile(i, k)] for k in range(tiles))
                _, _, drate = lax.fori_loop(0, tokens // GROUP, group, (none, final, none))
                for k in range(tiles):
                    grads_o[l, GA:GA + states, tile(i, k)] = drate[k] * (rates[k] * LN2)
                du = flat(dact[:, :, c])
                dv = (flat(dsz[:, :, c]) * LN2 + du * a) * sig[l, :, c]
                dact[:, :, c] = grouped(du * step[l, :, c] + dp * small[l, DS:DS + 1, c])
                dtg[:, c] = dv.astype(bf16)
                grads_o[l, GT:GT + 1, c] = jnp.sum(dv, axis=0, keepdims=True)
                return 0

            lax.fori_loop(0, steps_wide, scan, 0)
            lane = lax.broadcasted_iota(jnp.int32, (states, LANES), 1)
            db = jnp.zeros((states, LANES), f32)
            dc = jnp.zeros((states, LANES), f32)
            for t in range(tokens):
                here = slice(t * states, (t + 1) * states)
                db = jnp.where(lane == t, jnp.sum(acc_b[here, :], axis=1, keepdims=True), db)
                dc = jnp.where(lane == t, jnp.sum(acc_c[here, :], axis=1, keepdims=True), dc)
            pg_t[0:rank, :] = nt(xd_w[l, low_rows:low_rows + rank, :], dtg[...]).astype(bf16)
            pg_t[rank:rank + states, :] = db[:, 0:tokens].astype(bf16)
            pg_t[rank + states:low_rows, :] = dc[:, 0:tokens].astype(bf16)

            def conv_back(i, _):
                c = wide(i)
                grads_o[l, GX:GX + low_rows, c] = nn(pg_t[...], act[l, :, c])
                grads_o[l, GD:GD + rank, c] = nn(low_t[l], dtg[:, c])
                da = tn(pg_t[...], xd_w[l, 0:low_rows, c]) + flat(dact[:, :, c])
                total = conv[l, :, c]
                s = sigmoid(total)
                dv = da * (s * (1.0 + total * (1.0 - s)))
                v = inner[l, :, c]
                grads_o[l, GB:GB + 1, c] = jnp.sum(dv, axis=0, keepdims=True)
                grads_o[l, GC + taps - 1:GC + taps, c] = jnp.sum(dv * v, axis=0, keepdims=True)
                dinner = small[l, CW + taps - 1:CW + taps, c] * dv
                for k in range(1, taps):
                    kept = jnp.where(keep(k), dv, 0.0)
                    grads_o[l, GC + taps - 1 - k:GC + taps - k, c] = jnp.sum(
                        kept * pltpu.roll(v, k, 0), axis=0, keepdims=True
                    )
                    dinner = dinner + small[l, CW + taps - 1 - k:CW + taps - k, c] * pltpu.roll(kept, tokens - k, 0)
                both_o[l, :, c] = dinner.astype(bf16)
                return 0

            lax.fori_loop(0, steps_wide, conv_back, 0)
            dn = nt(both_o[l], in_w[l])
            x = resid[l]
            r = norm_r[l][:, 0:1]
            xr = x * r
            grads_o[l, GG:GG + 1, :] = jnp.zeros((1, e), f32)
            grads_o[l, GG:GG + 1, 0:width] = jnp.sum(dn * xr, axis=0, keepdims=True)
            dxr = dn * small[l, GN:GN + 1, 0:width]
            grad_in = upstream[...] + r * (dxr - xr * jnp.mean(dxr * xr, axis=1, keepdims=True))
            gin_o[...] = grad_in
            upstream[...] = grad_in.astype(bf16).astype(f32)
            return 0

        lax.fori_loop(0, 2, backward, 0)

    grad_rows = GG + 1
    param_rows = GN + 1
    return kernel, grad_rows, param_rows


def run_layers(section, lengths, x, cot, small, in_own, in_recv, xd_own, xd_recv, out_own, out_recv, states, taps, rank):
    tokens, width = x.shape
    e = out_own.shape[0]
    kernel, grad_rows, _ = make_layers_kernel(tokens, width, e, states, taps, rank)
    shaped = jax.ShapeDtypeStruct
    vmem = pl.BlockSpec(memory_space=pltpu.VMEM)
    smem = pl.BlockSpec(memory_space=pltpu.SMEM)
    anywhere = pl.BlockSpec(memory_space=pl.ANY)
    V = pltpu.VMEM
    outs = (
        shaped((tokens, width), f32),
        shaped((tokens, width), f32),
        shaped((2, tokens, width), bf16),
        shaped((2, tokens, 2 * e), bf16),
        shaped((2, tokens, e), bf16),
        shaped((2, tokens, width), bf16),
        shaped((2, grad_rows, e), f32),
    )
    by_token = lambda kind: V((2, tokens, e), kind)
    by_row = lambda *lead: V(lead + (tokens // GROUP, GROUP, e), f32)
    return pl.pallas_call(
        kernel,
        out_shape=outs,
        in_specs=[smem, smem, vmem, vmem, vmem] + [anywhere] * 6,
        out_specs=(vmem,) * len(outs),
        scratch_shapes=[
            V((2,) + in_own.shape, bf16), V((2,) + xd_own.shape, bf16), V((2,) + out_own.shape, bf16),
            pltpu.SemaphoreType.DMA((2, 3)), V((tokens, LANES), jnp.int32),
            V((3, tokens, width), f32), V((2, tokens, LANES), f32),
            by_token(f32), by_token(f32), by_token(f32), by_token(bf16),
            by_row(2), by_token(f32), by_token(f32), by_row(2), by_row(2),
            V((2, rank, tokens), bf16),
            V((2, tokens * states, LANES), f32), V((2, tokens * states, LANES), f32),
            V((2, states, e), f32), V((2, (tokens + 1) * states, e), f32),
            by_row(), by_row(), by_row(), V((tokens, e), bf16),
            V((tokens * states, LANES), f32), V((tokens * states, LANES), f32),
            V((rank + 2 * states, tokens), bf16), V((tokens, width), f32),
        ],
        compiler_params=pltpu.CompilerParams(vmem_limit_bytes=58 * 1024 * 1024),
        name="layers",
    )(section, lengths, x, cot, small, in_own, in_recv, xd_own, xd_recv, out_own, out_recv)


def per_device(
    ends_in, lengths, norm_gain, in_weight, conv_weight, conv_bias, xproj_weight,
    dtproj_weight, dt_bias, a_log, d_skip, out_weight,
):
    section = lax.axis_index("section")
    first = section == 0
    width, e = norm_gain.shape[1], conv_bias.shape[1]
    states, taps, rank = a_log.shape[1], conv_weight.shape[1], dtproj_weight.shape[1]
    rows = ends_in.shape[1]
    half = rows // 2
    micro = lengths.shape[0]
    swap = [(0, 1), (1, 0)]

    def across(array):
        return lax.ppermute(array, "section", swap)

    small_own = jnp.concatenate(
        [
            a_log[0], conv_weight[0], conv_bias, dt_bias, d_skip,
            jnp.pad(norm_gain, ((0, 0), (0, e - width))),
        ],
        axis=0,
    )
    xd_own = jnp.concatenate([xproj_weight[0].T, dtproj_weight[0]], axis=0)
    halves = ends_in[0].reshape(2, half, width)
    mine = lax.dynamic_index_in_dim(halves, section, 0, keepdims=False)
    theirs = lax.dynamic_index_in_dim(halves, 1 - section, 0, keepdims=False)
    in_recv = across(in_weight[0])
    ends_recv = across(theirs)
    small_recv = across(small_own)
    xd_recv = across(xd_own)
    out_recv = across(out_weight[0])
    small = jnp.where(first, jnp.stack([small_own, small_recv]), jnp.stack([small_recv, small_own]))
    x = jnp.where(first, mine, ends_recv)
    cot = jnp.where(first, ends_recv, mine)
    my_lengths = lax.dynamic_slice_in_dim(lengths, section * (micro // 2), micro // 2, 0)
    out, gin, normed, both, gated, outg, grads = run_layers(
        section.astype(jnp.int32).reshape(1), my_lengths, x, cot, small,
        in_weight[0], in_recv, xd_own, xd_recv, out_weight[0], out_recv, states, taps, rank,
    )
    kept = jnp.where(first, gin, out)
    came = across(jnp.where(first, out, gin))
    ends = jnp.where(first, jnp.concatenate([kept, came]), jnp.concatenate([came, kept]))[None]

    def pick(array):
        own = lax.dynamic_index_in_dim(array, section, 0, keepdims=False)
        other = across(lax.dynamic_index_in_dim(array, 1 - section, 0, keepdims=False))
        return jnp.concatenate([own, other], axis=0)

    normed, both, gated, outg = pick(normed), pick(both), pick(gated), pick(outg)
    grads = pick(grads[:, None]).sum(0)
    grad_in, grad_out, grads = lax.psum(
        (tn(normed, both).astype(bf16), tn(gated, outg).astype(bf16), grads.astype(bf16)), "dp"
    )
    grads = grads.astype(f32)
    low_rows = rank + 2 * states
    at = [low_rows, low_rows + rank]
    at += [at[-1] + states]
    at += [at[-1] + taps]
    return (
        ends,
        grads[-1:, :width],
        grad_in.astype(f32)[None],
        grads[at[2]:at[3]][None],
        grads[at[3]:at[3] + 1],
        grads[0:at[0]].T[None],
        grads[at[0]:at[1]][None],
        grads[at[3] + 1:at[3] + 2],
        grads[at[1]:at[2]][None],
        grads[at[3] + 2:at[3] + 3],
        grad_out.astype(f32)[None],
    )


def solution(mesh):
    in_specs = (
        P("section", "dp", None), P("dp", None), P("section", None), P("section", None, None),
        P("section", None, None), P("section", None), P("section", None, None), P("section", None, None),
        P("section", None), P("section", None, None), P("section", None), P("section", None, None),
    )
    out_specs = (
        P("section", "dp", None), P("section", None), P("section", None, None), P("section", None, None),
        P("section", None), P("section", None, None), P("section", None, None), P("section", None),
        P("section", None, None), P("section", None), P("section", None, None),
    )
    return jax.shard_map(per_device, mesh=mesh, in_specs=in_specs, out_specs=out_specs, check_vma=False)
```

```python
import jax
import jax.numpy as jnp
from jax import lax
from jax.experimental import pallas as pl
from jax.experimental.pallas import tpu as pltpu
from jax.sharding import PartitionSpec as P

EPSILON = 1e-05
LOG2E = 1.4426950408889634
LN2 = 0.6931471805599453
CUT = 1e6
LANES = 128
WIDE = 512
GROUP = 8

bf16, f32 = jnp.bfloat16, jnp.float32


def nn(a, b):
    return jnp.dot(a, b, preferred_element_type=f32)


def nt(a, b):
    return lax.dot_general(a, b, (((1,), (1,)), ((), ())), preferred_element_type=f32)


def tn(a, b):
    return lax.dot_general(a, b, (((0,), (0,)), ((), ())), preferred_element_type=f32)


def sigmoid(v):
    return 1.0 / (1.0 + jnp.exp(-v))


def make_layers_kernel(tokens, width, e, states, taps, rank):
    steps_wide = e // WIDE
    tiles = WIDE // LANES
    low_rows = rank + 2 * states
    AL, CW, CB, DB, DS, GN = 0, states, states + taps, states + taps + 1, states + taps + 2, states + taps + 3
    GX, GD = 0, low_rows
    GA = GD + rank
    GC = GA + states
    GB, GT, GS, GG = GC + taps, GC + taps + 1, GC + taps + 2, GC + taps + 3

    NORMED, BOTH = slice(0, width), width
    GATED, OUTG = width + 2 * e, width + 3 * e

    def wide(i, base=0):
        return pl.ds(pl.multiple_of(i * WIDE + base, LANES), WIDE)

    def tile(i, k):
        return pl.ds(pl.multiple_of(i * WIDE + k * LANES, LANES), LANES)

    def of_state(t):
        return pl.ds(pl.multiple_of(t * states, states), states)

    def grouped(value):
        return value.reshape(tokens // GROUP, GROUP, value.shape[1])

    def flat(value):
        return value.reshape(tokens, value.shape[2])

    def kernel(
        sec, lengths, x_in, cot_in, small,
        in_own, in_recv, xd_own, xd_recv, out_own, out_recv,
        out_o, gin_o, fac_own, fac_other, grads_own, grads_other,
        fac, grads_o, in_w, xd_w, out_w, sems, offs,
        resid, norm_r, inner, gate, conv, act, size, step, sig, yscan, uin, low_t, bb, cb, rate, hist,
        dyscan, dact, dsz, dtg, acc_b, acc_c, pg_t, upstream,
    ):
        me = sec[0]
        weights = ((in_own, in_recv, in_w), (xd_own, xd_recv, xd_w), (out_own, out_recv, out_w))
        for l in range(2):
            for k, (own, recv, dst) in enumerate(weights):
                @pl.when(me == l)
                def _(own=own, dst=dst, l=l, k=k):
                    pltpu.make_async_copy(own, dst.at[l], sems.at[l, k]).start()

                @pl.when(me != l)
                def _(recv=recv, dst=dst, l=l, k=k):
                    pltpu.make_async_copy(recv, dst.at[l], sems.at[l, k]).start()

        def arrived(l, k):
            own, _, dst = weights[k]
            pltpu.make_async_copy(own, dst.at[l], sems.at[l, k]).wait()

        micro = lengths.shape[0]
        count = tokens // micro
        row = lax.broadcasted_iota(jnp.int32, (tokens, LANES), 0)
        begin = jnp.zeros_like(row)
        for m in range(micro):
            a = lengths[m, 0] + m * count
            b = a + lengths[m, 1]
            begin = jnp.where(row >= m * count, m * count, begin)
            begin = jnp.where(row >= a, a, begin)
            begin = jnp.where(row >= b, b, begin)
        offs[...] = row - begin

        def keep(k):
            return jnp.concatenate([offs[...]] * tiles, axis=1) >= k

        for l in range(2):
            hist[l, 0:states, :] = jnp.zeros((states, e), f32)
        resid[0] = x_in[...].astype(f32)
        upstream[...] = cot_in[...].astype(f32)

        def forward(l, _):
            x = resid[l]
            r = lax.rsqrt(jnp.mean(x * x, axis=1, keepdims=True) + EPSILON)
            norm_r[l] = jnp.broadcast_to(r, (tokens, LANES))
            fac[l, :, NORMED] = (x * r * small[l, GN:GN + 1, 0:width]).astype(bf16)
            arrived(l, 0)

            def project(i, _):
                c = wide(i)
                v = nn(fac[l, :, NORMED], in_w[l, :, c])
                inner[l, :, c] = v
                gate[l, :, c] = nn(fac[l, :, NORMED], in_w[l, :, wide(i, e)])
                total = small[l, CB:CB + 1, c] + small[l, CW + taps - 1:CW + taps, c] * v
                for k in range(1, taps):
                    before = jnp.where(keep(k), pltpu.roll(v, k, 0), 0.0)
                    total = total + small[l, CW + taps - 1 - k:CW + taps - k, c] * before
                conv[l, :, c] = total
                act[l, :, c] = (total * sigmoid(total)).astype(bf16)
                return 0

            lax.fori_loop(0, steps_wide, project, 0)
            arrived(l, 1)
            a = act[l]
            low = nt(a, xd_w[l, 0:rank, :]).astype(bf16)
            proj_t = nt(xd_w[l, 0:low_rows, :], a)
            low_t[l] = proj_t[0:rank].astype(bf16)
            for t in range(tokens):
                here = slice(t * states, (t + 1) * states)
                bb[l, here, :] = jnp.broadcast_to(proj_t[rank:rank + states, t:t + 1], (states, LANES))
                cb[l, here, :] = jnp.broadcast_to(proj_t[rank + states:, t:t + 1], (states, LANES))
            rate[l] = -jnp.exp(small[l, AL:AL + states, :]) * LOG2E

            def scan(i, _):
                c = wide(i)
                v = nn(low, xd_w[l, low_rows:low_rows + rank, c]) + small[l, DB:DB + 1, c]
                shrunk = jnp.exp(-jnp.abs(v))
                s = jnp.maximum(v, 0.0) + jnp.log1p(shrunk)
                inverse = 1.0 / (1.0 + shrunk)
                sig[l, :, c] = jnp.where(v >= 0, inverse, shrunk * inverse)
                step[l, :, c] = s
                uin[l, :, :, c] = grouped(s * act[l, :, c].astype(f32))
                size[l, :, :, c] = grouped(jnp.where(keep(1), s, CUT))
                rates = [rate[l, :, tile(i, k)] for k in range(tiles)]

                def group(g, h):
                    h = list(h)
                    for j in range(GROUP):
                        t = g * GROUP + j
                        bt, ct = bb[l, of_state(t), :], cb[l, of_state(t), :]
                        for k in range(tiles):
                            f = jnp.exp2(size[l, g, j:j + 1, tile(i, k)] * rates[k])
                            h[k] = f * h[k] + bt * uin[l, g, j:j + 1, tile(i, k)]
                            hist[l, of_state(t + 1), tile(i, k)] = h[k]
                            yscan[l, g, j:j + 1, tile(i, k)] = jnp.sum(ct * h[k], axis=0, keepdims=True)
                    return tuple(h)

                none = tuple(jnp.zeros((states, LANES), f32) for _ in range(tiles))
                lax.fori_loop(0, tokens // GROUP, group, none)
                z = gate[l, :, c]
                p = flat(yscan[l, :, :, c]) + small[l, DS:DS + 1, c] * act[l, :, c].astype(f32)
                fac[l, :, wide(i, GATED)] = (p * (z * sigmoid(z))).astype(bf16)
                return 0

            lax.fori_loop(0, steps_wide, scan, 0)
            arrived(l, 2)
            result = x + nn(fac[l, :, GATED:GATED + e], out_w[l])
            out_o[...] = result
            resid[l + 1] = result.astype(bf16).astype(f32)
            return 0

        lax.fori_loop(0, 2, forward, 0)

        def backward(back, _):
            l = 1 - back
            fac[l, :, OUTG:OUTG + width] = upstream[...].astype(bf16)
            acc_b[...] = jnp.zeros_like(acc_b)
            acc_c[...] = jnp.zeros_like(acc_c)
            rest = grads_o.shape[1] - GG
            grads_o[l, GG:, :] = jnp.zeros((rest, e), f32)

            def scan(i, _):
                c = wide(i)
                from_out = nt(fac[l, :, OUTG:OUTG + width], out_w[l, c, :])
                a = act[l, :, c].astype(f32)
                z = gate[l, :, c]
                s = sigmoid(z)
                p = flat(yscan[l, :, :, c]) + small[l, DS:DS + 1, c] * a
                dp = from_out * (z * s)
                dyscan[:, :, c] = grouped(dp)
                fac[l, :, wide(i, BOTH + e)] = (from_out * p * (s * (1.0 + z * (1.0 - s)))).astype(bf16)
                grads_o[l, GS:GS + 1, c] = jnp.sum(dp * a, axis=0, keepdims=True)
                rates = [rate[l, :, tile(i, k)] for k in range(tiles)]

                def group(backwards, carried):
                    carry, now, drate = (list(v) for v in carried)
                    g = tokens // GROUP - 1 - backwards
                    for j in reversed(range(GROUP)):
                        t = g * GROUP + j
                        bt, ct = bb[l, of_state(t), :], cb[l, of_state(t), :]
                        sum_b = sum_c = None
                        for k in range(tiles):
                            sz = size[l, g, j:j + 1, tile(i, k)]
                            dy = dyscan[g, j:j + 1, tile(i, k)]
                            grad = carry[k] + ct * dy
                            part_b = grad * uin[l, g, j:j + 1, tile(i, k)]
                            part_c = now[k] * dy
                            sum_b = part_b if sum_b is None else sum_b + part_b
                            sum_c = part_c if sum_c is None else sum_c + part_c
                            dact[g, j:j + 1, tile(i, k)] = jnp.sum(bt * grad, axis=0, keepdims=True)
                            carry[k] = jnp.exp2(sz * rates[k]) * grad
                            now[k] = hist[l, of_state(t), tile(i, k)]
                            w = carry[k] * now[k]
                            dsz[g, j:j + 1, tile(i, k)] = jnp.sum(w * rates[k], axis=0, keepdims=True)
                            drate[k] = drate[k] + sz * w
                        acc_b[of_state(t), :] += sum_b
                        acc_c[of_state(t), :] += sum_c
                    return tuple(carry), tuple(now), tuple(drate)

                none = tuple(jnp.zeros((states, LANES), f32) for _ in range(tiles))
                final = tuple(hist[l, of_state(tokens), tile(i, k)] for k in range(tiles))
                _, _, drate = lax.fori_loop(0, tokens // GROUP, group, (none, final, none))
                for k in range(tiles):
                    grads_o[l, GA:GA + states, tile(i, k)] = drate[k] * (rates[k] * LN2)
                du = flat(dact[:, :, c])
                dv = (flat(dsz[:, :, c]) * LN2 + du * a) * sig[l, :, c]
                dact[:, :, c] = grouped(du * step[l, :, c] + dp * small[l, DS:DS + 1, c])
                dtg[:, c] = dv.astype(bf16)
                grads_o[l, GT:GT + 1, c] = jnp.sum(dv, axis=0, keepdims=True)
                return 0

            lax.fori_loop(0, steps_wide, scan, 0)
            lane = lax.broadcasted_iota(jnp.int32, (states, LANES), 1)
            db = jnp.zeros((states, LANES), f32)
            dc = jnp.zeros((states, LANES), f32)
            for t in range(tokens):
                here = slice(t * states, (t + 1) * states)
                db = jnp.where(lane == t, jnp.sum(acc_b[here, :], axis=1, keepdims=True), db)
                dc = jnp.where(lane == t, jnp.sum(acc_c[here, :], axis=1, keepdims=True), dc)
            pg_t[0:rank, :] = nt(xd_w[l, low_rows:low_rows + rank, :], dtg[...]).astype(bf16)
            pg_t[rank:rank + states, :] = db[:, 0:tokens].astype(bf16)
            pg_t[rank + states:low_rows, :] = dc[:, 0:tokens].astype(bf16)

            def conv_back(i, _):
                c = wide(i)
                grads_o[l, GX:GX + low_rows, c] = nn(pg_t[...], act[l, :, c])
                grads_o[l, GD:GD + rank, c] = nn(low_t[l], dtg[:, c])
                da = tn(pg_t[...], xd_w[l, 0:low_rows, c]) + flat(dact[:, :, c])
                total = conv[l, :, c]
                s = sigmoid(total)
                dv = da * (s * (1.0 + total * (1.0 - s)))
                v = inner[l, :, c]
                grads_o[l, GB:GB + 1, c] = jnp.sum(dv, axis=0, keepdims=True)
                grads_o[l, GC + taps - 1:GC + taps, c] = jnp.sum(dv * v, axis=0, keepdims=True)
                dinner = small[l, CW + taps - 1:CW + taps, c] * dv
                for k in range(1, taps):
                    kept = jnp.where(keep(k), dv, 0.0)
                    grads_o[l, GC + taps - 1 - k:GC + taps - k, c] = jnp.sum(
                        kept * pltpu.roll(v, k, 0), axis=0, keepdims=True
                    )
                    dinner = dinner + small[l, CW + taps - 1 - k:CW + taps - k, c] * pltpu.roll(kept, tokens - k, 0)
                fac[l, :, wide(i, BOTH)] = dinner.astype(bf16)
                return 0

            lax.fori_loop(0, steps_wide, conv_back, 0)
            dn = nt(fac[l, :, BOTH:GATED], in_w[l])
            x = resid[l]
            r = norm_r[l][:, 0:1]
            xr = x * r
            grads_o[l, GG:GG + 1, 0:width] = jnp.sum(dn * xr, axis=0, keepdims=True)
            dxr = dn * small[l, GN:GN + 1, 0:width]
            grad_in = upstream[...] + r * (dxr - xr * jnp.mean(dxr * xr, axis=1, keepdims=True))
            gin_o[...] = grad_in
            upstream[...] = grad_in.astype(bf16).astype(f32)
            return 0

        lax.fori_loop(0, 2, backward, 0)
        fac_own[...] = fac[me]
        fac_other[...] = fac[1 - me]
        grads_own[...] = grads_o[me]
        grads_other[...] = grads_o[1 - me]

    grad_rows = (GG + 1 + 63) // 64 * 64
    param_rows = GN + 1
    return kernel, grad_rows, param_rows


def run_layers(section, lengths, x, cot, small, in_own, in_recv, xd_own, xd_recv, out_own, out_recv, states, taps, rank):
    tokens, width = x.shape
    e = out_own.shape[0]
    kernel, grad_rows, _ = make_layers_kernel(tokens, width, e, states, taps, rank)
    shaped = jax.ShapeDtypeStruct
    vmem = pl.BlockSpec(memory_space=pltpu.VMEM)
    smem = pl.BlockSpec(memory_space=pltpu.SMEM)
    anywhere = pl.BlockSpec(memory_space=pl.ANY)
    V = pltpu.VMEM
    outs = (
        shaped((tokens, width), f32),
        shaped((tokens, width), f32),
        shaped((tokens, 2 * width + 3 * e), bf16),
        shaped((tokens, 2 * width + 3 * e), bf16),
        shaped((grad_rows, e), f32),
        shaped((grad_rows, e), f32),
    )
    by_token = lambda kind: V((2, tokens, e), kind)
    by_row = lambda *lead: V(lead + (tokens // GROUP, GROUP, e), f32)
    return pl.pallas_call(
        kernel,
        out_shape=outs,
        in_specs=[smem, smem, vmem, vmem, vmem] + [anywhere] * 6,
        out_specs=(vmem,) * len(outs),
        scratch_shapes=[
            V((2, tokens, 2 * width + 3 * e), bf16), V((2, grad_rows, e), f32),
            V((2,) + in_own.shape, bf16), V((2,) + xd_own.shape, bf16), V((2,) + out_own.shape, bf16),
            pltpu.SemaphoreType.DMA((2, 3)), V((tokens, LANES), jnp.int32),
            V((3, tokens, width), f32), V((2, tokens, LANES), f32),
            by_token(f32), by_token(f32), by_token(f32), by_token(bf16),
            by_row(2), by_token(f32), by_token(f32), by_row(2), by_row(2),
            V((2, rank, tokens), bf16),
            V((2, tokens * states, LANES), f32), V((2, tokens * states, LANES), f32),
            V((2, states, e), f32), V((2, (tokens + 1) * states, e), f32),
            by_row(), by_row(), by_row(), V((tokens, e), bf16),
            V((tokens * states, LANES), f32), V((tokens * states, LANES), f32),
            V((rank + 2 * states, tokens), bf16), V((tokens, width), f32),
        ],
        compiler_params=pltpu.CompilerParams(vmem_limit_bytes=58 * 1024 * 1024),
        name="layers",
    )(section, lengths, x, cot, small, in_own, in_recv, xd_own, xd_recv, out_own, out_recv)


PLANE = 4


def call(kernel, outs, args, smem=1, name=None, deps=()):
    vmem = pl.BlockSpec(memory_space=pltpu.VMEM)
    specs = [pl.BlockSpec(memory_space=pltpu.SMEM)] * smem + [vmem] * (len(args) - smem)
    specs += [pl.BlockSpec(memory_space=pl.ANY)] * len(deps)
    return pl.pallas_call(
        kernel, out_shape=outs, in_specs=specs, out_specs=jax.tree.map(lambda _: vmem, outs), name=name,
        compiler_params=pltpu.CompilerParams(vmem_limit_bytes=48 * 1024 * 1024),
    )(*args, *deps)


def with_deps(kernel, n_deps, at):
    def wrapped(*refs):
        return kernel(*refs[:at], *refs[at + n_deps:])

    return wrapped


def pack(place, own, other, width, e, which, small=(), deps=()):
    tokens = own.shape[0]
    part = e // PLANE
    NORMED, BOTH, GATED, OUTG = 0, width, width + 2 * e, width + 3 * e
    whole_at = {"out": OUTG, "in_low": NORMED, "in_high": None}[which]
    part_at, stride = {"out": (GATED, part), "in_low": (BOTH, 2 * part), "in_high": (BOTH + part, 2 * part)}[which]
    base = 0 if whole_at is None else 2 * tokens
    small_rows = small[0].shape[0] // PLANE if small else 0
    rows = base + tokens + 2 * small_rows

    def kernel(at, own, other, *rest):
        smalls, outs = rest[:len(small)], rest[len(small):]
        for mask in range(PLANE):
            q = at[0] ^ mask
            out = outs[mask]
            for k, side in enumerate((own, other)):
                if whole_at is not None:
                    out[k * tokens:(k + 1) * tokens, :] = side[:, whole_at:whole_at + width]
                here = pl.ds(pl.multiple_of(part_at + q * stride, LANES), part)
                out[base:base + tokens, k * part:(k + 1) * part] = side[:, here]
            if smalls:
                block = pl.ds(pl.multiple_of(q * small_rows, 8), small_rows)
                for k in range(2):
                    cols = slice(k * width, (k + 1) * width)
                    at_row = base + tokens + k * small_rows
                    out[at_row:at_row + small_rows, :] = (smalls[0][block, cols] + smalls[1][block, cols]).astype(bf16)

    outs = (jax.ShapeDtypeStruct((rows, width), bf16),) * PLANE
    args = (place, own, other) + tuple(small)
    return call(with_deps(kernel, len(deps), len(args)), outs, args, name="pack_" + which, deps=deps)


def product(place, tall, thin, swapped, small_rows, name):
    n = len(tall)
    width = tall[0].shape[1]
    half = width // 2
    tokens = tall[0].shape[0] // 3
    base = 2 * tokens if thin is None else 0
    many = n * 2 * tokens
    rows, cols = (half, width) if swapped else (width, half)
    shard = rows // 4

    def kernel(at, *refs):
        ins, (keep, send, full, narrow, total) = refs[:-5], refs[-5:]
        talls, thins = ins[:n], (ins[n:] or ins[:n])
        for k in range(n):
            full[k * 2 * tokens:(k + 1) * 2 * tokens, :] = talls[k][0:2 * tokens, :]
            for j in range(2):
                narrow[(2 * k + j) * tokens:(2 * k + j + 1) * tokens, :] = thins[k][base:base + tokens, j * half:(j + 1) * half]
        left, right = (narrow, full) if swapped else (full, narrow)
        total[:, :, 0:shard, :] = tn(left[...], right[...]).reshape(2, 2, shard, cols)
        for b1 in range(2 if small_rows else 0):
            block = slice(base + tokens + b1 * small_rows, base + tokens + (b1 + 1) * small_rows)
            both = sum(thins[k][block, :].astype(f32) for k in range(n))
            for b0 in range(2):
                total[b1, b0, shard:, :] = both[:, b0 * half:(b0 + 1) * half]
        b0 = at[1]
        for j in range(2):
            keep[j] = total[j, b0]
            send[j] = total[j, 1 - b0].astype(bf16)

    shape = (2, shard + small_rows, cols)
    V = pltpu.VMEM
    args = [place] + list(tall) + list(thin or ())
    vmem = pl.BlockSpec(memory_space=pltpu.VMEM)
    return pl.pallas_call(
        kernel, out_shape=(jax.ShapeDtypeStruct(shape, f32), jax.ShapeDtypeStruct(shape, bf16)),
        in_specs=[pl.BlockSpec(memory_space=pltpu.SMEM)] + [vmem] * (len(args) - 1), out_specs=(vmem, vmem),
        scratch_shapes=[V((many, width), bf16), V((many, half), bf16), V((2,) + shape, f32)],
        compiler_params=pltpu.CompilerParams(vmem_limit_bytes=48 * 1024 * 1024), name=name,
    )(*args)


def add_near(place, keep, came):
    def kernel(at, keep, came, mine, send):
        b1 = at[2]
        mine[...] = keep[b1] + came[b1].astype(f32)
        send[...] = (keep[1 - b1] + came[1 - b1].astype(f32)).astype(bf16)

    shape = keep.shape[1:]
    return call(kernel, (jax.ShapeDtypeStruct(shape, f32), jax.ShapeDtypeStruct(shape, bf16)), (place, keep, came), name="add_near")


def pair_up(place, own, came):
    def kernel(at, own, came, out):
        b1 = at[2]
        out[b1] = own[...]
        out[1 - b1] = came[...]

    return call(kernel, jax.ShapeDtypeStruct((2,) + own.shape, bf16), (place, own, came), name="pair_up")


def quarter_of(place, own, came):
    def kernel(at, own, came, out):
        b0 = at[1]
        for j in range(2):
            out[j, b0] = own[j]
            out[j, 1 - b0] = came[j]

    shape = (2, 2) + own.shape[1:]
    return call(kernel, jax.ShapeDtypeStruct(shape, bf16), (place, own, came), name="quarter_of")


def spread(place, quarter, shared, shape, by_rows, slot, slots, base, small, name):
    by_x, by_y, far_low, far_high = shared
    small_rows = small[0] if small else 0
    shard, cols = quarter.shape[2] - small_rows, quarter.shape[3]
    rows = 4 * shard
    args = [quarter, by_x, by_y, far_low, far_high]

    def kernel(at, own, by_x, by_y, far_low, far_high, *rest):
        rest = rest[1 if base is not None else 0:]
        out, outs = rest[0], rest[1:]
        step = pl.program_id(0)

        def put(ref, b1, source):
            for b0 in range(2):
                z = 2 * b1 + b0
                out[z * shard:(z + 1) * shard, :] = source(ref, b0)[0:shard, :].astype(f32)
                if small:
                    block = pl.ds(pl.multiple_of((at[0] ^ step) * small_rows, 8), small_rows)
                    outs[-1][block, z * cols:(z + 1) * cols] = source(ref, b0)[shard:, :].astype(f32)

        for k, ref in enumerate((own, by_x, by_y)):
            @pl.when(step == k)
            def _(ref=ref):
                for b1 in range(2):
                    put(ref, b1, lambda ref, b0, b1=b1: ref[b1, b0])

        @pl.when(step == 3)
        def _():
            for b1, ref in enumerate((far_low, far_high)):
                put(ref, b1, lambda ref, b0: ref[b0])
            if small:
                at_row = 0
                for out_s in outs[:-1]:
                    n = out_s.shape[0]
                    out_s[...] = outs[-1][at_row:at_row + n, 0:out_s.shape[1]]
                    at_row += n

    if by_rows:
        index = lambda step, at: (at[0] ^ step, 0)
    else:
        index = lambda step, at: (0, (at[0] ^ step) * slots + slot)
    in_specs = [pl.BlockSpec(a.shape, lambda step, at, n=len(a.shape): (0,) * n) for a in args]
    aliases = {}
    if base is not None:
        args.append(base)
        in_specs.append(pl.BlockSpec(memory_space=pl.ANY))
        aliases = {len(args): 0}
    outs = [jax.ShapeDtypeStruct(shape, f32)]
    out_specs = [pl.BlockSpec((rows, cols), index)]
    scratch = []
    if small:
        for n in small[1]:
            outs.append(jax.ShapeDtypeStruct(n, f32))
            out_specs.append(pl.BlockSpec(n, lambda step, at: (0, 0)))
        scratch = [pltpu.VMEM((PLANE * small_rows, 4 * cols), f32)]
    return pl.pallas_call(
        kernel, out_shape=tuple(outs),
        grid_spec=pltpu.PrefetchScalarGridSpec(
            num_scalar_prefetch=1, grid=(4,), in_specs=in_specs, out_specs=tuple(out_specs), scratch_shapes=scratch,
        ),
        input_output_aliases=aliases,
        compiler_params=pltpu.CompilerParams(vmem_limit_bytes=48 * 1024 * 1024), name=name,
    )(place, *args)


def chip_swap(array, mask):
    chips = lax.axis_size("dp")
    return lax.ppermute(array, "dp", [(i, i ^ mask) for i in range(chips)])


def reduce_shards(place, keep, send):
    mine, send = add_near(place, keep, chip_swap(send, PLANE))
    total = (mine + chip_swap(send, 2 * PLANE).astype(f32)).astype(bf16)
    mask = 4 * PLANE
    while mask < lax.axis_size("dp"):
        total = (total.astype(f32) + chip_swap(total, mask).astype(f32)).astype(bf16)
        mask *= 2
    pair = pair_up(place, total, chip_swap(total, 2 * PLANE))
    return quarter_of(place, pair, chip_swap(pair, PLANE))


def share_quarters(quarter):
    by_x, by_y = chip_swap(quarter, 1), chip_swap(quarter, 2)
    return by_x, by_y, chip_swap(by_y[0], 1), chip_swap(by_x[1], 2)


def per_device(
    ends_in, lengths, norm_gain, in_weight, conv_weight, conv_bias, xproj_weight,
    dtproj_weight, dt_bias, a_log, d_skip, out_weight,
):
    section = lax.axis_index("section")
    first = section == 0
    width, e = norm_gain.shape[1], conv_bias.shape[1]
    states, taps, rank = a_log.shape[1], conv_weight.shape[1], dtproj_weight.shape[1]
    rows = ends_in.shape[1]
    half = rows // 2
    micro = lengths.shape[0]
    swap = [(0, 1), (1, 0)]

    def across(array):
        return lax.ppermute(array, "section", swap)

    small_own = jnp.concatenate(
        [
            a_log[0], conv_weight[0], conv_bias, dt_bias, d_skip,
            jnp.pad(norm_gain, ((0, 0), (0, e - width))),
        ],
        axis=0,
    )
    xd_own = jnp.concatenate([xproj_weight[0].T, dtproj_weight[0]], axis=0)
    halves = ends_in[0].reshape(2, half, width)
    mine = lax.dynamic_index_in_dim(halves, section, 0, keepdims=False)
    theirs = lax.dynamic_index_in_dim(halves, 1 - section, 0, keepdims=False)
    in_recv = across(in_weight[0])
    ends_recv = across(theirs)
    small_recv = across(small_own)
    xd_recv = across(xd_own)
    out_recv = across(out_weight[0])
    small = jnp.where(first, jnp.stack([small_own, small_recv]), jnp.stack([small_recv, small_own]))
    x = jnp.where(first, mine, ends_recv)
    cot = jnp.where(first, ends_recv, mine)
    my_lengths = lax.dynamic_slice_in_dim(lengths, section * (micro // 2), micro // 2, 0)
    out, gin, fac_own, fac_other, grads_own, grads_other = run_layers(
        section.astype(jnp.int32).reshape(1), my_lengths, x, cot, small,
        in_weight[0], in_recv, xd_own, xd_recv, out_weight[0], out_recv, states, taps, rank,
    )
    fac_other = across(fac_other)
    grads_other = across(grads_other)
    kept = jnp.where(first, gin, out)
    came = across(jnp.where(first, out, gin))
    ends = jnp.where(first, jnp.concatenate([kept, came]), jnp.concatenate([came, kept]))[None]
    chip = lax.axis_index("dp")
    place = jnp.stack([chip % PLANE, chip // PLANE % 2, chip // (2 * PLANE) % 2]).astype(jnp.int32)

    def around(part):
        return [part[0]] + [chip_swap(part[m], m) for m in range(1, PLANE)]

    out_parts = around(pack(place, fac_own, fac_other, width, e, "out"))
    low_parts = around(pack(place, fac_own, fac_other, width, e, "in_low", deps=out_parts[1:]))
    high_parts = around(
        pack(place, fac_own, fac_other, width, e, "in_high", small=(grads_own, grads_other), deps=low_parts[1:])
    )
    small_rows = grads_own.shape[0] // PLANE
    out_q = reduce_shards(place, *product(place, out_parts, None, True, 0, "product_out"))
    low_q = reduce_shards(place, *product(place, low_parts, None, False, 0, "product_in_low"))
    high_q = reduce_shards(place, *product(place, low_parts, high_parts, False, small_rows, "product_in_high"))
    out_s, low_s, high_s = share_quarters(out_q), share_quarters(low_q), share_quarters(high_q)
    grad_out, = spread(place, out_q, out_s, (e, width), True, 0, 1, None, None, "spread_out")
    grad_in, = spread(place, low_q, low_s, (width, 2 * e), False, 0, 2, None, None, "spread_in_low")
    low_rows = rank + 2 * states
    one = (1, e)
    shapes = [(low_rows, e), (rank, e), (states, e), (taps, e), one, one, one, (1, width)]
    grad_in, xproj, dtproj, alog, conv_w, conv_b, dt_b, dskip, gain = spread(
        place, high_q, high_s, (width, 2 * e), False, 1, 2, grad_in, (small_rows, shapes), "spread_in_high"
    )
    return (
        ends, gain, grad_in[None], conv_w[None], conv_b, xproj.T[None], dtproj[None], dt_b, alog[None], dskip,
        grad_out[None],
    )


def solution(mesh):
    in_specs = (
        P("section", "dp", None), P("dp", None), P("section", None), P("section", None, None),
        P("section", None, None), P("section", None), P("section", None, None), P("section", None, None),
        P("section", None), P("section", None, None), P("section", None), P("section", None, None),
    )
    out_specs = (
        P("section", "dp", None), P("section", None), P("section", None, None), P("section", None, None),
        P("section", None), P("section", None, None), P("section", None, None), P("section", None),
        P("section", None, None), P("section", None), P("section", None, None),
    )
    return jax.shard_map(per_device, mesh=mesh, in_specs=in_specs, out_specs=out_specs, check_vma=False)
```

```python
from types import SimpleNamespace

import jax
import jax.numpy as jnp
from jax import lax
from jax.experimental import pallas as pl
from jax.experimental.pallas import tpu as pltpu
from jax.sharding import PartitionSpec as P

EPSILON = 1e-05
LOG2E = 1.4426950408889634
LN2 = 0.6931471805599453
CUT = 1e6
LANES = 128
WIDE = 512
GROUP = 8
PLANE = 4
MIB = 1024 * 1024

bf16, f32 = jnp.bfloat16, jnp.float32
VMEM = pl.BlockSpec(memory_space=pltpu.VMEM)
SMEM = pl.BlockSpec(memory_space=pltpu.SMEM)
ANYWHERE = pl.BlockSpec(memory_space=pl.ANY)


def shaped(shape, kind):
    return jax.ShapeDtypeStruct(shape, kind)


def nn(a, b):
    return jnp.dot(a, b, preferred_element_type=f32)


def nt(a, b):
    return lax.dot_general(a, b, (((1,), (1,)), ((), ())), preferred_element_type=f32)


def tn(a, b):
    return lax.dot_general(a, b, (((0,), (0,)), ((), ())), preferred_element_type=f32)


def sigmoid(v):
    return 1.0 / (1.0 + jnp.exp(-v))


def with_deps(kernel, n_deps, at):
    def wrapped(*refs):
        return kernel(*refs[:at], *refs[at + n_deps:])

    return wrapped


def call(kernel, outs, args, name, smem=1, deps=(), scratch=(), limit=16, cost=None):
    specs = [SMEM] * smem + [VMEM] * (len(args) - smem) + [ANYWHERE] * len(deps)
    return pl.pallas_call(
        with_deps(kernel, len(deps), len(args)), out_shape=outs, in_specs=specs,
        out_specs=jax.tree.map(lambda _: VMEM, outs), scratch_shapes=list(scratch), name=name,
        cost_estimate=cost or pl.CostEstimate(flops=1, bytes_accessed=1, transcendentals=0),
        compiler_params=pltpu.CompilerParams(vmem_limit_bytes=limit * MIB),
    )(*args, *deps)


def pack_params(a_log, conv_weight, conv_bias, dt_bias, d_skip, norm_gain):
    rows = sum(a.shape[-2] for a in (a_log, conv_weight, conv_bias, dt_bias, d_skip, norm_gain))
    e, width = d_skip.shape[1], norm_gain.shape[1]

    def kernel(*refs):
        out = refs[-1]
        at_row = 0
        for ref in refs[:-1]:
            n, columns = ref.shape
            out[at_row:at_row + n, 0:columns] = ref[...]
            at_row += n
        out[at_row - 1:at_row, width:] = jnp.zeros((1, e - width), f32)

    args = (a_log, conv_weight, conv_bias, dt_bias, d_skip, norm_gain)
    return call(kernel, shaped((rows, e), f32), args, "pack_params", smem=0)


def make_layers(tokens, width, e, states, taps, rank):
    steps_wide = e // WIDE
    tiles = WIDE // LANES
    low_rows = rank + 2 * states
    AL, CW, CB, DB, DS, GN = 0, states, states + taps, states + taps + 1, states + taps + 2, states + taps + 3
    GX, GD = 0, low_rows
    GA = GD + rank
    GC = GA + states
    GB, GT, GS, GG = GC + taps, GC + taps + 1, GC + taps + 2, GC + taps + 3

    def wide(i, base=0):
        return pl.ds(pl.multiple_of(i * WIDE + base, LANES), WIDE)

    def tile(i, k):
        return pl.ds(pl.multiple_of(i * WIDE + k * LANES, LANES), LANES)

    def of_state(t):
        return pl.ds(pl.multiple_of(t * states, states), states)

    def grouped(value):
        return value.reshape(tokens // GROUP, GROUP, value.shape[1])

    def flat(value):
        return value.reshape(tokens, value.shape[2])

    def half_sum(value):
        return sum(value[n * 8:(n + 1) * 8] for n in range(states // 8))

    def row_sums(rows, k):
        return sum(rows[k, pl.ds(n, GROUP, stride=8), :] for n in range(8))

    def keep(r, k):
        return jnp.concatenate([r.offs[...]] * tiles, axis=1) >= k

    def fill_offsets(offs, lengths):
        micro = lengths.shape[0]
        count = tokens // micro
        row = lax.broadcasted_iota(jnp.int32, (tokens, LANES), 0)
        begin = jnp.zeros_like(row)
        for m in range(micro):
            a = lengths[m, 0] + m * count
            b = a + lengths[m, 1]
            begin = jnp.where(row >= m * count, m * count, begin)
            begin = jnp.where(row >= a, a, begin)
            begin = jnp.where(row >= b, b, begin)
        offs[...] = row - begin

    def fill_rate(r, l):
        r.rate[l] = -jnp.exp(r.small[l, AL:AL + states, :]) * LOG2E

    def forward(l, r):
        x = r.resid[l]
        norm = lax.rsqrt(jnp.mean(x * x, axis=1, keepdims=True) + EPSILON)
        r.nrm[l] = (x * norm * r.small[l, GN:GN + 1, 0:width]).astype(bf16)
        r.arrived(l, 0)

        def project(i, _):
            c = wide(i)
            v = nn(r.nrm[l], r.in_w[l, :, c])
            r.inner[l, :, c] = v
            r.gate[l, :, c] = nn(r.nrm[l], r.in_w[l, :, wide(i, e)])
            total = r.small[l, CB:CB + 1, c] + r.small[l, CW + taps - 1:CW + taps, c] * v
            for k in range(1, taps):
                before = jnp.where(keep(r, k), pltpu.roll(v, k, 0), 0.0)
                total = total + r.small[l, CW + taps - 1 - k:CW + taps - k, c] * before
            r.conv[l, :, c] = total
            r.act[l, :, c] = (total * sigmoid(total)).astype(bf16)
            return 0

        lax.fori_loop(0, steps_wide, project, 0)
        r.arrived(l, 1)
        a = r.act[l]
        low = nt(a, r.xd_w[l, 0:rank, :]).astype(bf16)
        proj_t = nt(r.xd_w[l, 0:low_rows, :], a)
        r.low_t[l] = proj_t[0:rank].astype(bf16)
        for t in range(tokens):
            here = slice(t * states, (t + 1) * states)
            r.bb[l, here, :] = jnp.broadcast_to(proj_t[rank:rank + states, t:t + 1], (states, LANES))
            r.cb[l, here, :] = jnp.broadcast_to(proj_t[rank + states:, t:t + 1], (states, LANES))
        fill_rate(r, l)

        def scan(i, _):
            c = wide(i)
            v = nn(low, r.xd_w[l, low_rows:low_rows + rank, c]) + r.small[l, DB:DB + 1, c]
            shrunk = jnp.exp(-jnp.abs(v))
            s = jnp.maximum(v, 0.0) + jnp.log1p(shrunk)
            inverse = 1.0 / (1.0 + shrunk)
            r.sig[l, :, c] = jnp.where(v >= 0, inverse, shrunk * inverse)
            r.step[l, :, c] = s
            r.uin[l, :, :, c] = grouped(s * r.act[l, :, c].astype(f32))
            r.size[l, :, :, c] = grouped(jnp.where(keep(r, 1), s, CUT))
            rates = [r.rate[l, :, tile(i, k)] for k in range(tiles)]

            def group(g, h):
                h = list(h)
                for j in range(GROUP):
                    t = g * GROUP + j
                    bt, ct = r.bb[l, of_state(t), :], r.cb[l, of_state(t), :]
                    for k in range(tiles):
                        f = jnp.exp2(r.size[l, g, j:j + 1, tile(i, k)] * rates[k])
                        h[k] = f * h[k] + bt * r.uin[l, g, j:j + 1, tile(i, k)]
                        r.hist[l, of_state(t + 1), tile(i, k)] = h[k]
                        r.rows_a[k, j * 8:(j + 1) * 8, :] = half_sum(ct * h[k])
                for k in range(tiles):
                    r.yscan[l, g, :, tile(i, k)] = row_sums(r.rows_a, k)
                return tuple(h)

            none = tuple(jnp.zeros((states, LANES), f32) for _ in range(tiles))
            lax.fori_loop(0, tokens // GROUP, group, none)
            z = r.gate[l, :, c]
            p = flat(r.yscan[l, :, :, c]) + r.small[l, DS:DS + 1, c] * r.act[l, :, c].astype(f32)
            r.gat[l, :, c] = (p * (z * sigmoid(z))).astype(bf16)
            return 0

        lax.fori_loop(0, steps_wide, scan, 0)
        r.arrived(l, 2)
        result = x + nn(r.gat[l], r.out_w[l])
        return result

    def backward(l, r):
        r.outg[...] = r.upstream[...].astype(bf16)
        r.acc_b[...] = jnp.zeros_like(r.acc_b)
        r.acc_c[...] = jnp.zeros_like(r.acc_c)
        rest = r.grads_o.shape[1] - GG
        r.grads_o[0, GG:, :] = jnp.zeros((rest, e), f32)

        def scan(i, _):
            c = wide(i)
            from_out = nt(r.outg[...], r.out_w[l, c, :])
            a = r.act[l, :, c].astype(f32)
            z = r.gate[l, :, c]
            s = sigmoid(z)
            p = flat(r.yscan[l, :, :, c]) + r.small[l, DS:DS + 1, c] * a
            dp = from_out * (z * s)
            r.dyscan[:, :, c] = grouped(dp)
            r.fi[:, wide(i, width + e)] = (from_out * p * (s * (1.0 + z * (1.0 - s)))).astype(bf16)
            r.grads_o[0, GS:GS + 1, c] = jnp.sum(dp * a, axis=0, keepdims=True)
            rates = [r.rate[l, :, tile(i, k)] for k in range(tiles)]

            def group(backwards, carried):
                carry, now, drate = (list(v) for v in carried)
                g = tokens // GROUP - 1 - backwards
                for j in reversed(range(GROUP)):
                    t = g * GROUP + j
                    bt, ct = r.bb[l, of_state(t), :], r.cb[l, of_state(t), :]
                    sum_b = sum_c = None
                    for k in range(tiles):
                        sz = r.size[l, g, j:j + 1, tile(i, k)]
                        dy = r.dyscan[g, j:j + 1, tile(i, k)]
                        grad = carry[k] + ct * dy
                        part_b = grad * r.uin[l, g, j:j + 1, tile(i, k)]
                        part_c = now[k] * dy
                        sum_b = part_b if sum_b is None else sum_b + part_b
                        sum_c = part_c if sum_c is None else sum_c + part_c
                        r.rows_a[k, j * 8:(j + 1) * 8, :] = half_sum(bt * grad)
                        carry[k] = jnp.exp2(sz * rates[k]) * grad
                        now[k] = r.hist[l, of_state(t), tile(i, k)]
                        w = carry[k] * now[k]
                        r.rows_b[k, j * 8:(j + 1) * 8, :] = half_sum(w * rates[k])
                        drate[k] = drate[k] + sz * w
                    r.acc_b[of_state(t), :] += sum_b
                    r.acc_c[of_state(t), :] += sum_c
                for k in range(tiles):
                    r.dact[g, :, tile(i, k)] = row_sums(r.rows_a, k)
                    r.dsz[g, :, tile(i, k)] = row_sums(r.rows_b, k)
                return tuple(carry), tuple(now), tuple(drate)

            none = tuple(jnp.zeros((states, LANES), f32) for _ in range(tiles))
            final = tuple(r.hist[l, of_state(tokens), tile(i, k)] for k in range(tiles))
            _, _, drate = lax.fori_loop(0, tokens // GROUP, group, (none, final, none))
            for k in range(tiles):
                r.grads_o[0, GA:GA + states, tile(i, k)] = drate[k] * (rates[k] * LN2)
            du = flat(r.dact[:, :, c])
            dv = (flat(r.dsz[:, :, c]) * LN2 + du * a) * r.sig[l, :, c]
            r.dact[:, :, c] = grouped(du * r.step[l, :, c] + dp * r.small[l, DS:DS + 1, c])
            r.dtg[:, c] = dv.astype(bf16)
            r.grads_o[0, GT:GT + 1, c] = jnp.sum(dv, axis=0, keepdims=True)
            return 0

        lax.fori_loop(0, steps_wide, scan, 0)
        lane = lax.broadcasted_iota(jnp.int32, (states, LANES), 1)
        db = jnp.zeros((states, LANES), f32)
        dc = jnp.zeros((states, LANES), f32)
        for t in range(tokens):
            here = slice(t * states, (t + 1) * states)
            db = jnp.where(lane == t, jnp.sum(r.acc_b[here, :], axis=1, keepdims=True), db)
            dc = jnp.where(lane == t, jnp.sum(r.acc_c[here, :], axis=1, keepdims=True), dc)
        r.pg_t[0:rank, :] = nt(r.xd_w[l, low_rows:low_rows + rank, :], r.dtg[...]).astype(bf16)
        r.pg_t[rank:rank + states, :] = db[:, 0:tokens].astype(bf16)
        r.pg_t[rank + states:low_rows, :] = dc[:, 0:tokens].astype(bf16)

        def conv_back(i, _):
            c = wide(i)
            r.grads_o[0, GX:GX + low_rows, c] = nn(r.pg_t[...], r.act[l, :, c])
            r.grads_o[0, GD:GD + rank, c] = nn(r.low_t[l], r.dtg[:, c])
            da = tn(r.pg_t[...], r.xd_w[l, 0:low_rows, c]) + flat(r.dact[:, :, c])
            total = r.conv[l, :, c]
            s = sigmoid(total)
            dv = da * (s * (1.0 + total * (1.0 - s)))
            v = r.inner[l, :, c]
            r.grads_o[0, GB:GB + 1, c] = jnp.sum(dv, axis=0, keepdims=True)
            r.grads_o[0, GC + taps - 1:GC + taps, c] = jnp.sum(dv * v, axis=0, keepdims=True)
            dinner = r.small[l, CW + taps - 1:CW + taps, c] * dv
            for k in range(1, taps):
                kept = jnp.where(keep(r, k), dv, 0.0)
                r.grads_o[0, GC + taps - 1 - k:GC + taps - k, c] = jnp.sum(
                    kept * pltpu.roll(v, k, 0), axis=0, keepdims=True
                )
                dinner = dinner + r.small[l, CW + taps - 1 - k:CW + taps - k, c] * pltpu.roll(kept, tokens - k, 0)
            r.fi[:, wide(i, width)] = dinner.astype(bf16)
            return 0

        lax.fori_loop(0, steps_wide, conv_back, 0)
        dn = nt(r.fi[:, width:width + 2 * e], r.in_w[l])
        x = r.resid[l]
        norm = lax.rsqrt(jnp.mean(x * x, axis=1, keepdims=True) + EPSILON)
        xr = x * norm
        r.grads_o[0, GG:GG + 1, 0:width] = jnp.sum(dn * xr, axis=0, keepdims=True)
        dxr = dn * r.small[l, GN:GN + 1, 0:width]
        grad_in = r.upstream[...] + norm * (dxr - xr * jnp.mean(dxr * xr, axis=1, keepdims=True))
        return grad_in

    def fetch(me, l, own, recv, dst, sem):
        @pl.when(me == l)
        def _():
            pltpu.make_async_copy(own, dst, sem).start()

        @pl.when(me != l)
        def _():
            pltpu.make_async_copy(recv, dst, sem).start()

    def forward_kernel(
        sec, lengths, mine, theirs, small_own, small_recv,
        in_own, in_recv, xd_own, xd_recv, out_own, out_recv, *refs,
    ):
        me = sec[0]
        n = len(STATE)
        first = SimpleNamespace(**dict(zip(STATE, refs[:n])))
        out_o, own_o, other_o, in_fac, grads, up_o = refs[n:n + 6]
        sems, *rest = refs[n + 6:]
        last = SimpleNamespace(**dict(zip(STATE, rest[:n])))
        scratch = dict(zip(SCRATCH, rest[n:]))
        for l, r in enumerate((first, last)):
            r.__dict__.update(scratch)
            r.offs = first.offs
            weights = ((in_own, in_recv, r.in_w), (xd_own, xd_recv, r.xd_w), (out_own, out_recv, r.out_w))
            for k, (own, recv, dst) in enumerate(weights):
                fetch(me, l, own, recv, dst.at[0], sems.at[l, k])

            def arrived(_, k, l=l, weights=weights):
                own, _, dst = weights[k]
                pltpu.make_async_copy(own, dst.at[0], sems.at[l, k]).wait()

            r.arrived = arrived
            r.hist[0, 0:states, :] = jnp.zeros((states, e), f32)
        fill_offsets(first.offs, lengths)
        last.fi = in_fac
        for core in range(2):
            @pl.when(me == core)
            def _():
                own, other = (mine, theirs) if core == 0 else (theirs, mine)
                first.resid[0] = own[...].astype(f32)
                last.outg[...] = other[...]
                last.upstream[...] = other[...].astype(f32)
                for l, r in enumerate((first, last)):
                    r.small[0] = small_own[...] if l == core else small_recv[...]

        last.resid[0] = forward(0, first).astype(bf16).astype(f32)
        out_o[...] = forward(0, last)
        up = backward(0, last).astype(bf16)
        up_o[...] = up
        in_fac[:, 0:width] = last.nrm[0]
        grads[...] = last.grads_o[0].astype(bf16)
        for core in range(2):
            @pl.when(me == core)
            def _():
                for l, to in enumerate((own_o, other_o) if core == 0 else (other_o, own_o)):
                    to[:, 0:e] = (first, last)[l].gat[0]
                    to[:, e:] = up if l == 0 else last.outg[...]

    def backward_kernel(up_in, *refs):
        n = len(STATE)
        r = SimpleNamespace(**dict(zip(STATE, refs[:n])))
        in_fac, grads, gin_o = refs[n:n + 3]
        r.__dict__.update(zip(SCRATCH, refs[n + 3:]))
        r.fi = in_fac
        r.outg[...] = up_in[...]
        r.upstream[...] = up_in[...].astype(f32)
        gin_o[...] = backward(0, r)
        in_fac[:, 0:width] = r.nrm[0]
        grads[...] = r.grads_o[0].astype(bf16)

    grad_rows = (GG + 1 + 63) // 64 * 64
    return forward_kernel, backward_kernel, grad_rows


STATE = (
    "in_w", "xd_w", "out_w", "small", "offs", "resid", "nrm", "gat", "inner", "gate", "conv", "act",
    "size", "step", "sig", "yscan", "uin", "low_t", "bb", "cb", "rate", "hist",
)
SCRATCH = (
    "grads_o", "dyscan", "dact", "dsz", "dtg", "acc_b", "acc_c", "pg_t", "upstream", "outg", "rows_a", "rows_b",
)


def run_layers(section, lengths, mine, theirs, small_own, small_recv, weights, states, taps, rank):
    tokens, width = mine.shape
    in_w, _, xd_w, _, out_w, _ = weights
    e = out_w.shape[0]
    V = pltpu.VMEM
    forward, backward, grad_rows = make_layers(tokens, width, e, states, taps, rank)
    by_token = lambda kind=f32: V((1, tokens, e), kind)
    by_row = lambda *lead: V(lead + (tokens // GROUP, GROUP, e), f32)
    by_state = lambda *lead: V(lead + (tokens * states, LANES), f32)
    sums = lambda: V((WIDE // LANES, GROUP * 8, LANES), f32)
    state = (
        V((1,) + in_w.shape, bf16), V((1,) + xd_w.shape, bf16), V((1,) + out_w.shape, bf16),
        V((1,) + small_own.shape, f32), V((tokens, LANES), jnp.int32), V((1, tokens, width), f32),
        V((1, tokens, width), bf16), by_token(bf16), by_token(), by_token(), by_token(), by_token(bf16),
        by_row(1), by_token(), by_token(), by_row(1), by_row(1), V((1, rank, tokens), bf16),
        by_state(1), by_state(1), V((1, states, e), f32), V((1, (tokens + 1) * states, e), f32),
    )
    scratch = (
        V((1, grad_rows, e), f32), by_row(), by_row(), by_row(), V((tokens, e), bf16), by_state(), by_state(),
        V((rank + 2 * states, tokens), bf16), V((tokens, width), f32), V((tokens, width), bf16), sums(), sums(),
    )
    n = len(STATE)
    work = pl.CostEstimate(flops=1 << 30, bytes_accessed=30 * MIB, transcendentals=0)
    factors, grads = shaped((tokens, width + 2 * e), bf16), shaped((grad_rows, e), bf16)
    of_out = shaped((tokens, width + e), bf16)
    outs = (shaped((tokens, width), f32),) + tuple(V(a.shape, bf16) for a in (of_out, of_out, factors, grads, shaped((tokens, width), bf16)))
    here = lambda a, space: pltpu.with_memory_space_constraint(a, space)
    own_hbm = [here(a, pltpu.HBM if k % 2 == 0 else pltpu.VMEM) for k, a in enumerate(weights)]
    got = pl.pallas_call(
        forward, out_shape=state + outs,
        in_specs=[SMEM, SMEM] + [VMEM] * 4 + [ANYWHERE] * 6, out_specs=(VMEM,) * (n + len(outs)),
        scratch_shapes=[pltpu.SemaphoreType.DMA((2, 3)), *state, *scratch],
        compiler_params=pltpu.CompilerParams(vmem_limit_bytes=28 * MIB), name="forward_both", cost_estimate=work,
    )(section, lengths, mine, here(theirs, pltpu.VMEM), small_own, here(small_recv, pltpu.VMEM), *own_hbm)
    held = [here(a, pltpu.VMEM) for a in got[:n]]
    out, own_o, other_o, in1, grads1, up = got[n:]

    def rest(run):
        outs = (factors, grads, shaped((tokens, width), f32))
        return run(backward, outs, (up, *held), "backward_first", smem=0, scratch=scratch, limit=10, cost=work)

    return out, own_o, other_o, in1, grads1, rest


def swap_chips(array, mask):
    chips = lax.axis_size("dp")
    return lax.ppermute(array, "dp", [(i, i ^ mask) for i in range(chips)])


class Chain:
    def __init__(self, after):
        self.after = after

    def __call__(self, kernel, outs, args, name, deps=(), **options):
        if self.after is not None:
            after = self.after
            if after.dtype == f32 and after.size > MIB:
                after = pltpu.with_memory_space_constraint(after, pltpu.HBM)
            deps = (after, *deps)
        got = call(kernel, outs, args, name, deps=deps, **options)
        self.after = jax.tree.leaves(got)[-1]
        return got


def pack(run, place, sides, parts, width, rows_more, name):
    tokens = place.tokens
    half = width // 2
    rows = sum(tokens if kind == "half" else 2 * tokens for kind, *_ in parts)
    given = list(sides)
    if rows_more:
        small_rows, own_small, column_small = rows_more
        rows += 2 * small_rows
        given.append(own_small)

    def kernel(at, *refs):
        first, second = refs[:2]
        outs = refs[len(given):]
        for mask in range(PLANE):
            q = at[0] ^ mask
            out = outs[mask]
            base = 0
            for kind, column, *stride in parts:
                for k, side in enumerate((first, second)):
                    if kind == "whole":
                        out[base + k * tokens:base + (k + 1) * tokens, :] = side[:, column:column + width]
                    else:
                        cols = pl.ds(pl.multiple_of(column + q * stride[0], LANES), half)
                        out[base:base + tokens, k * half:(k + 1) * half] = side[:, cols]
                base += tokens if kind == "half" else 2 * tokens
            if rows_more:
                block = pl.ds(pl.multiple_of(q * small_rows, 16), small_rows)
                for k in range(2):
                    cols = slice(k * width, (k + 1) * width)
                    there = pl.ds(pl.multiple_of(column_small + q * 2 * width + k * width, LANES), width)
                    total = refs[2][block, cols].astype(f32) + second[0:small_rows, there].astype(f32)
                    out[base:base + small_rows, :] = total.astype(bf16)
                    base += small_rows

    return run(kernel, (shaped((rows, width), bf16),) * PLANE, (place.array, *given), name)


def choose(run, place, first, last, small_first, small_last, gin, out, deps):
    tokens, columns = first.shape
    rows, e = small_first.shape
    block = rows // PLANE

    def kernel(at, first, last, small_first, small_last, gin, out, own, own_small, send, own_end, send_end):
        for core in range(2):
            @pl.when(at[3] == core)
            def _():
                mine, theirs = ((first, small_first), (last, small_last))[:: 1 if core == 0 else -1]
                own[...] = mine[0][...]
                own_small[...] = mine[1][...]
                own_end[...], send_end[...] = (gin[...], out[...]) if core == 0 else (out[...], gin[...])
                send[:, 0:columns] = theirs[0][...]
                for q in range(PLANE):
                    send[0:block, columns + q * e:columns + (q + 1) * e] = theirs[1][q * block:(q + 1) * block, :]

    end = shaped(gin.shape, f32)
    outs = (shaped(first.shape, bf16), shaped(small_first.shape, bf16), shaped((tokens, columns + PLANE * e), bf16), end, end)
    return run(kernel, outs, (place.array, first, last, small_first, small_last, gin, out), "choose", deps=deps)


def place_ends(run, place, own, came):
    tokens, width = own.shape

    def kernel(at, own, came, out):
        for core in range(2):
            @pl.when(at[3] == core)
            def _():
                out[core * tokens:(core + 1) * tokens, :] = own[...]
                out[(1 - core) * tokens:(2 - core) * tokens, :] = came[...]

    return run(kernel, shaped((2 * tokens, width), f32), (place.array, own, came), "place_ends")


def other_layers(run, place, parts, width):
    tokens, half = place.tokens, width // 2

    def kernel(at, *refs):
        out = refs[-1]
        for k, ref in enumerate(refs[:-1]):
            out[k * tokens:(k + 1) * tokens, :] = ref[tokens:2 * tokens, :]
            at_row = (PLANE + k // 2) * tokens
            out[at_row:at_row + tokens, (k % 2) * half:(k % 2 + 1) * half] = ref[2 * tokens:3 * tokens, half:width]

    return run(kernel, shaped((PLANE * tokens * 3 // 2, width), bf16), (place.array, *parts), "other_layers")


def store_sums(at, total, keep, send):
    b0 = at[1]
    for j in range(2):
        keep[j] = total[j, b0]
        send[j] = total[j, 1 - b0].astype(bf16)


def product_out(run, place, parts, came, width):
    tokens, half = place.tokens, width // 2
    many = 2 * PLANE * tokens
    shape = (2, half // 4, width)

    def kernel(at, *refs):
        came, keep, send, left, right, total = refs[PLANE:]
        for k, ref in enumerate(refs[:PLANE]):
            right[k * tokens:(k + 1) * tokens, :] = ref[0:tokens, :]
            left[k * tokens:(k + 1) * tokens, :] = ref[2 * tokens:3 * tokens, 0:half]
            there = (PLANE + k) * tokens
            right[there:there + tokens, :] = came[k * tokens:(k + 1) * tokens, :]
            at_row = (PLANE + k // 2) * tokens
            left[there:there + tokens, :] = came[at_row:at_row + tokens, (k % 2) * half:(k % 2 + 1) * half]
        total[...] = tn(left[...], right[...]).reshape(2, *shape)
        store_sums(at, total, keep, send)

    V = pltpu.VMEM
    scratch = [V((many, half), bf16), V((many, width), bf16), V((2,) + shape, f32)]
    outs = (shaped(shape, f32), shaped(shape, bf16))
    return run(kernel, outs, (place.array, *parts, came), "product_out", scratch=scratch)


def product_in(run, place, tall, thin, base, small_rows, width, name):
    tokens, half = place.tokens, width // 2
    many = 2 * PLANE * tokens
    shard = width // 4
    shape = (2, shard + small_rows, half)
    args = (place.array, *tall) + (() if thin is tall else tuple(thin))

    def kernel(at, *refs):
        ins, (keep, send, left, right, total) = refs[:-5], refs[-5:]
        for k in range(PLANE):
            side = ins[-PLANE + k]
            left[2 * k * tokens:2 * (k + 1) * tokens, :] = ins[k][0:2 * tokens, :]
            for j in range(2):
                here = slice((2 * k + j) * tokens, (2 * k + j + 1) * tokens)
                right[here, :] = side[base:base + tokens, j * half:(j + 1) * half]
        total[:, :, 0:shard, :] = tn(left[...], right[...]).reshape(2, 2, shard, half)
        if small_rows:
            end = base + tokens
            mixed = sum(ins[-PLANE + k][end:end + 2 * small_rows, :].astype(f32) for k in range(PLANE))
            for b1 in range(2):
                for b0 in range(2):
                    block = mixed[b1 * small_rows:(b1 + 1) * small_rows, b0 * half:(b0 + 1) * half]
                    total[b1, b0, shard:, :] = block
        store_sums(at, total, keep, send)

    V = pltpu.VMEM
    scratch = [V((many, width), bf16), V((many, half), bf16), V((2,) + shape, f32)]
    return run(kernel, (shaped(shape, f32), shaped(shape, bf16)), args, name, scratch=scratch)


def add_near(run, place, keep, came):
    def kernel(at, keep, came, mine, send):
        b1 = at[2]
        mine[...] = keep[b1] + came[b1].astype(f32)
        send[...] = (keep[1 - b1] + came[1 - b1].astype(f32)).astype(bf16)

    shape = keep.shape[1:]
    return run(kernel, (shaped(shape, f32), shaped(shape, bf16)), (place.array, keep, came), "add_near")


def add_far(run, place, mine, came):
    def kernel(at, mine, came, out):
        out[...] = (mine[...].astype(f32) + came[...].astype(f32)).astype(bf16)

    total = run(kernel, shaped(mine.shape, bf16), (place.array, mine, came), "add_far")
    mask = 4 * PLANE
    while mask < lax.axis_size("dp"):
        total = run(kernel, shaped(mine.shape, bf16), (place.array, total, swap_chips(total, mask)), "add_far")
        mask *= 2
    return total


def pair_up(run, place, own, came):
    def kernel(at, own, came, out):
        b1 = at[2]
        out[b1] = own[...]
        out[1 - b1] = came[...]

    return run(kernel, shaped((2,) + own.shape, bf16), (place.array, own, came), "pair_up")


def quarter_of(run, place, own, came, far=None):
    rows, cols = own.shape[1:]

    def kernel(at, own, came, *rest):
        b0 = at[1]
        out = rest[0] if far is None else rest[2]
        for j in range(2):
            out[j, b0] = own[j]
            out[j, 1 - b0] = came[j]
        if far is not None:
            by_x, by_y, out, to_x, to_y = rest
            for to, ref, cut in ((to_x, by_y, far[2]), (to_y, by_x, far[3])):
                for j in range(2):
                    for i in range(2):
                        to[(2 * j + i) * rows:(2 * j + i + 1) * rows, :] = out[j, i]
                at_row = 4 * rows
                for piece in cut(ref):
                    for column in range(0, piece.shape[1], cols):
                        to[at_row:at_row + piece.shape[0], :] = piece[:, column:column + cols]
                        at_row += piece.shape[0]

    outs = shaped((2, 2, rows, cols), bf16)
    args = (place.array, own, came)
    if far is not None:
        sent = shaped((4 * rows + far[4] // cols, cols), bf16)
        outs, args = (outs, sent, sent), args + tuple(far[:2])
    return run(kernel, outs, args, "quarter_of")


def far_halves(run, place, by_x, by_y, rows):
    cols = by_x.shape[1]

    def kernel(at, by_x, by_y, low, high):
        low[...] = by_y[0:2 * rows, :]
        high[...] = by_x[2 * rows:4 * rows, :]

    return run(kernel, (shaped((2 * rows, cols), bf16),) * 2, (place.array, by_x, by_y), "far_halves")


def spread(run, place, arrays, find, columns, shape, by_rows, slot, slots, base, small, name):
    rows, cols = columns
    shard = rows // 4

    def kernel(at, *refs):
        ins, rest = refs[:len(arrays)], refs[len(arrays):]
        rest = rest[1 if base is not None else 0:]
        out, outs = rest[0], rest[1:]
        step = pl.program_id(0)
        for k in range(PLANE):
            @pl.when(step == k)
            def _(k=k):
                for z in range(4):
                    value = find(ins, k, z).astype(f32)
                    out[z * shard:(z + 1) * shard, :] = value[0:shard]
                    if small:
                        block = pl.ds(pl.multiple_of((at[0] ^ k) * small[0], 8), small[0])
                        outs[-1][block, z * cols:(z + 1) * cols] = value[shard:]

        if small:
            @pl.when(step == PLANE - 1)
            def _():
                at_row = 0
                for out_s in outs[:-1]:
                    n = out_s.shape[0]
                    out_s[...] = outs[-1][at_row:at_row + n, 0:out_s.shape[1]]
                    at_row += n

    if by_rows:
        index = lambda step, at: (at[0] ^ step, 0)
    else:
        index = lambda step, at: (0, (at[0] ^ step) * slots + slot)
    args = list(arrays)
    in_specs = [pl.BlockSpec(a.shape, lambda step, at, n=len(a.shape): (0,) * n) for a in args]
    aliases = {}
    if base is not None:
        args.append(base)
        in_specs.append(ANYWHERE)
        aliases = {len(args): 0}
    given = len(args)
    if base is None:
        big = run.after.size > MIB // 8
        args.append(pltpu.with_memory_space_constraint(run.after, pltpu.HBM) if big else run.after)
        in_specs.append(ANYWHERE)
    outs, out_specs, scratch = [pltpu.HBM(shape, f32)], [pl.BlockSpec((rows, cols), index)], []
    if small:
        for n in small[1]:
            outs.append(shaped(n, f32))
            out_specs.append(pl.BlockSpec(n, lambda step, at: (0, 0)))
        scratch = [pltpu.VMEM((PLANE * small[0], 4 * cols), f32)]
    got = pl.pallas_call(
        with_deps(kernel, len(args) - given, 1 + given), out_shape=tuple(outs),
        grid_spec=pltpu.PrefetchScalarGridSpec(
            num_scalar_prefetch=1, grid=(PLANE,), in_specs=in_specs, out_specs=tuple(out_specs), scratch_shapes=scratch,
        ),
        input_output_aliases=aliases,
        compiler_params=pltpu.CompilerParams(vmem_limit_bytes=24 * MIB), name=name,
    )(place.array, *args)
    run.after = got[-1]
    return got


def per_device(
    ends_in, lengths, norm_gain, in_weight, conv_weight, conv_bias, xproj_weight,
    dtproj_weight, dt_bias, a_log, d_skip, out_weight,
):
    section = lax.axis_index("section")
    first = section == 0
    width, e = norm_gain.shape[1], conv_bias.shape[1]
    states, taps, rank = a_log.shape[1], conv_weight.shape[1], dtproj_weight.shape[1]
    tokens = ends_in.shape[1] // 2
    micro = lengths.shape[0]

    def across(array, pairs=((0, 1), (1, 0))):
        return lax.ppermute(array, "section", pairs)

    in_recv = across(in_weight[0])
    halves = ends_in[0].reshape(2, tokens, width)
    mine = lax.dynamic_index_in_dim(halves, section, 0, keepdims=False)
    theirs = across(lax.dynamic_index_in_dim(halves, 1 - section, 0, keepdims=False))
    small_own = pack_params(a_log[0], conv_weight[0], conv_bias, dt_bias, d_skip, norm_gain)
    small_recv = across(small_own)
    xd_own = jnp.concatenate([xproj_weight[0].T, dtproj_weight[0]], axis=0)
    xd_recv = across(xd_own)
    out_recv = across(out_weight[0])
    my_lengths = lax.dynamic_slice_in_dim(lengths, section * (micro // 2), micro // 2, 0)
    weights = (in_weight[0], in_recv, xd_own, xd_recv, out_weight[0], out_recv)
    chip = lax.axis_index("dp")
    coords = jnp.stack([chip % PLANE, chip // PLANE % 2, chip // (2 * PLANE) % 2, section]).astype(jnp.int32)
    place = SimpleNamespace(array=coords, tokens=tokens)

    out, own_o, other_o, in1, grads1, backward_first = run_layers(
        section.astype(jnp.int32).reshape(1), my_lengths, mine, theirs, small_own, small_recv, weights, states, taps, rank
    )

    def around(parts):
        return [parts[0]] + [swap_chips(parts[m], m) for m in range(1, PLANE)]

    part = e // PLANE
    run = Chain(None)
    out_parts = around(pack(run, place, (own_o, other_o), (("whole", e), ("half", 0, part)), width, None, "pack_out"))
    in0, grads0, gin = backward_first(run)
    own, own_small, send, own_end, send_end = choose(run, place, in0, in1, grads0, grads1, gin, out, out_parts[1:])
    other = across(send)
    out_other = across(other_layers(run, place, out_parts, width))
    small_rows = grads0.shape[0] // PLANE
    came_end = across(send_end)

    low_parts = around(pack(run, place, (own, other), (("whole", 0), ("half", width, 2 * part)), width, None, "pack_low"))
    keep1, send1 = product_out(run, place, out_parts, out_other, width)
    mine1, send1 = add_near(run, place, keep1, swap_chips(send1, PLANE))
    small_at = (small_rows, own_small, own.shape[1])
    high_parts = around(pack(run, place, (own, other), (("half", width + part, 2 * part),), width, small_at, "pack_high"))
    keep2, send2 = product_in(run, place, low_parts, low_parts, 2 * tokens, 0, width, "product_low")
    total1 = add_far(run, place, mine1, swap_chips(send1, 2 * PLANE))
    mine2, send2 = add_near(run, place, keep2, swap_chips(send2, PLANE))
    keep3, send3 = product_in(run, place, low_parts, high_parts, 0, small_rows, width, "product_high")
    pair1 = pair_up(run, place, total1, swap_chips(total1, 2 * PLANE))
    out_q = quarter_of(run, place, pair1, swap_chips(pair1, PLANE))
    out_x, out_y = swap_chips(out_q, 1), swap_chips(out_q, 2)
    ends = place_ends(run, place, own_end, came_end)[None]
    total2 = add_far(run, place, mine2, swap_chips(send2, 2 * PLANE))
    mine3, send3 = add_near(run, place, keep3, swap_chips(send3, PLANE))
    pair2 = pair_up(run, place, total2, swap_chips(total2, 2 * PLANE))
    total3 = add_far(run, place, mine3, swap_chips(send3, 2 * PLANE))
    lower, upper = (lambda ref: [ref[0, 0], ref[0, 1]]), (lambda ref: [ref[1, 0], ref[1, 1]])
    low_q, to_x, to_y = quarter_of(
        run, place, pair2, swap_chips(pair2, PLANE), far=(out_x, out_y, lower, upper, out_q.size // 2)
    )
    low_x, low_y = swap_chips(to_x, 1), swap_chips(to_y, 2)
    pair3 = pair_up(run, place, total3, swap_chips(total3, 2 * PLANE))
    rows_out, rows_low, rows_high = out_q.shape[2], low_q.shape[2], pair3.shape[1]
    lower, upper = (lambda ref: [ref[0:2 * rows_low, :]]), (lambda ref: [ref[2 * rows_low:4 * rows_low, :]])
    high_q, to_x, to_y = quarter_of(
        run, place, pair3, swap_chips(pair3, PLANE), far=(low_x, low_y, lower, upper, low_q.size // 2)
    )
    high_x, high_y = swap_chips(to_x, 1), swap_chips(to_y, 2)
    def find_out(refs, step, z):
        if step < 3:
            return refs[step][z // 2, z % 2]
        ref = refs[3 + z // 2]
        at_row = 4 * rows_low + (z % 2) * 2 * rows_out
        return jnp.concatenate([ref[at_row:at_row + rows_out, :], ref[at_row + rows_out:at_row + 2 * rows_out, :]], axis=1)

    def find_low(refs, step, z):
        if step == 0:
            return refs[0][z // 2, z % 2]
        if step < 3:
            return refs[step][z * rows_low:(z + 1) * rows_low, :]
        at_row = 4 * rows_high + (z % 2) * rows_low
        return refs[3 + z // 2][at_row:at_row + rows_low, :]

    def find_high(refs, step, z):
        if step == 0:
            return refs[0][z // 2, z % 2]
        at_row = (z if step < 3 else z % 2) * rows_high
        return refs[step if step < 3 else 3 + z // 2][at_row:at_row + rows_high, :]

    set_out, set_low = (out_q, out_x, out_y, low_x, low_y), (low_q, low_x, low_y, high_x, high_y)
    one = (1, e)
    low_rows = rank + 2 * states
    shapes = [(low_rows, e), (rank, e), (states, e), (taps, e), one, one, one, (1, width)]
    grad_out, = spread(
        run, place, set_out, find_out, (part, width), (e, width), True, 0, 1, None, None, "spread_out"
    )
    low_half, high_half = far_halves(run, place, high_x, high_y, rows_high)
    far_low, far_high = swap_chips(low_half, 1), swap_chips(high_half, 2)
    set_high = (high_q, high_x, high_y, far_low, far_high)
    grad_in, = spread(
        run, place, set_low, find_low, (width, part), (width, 2 * e), False, 0, 2, None, None, "spread_low"
    )
    grad_in, xproj, dtproj, alog, conv_w, conv_b, dt_b, dskip, gain = spread(
        run, place, set_high, find_high, (width, part), (width, 2 * e), False, 1, 2, grad_in, (small_rows, shapes), "spread_high"
    )
    return (
        ends, gain, grad_in[None], conv_w[None], conv_b, xproj.T[None], dtproj[None], dt_b, alog[None], dskip,
        grad_out[None],
    )


def solution(mesh):
    in_specs = (
        P("section", "dp", None), P("dp", None), P("section", None), P("section", None, None),
        P("section", None, None), P("section", None), P("section", None, None), P("section", None, None),
        P("section", None), P("section", None, None), P("section", None), P("section", None, None),
    )
    out_specs = (
        P("section", "dp", None), P("section", None), P("section", None, None), P("section", None, None),
        P("section", None), P("section", None, None), P("section", None, None), P("section", None),
        P("section", None, None), P("section", None), P("section", None, None),
    )
    return jax.shard_map(per_device, mesh=mesh, in_specs=in_specs, out_specs=out_specs, check_vma=False)
```

```python
from types import SimpleNamespace

import jax
import jax.numpy as jnp
from jax import lax
from jax.experimental import pallas as pl
from jax.experimental.pallas import tpu as pltpu
from jax.sharding import PartitionSpec as P

EPSILON = 1e-05
LOG2E = 1.4426950408889634
LN2 = 0.6931471805599453
CUT = 1e6
LANES = 128
WIDE = 512
GROUP = 8
PLANE = 4
MIB = 1024 * 1024

bf16, f32 = jnp.bfloat16, jnp.float32
VMEM = pl.BlockSpec(memory_space=pltpu.VMEM)
SMEM = pl.BlockSpec(memory_space=pltpu.SMEM)
ANYWHERE = pl.BlockSpec(memory_space=pl.ANY)


def shaped(shape, kind):
    return jax.ShapeDtypeStruct(shape, kind)


def nn(a, b):
    return jnp.dot(a, b, preferred_element_type=f32)


def nt(a, b):
    return lax.dot_general(a, b, (((1,), (1,)), ((), ())), preferred_element_type=f32)


def tn(a, b):
    return lax.dot_general(a, b, (((0,), (0,)), ((), ())), preferred_element_type=f32)


def sigmoid(v):
    return 1.0 / (1.0 + jnp.exp(-v))


def with_deps(kernel, n_deps, at):
    def wrapped(*refs):
        return kernel(*refs[:at], *refs[at + n_deps:])

    return wrapped


def call(kernel, outs, args, name, smem=1, deps=(), scratch=(), limit=16, cost=None):
    specs = [SMEM] * smem + [VMEM] * (len(args) - smem) + [ANYWHERE] * len(deps)
    return pl.pallas_call(
        with_deps(kernel, len(deps), len(args)), out_shape=outs, in_specs=specs,
        out_specs=jax.tree.map(lambda _: VMEM, outs), scratch_shapes=list(scratch), name=name,
        cost_estimate=cost or pl.CostEstimate(flops=1, bytes_accessed=1, transcendentals=0),
        compiler_params=pltpu.CompilerParams(vmem_limit_bytes=limit * MIB),
    )(*args, *deps)


def pack_params(a_log, conv_weight, conv_bias, dt_bias, d_skip, norm_gain):
    rows = sum(a.shape[-2] for a in (a_log, conv_weight, conv_bias, dt_bias, d_skip, norm_gain))
    e, width = d_skip.shape[1], norm_gain.shape[1]

    def kernel(*refs):
        out = refs[-1]
        at_row = 0
        for ref in refs[:-1]:
            n, columns = ref.shape
            out[at_row:at_row + n, 0:columns] = ref[...]
            at_row += n
        out[at_row - 1:at_row, width:] = jnp.zeros((1, e - width), f32)

    args = (a_log, conv_weight, conv_bias, dt_bias, d_skip, norm_gain)
    return call(kernel, shaped((rows, e), f32), args, "pack_params", smem=0)


def make_layers(tokens, width, e, states, taps, rank):
    steps_wide = e // WIDE
    tiles = WIDE // LANES
    low_rows = rank + 2 * states
    AL, CW, CB, DB, DS, GN = 0, states, states + taps, states + taps + 1, states + taps + 2, states + taps + 3
    GX, GD = 0, low_rows
    GA = GD + rank
    GC = GA + states
    GB, GT, GS, GG = GC + taps, GC + taps + 1, GC + taps + 2, GC + taps + 3

    def wide(i, base=0):
        return pl.ds(pl.multiple_of(i * WIDE + base, LANES), WIDE)

    def tile(i, k):
        return pl.ds(pl.multiple_of(i * WIDE + k * LANES, LANES), LANES)

    def of_state(t):
        return pl.ds(pl.multiple_of(t * states, states), states)

    def grouped(value):
        return value.reshape(tokens // GROUP, GROUP, value.shape[1])

    def flat(value):
        return value.reshape(tokens, value.shape[2])

    def half_sum(value):
        return sum(value[n * 8:(n + 1) * 8] for n in range(states // 8))

    def row_sums(rows, k):
        return sum(rows[k, pl.ds(n, GROUP, stride=8), :] for n in range(8))

    def chunks(sums, here):
        return sum(sums[i, here, :] for i in range(steps_wide))

    def keep(r, k):
        return jnp.concatenate([r.offs[...]] * tiles, axis=1) >= k

    def fill_offsets(offs, lengths):
        micro = lengths.shape[0]
        count = tokens // micro
        row = lax.broadcasted_iota(jnp.int32, (tokens, LANES), 0)
        begin = jnp.zeros_like(row)
        for m in range(micro):
            a = lengths[m, 0] + m * count
            b = a + lengths[m, 1]
            begin = jnp.where(row >= m * count, m * count, begin)
            begin = jnp.where(row >= a, a, begin)
            begin = jnp.where(row >= b, b, begin)
        offs[...] = row - begin

    def fill_rate(r, l):
        r.rate[l] = -jnp.exp(r.small[l, AL:AL + states, :]) * LOG2E

    def forward(l, r):
        x = r.resid[l]
        norm = lax.rsqrt(jnp.mean(x * x, axis=1, keepdims=True) + EPSILON)
        r.nrm[l] = (x * norm * r.small[l, GN:GN + 1, 0:width]).astype(bf16)

        def project(i, _):
            c = wide(i)
            r.arrived_in(i)
            v = nn(r.nrm[l], r.in_w[l, :, c])
            r.inner[l, :, c] = v
            r.gate[l, :, c] = nn(r.nrm[l], r.in_w[l, :, wide(i, e)])
            total = r.small[l, CB:CB + 1, c] + r.small[l, CW + taps - 1:CW + taps, c] * v
            for k in range(1, taps):
                before = jnp.where(keep(r, k), pltpu.roll(v, k, 0), 0.0)
                total = total + r.small[l, CW + taps - 1 - k:CW + taps - k, c] * before
            r.conv[l, :, c] = total
            r.act[l, :, c] = (total * sigmoid(total)).astype(bf16)
            return 0

        lax.fori_loop(0, steps_wide, project, 0)
        r.arrived(l, 1)
        a = r.act[l]
        low = nt(a, r.xd_w[l, 0:rank, :]).astype(bf16)
        proj_t = nt(r.xd_w[l, 0:low_rows, :], a)
        r.low_t[l] = proj_t[0:rank].astype(bf16)
        for t in range(tokens):
            here = slice(t * states, (t + 1) * states)
            r.bb[l, here, :] = jnp.broadcast_to(proj_t[rank:rank + states, t:t + 1], (states, LANES))
            r.cb[l, here, :] = jnp.broadcast_to(proj_t[rank + states:, t:t + 1], (states, LANES))
        fill_rate(r, l)

        def scan(i, _):
            c = wide(i)
            v = nn(low, r.xd_w[l, low_rows:low_rows + rank, c]) + r.small[l, DB:DB + 1, c]
            shrunk = jnp.exp(-jnp.abs(v))
            s = jnp.maximum(v, 0.0) + jnp.log1p(shrunk)
            inverse = 1.0 / (1.0 + shrunk)
            r.sig[l, :, c] = jnp.where(v >= 0, inverse, shrunk * inverse)
            r.step[l, :, c] = s
            r.uin[l, :, :, c] = grouped(s * r.act[l, :, c].astype(f32))
            r.size[l, :, :, c] = grouped(jnp.where(keep(r, 1), s, CUT))
            rates = [r.rate[l, :, tile(i, k)] for k in range(tiles)]

            def group(g, h):
                h = list(h)
                for j in range(GROUP):
                    t = g * GROUP + j
                    bt, ct = r.bb[l, of_state(t), :], r.cb[l, of_state(t), :]
                    for k in range(tiles):
                        f = jnp.exp2(r.size[l, g, j:j + 1, tile(i, k)] * rates[k])
                        h[k] = f * h[k] + bt * r.uin[l, g, j:j + 1, tile(i, k)]
                        r.hist[l, of_state(t + 1), tile(i, k)] = h[k]
                        r.rows_a[k, j * 8:(j + 1) * 8, :] = half_sum(ct * h[k])
                for k in range(tiles):
                    r.yscan[l, g, :, tile(i, k)] = row_sums(r.rows_a, k)
                return tuple(h)

            none = tuple(jnp.zeros((states, LANES), f32) for _ in range(tiles))
            lax.fori_loop(0, tokens // GROUP, group, none)
            z = r.gate[l, :, c]
            p = flat(r.yscan[l, :, :, c]) + r.small[l, DS:DS + 1, c] * r.act[l, :, c].astype(f32)
            r.gat[l, :, c] = (p * (z * sigmoid(z))).astype(bf16)
            return 0

        lax.fori_loop(0, steps_wide, scan, 0)
        r.arrived(l, 2)
        result = x + nn(r.gat[l], r.out_w[l])
        return result

    def backward(l, r):
        r.outg[...] = r.upstream[...].astype(bf16)
        rest = r.grads_o.shape[1] - GG
        r.grads_o[0, GG:, :] = jnp.zeros((rest, e), f32)

        def scan(i, _):
            c = wide(i)
            from_out = nt(r.outg[...], r.out_w[l, c, :])
            a = r.act[l, :, c].astype(f32)
            z = r.gate[l, :, c]
            s = sigmoid(z)
            p = flat(r.yscan[l, :, :, c]) + r.small[l, DS:DS + 1, c] * a
            dp = from_out * (z * s)
            r.dyscan[:, :, c] = grouped(dp)
            r.fi[:, wide(i, width + e)] = (from_out * p * (s * (1.0 + z * (1.0 - s)))).astype(bf16)
            r.grads_o[0, GS:GS + 1, c] = jnp.sum(dp * a, axis=0, keepdims=True)
            rates = [r.rate[l, :, tile(i, k)] for k in range(tiles)]

            def group(backwards, carried):
                carry, now, drate = (list(v) for v in carried)
                g = tokens // GROUP - 1 - backwards
                for j in reversed(range(GROUP)):
                    t = g * GROUP + j
                    bt, ct = r.bb[l, of_state(t), :], r.cb[l, of_state(t), :]
                    sum_b = sum_c = None
                    for k in range(tiles):
                        sz = r.size[l, g, j:j + 1, tile(i, k)]
                        dy = r.dyscan[g, j:j + 1, tile(i, k)]
                        grad = carry[k] + ct * dy
                        part_b = grad * r.uin[l, g, j:j + 1, tile(i, k)]
                        part_c = now[k] * dy
                        sum_b = part_b if sum_b is None else sum_b + part_b
                        sum_c = part_c if sum_c is None else sum_c + part_c
                        r.rows_a[k, j * 8:(j + 1) * 8, :] = half_sum(bt * grad)
                        carry[k] = jnp.exp2(sz * rates[k]) * grad
                        now[k] = r.hist[l, of_state(t), tile(i, k)]
                        w = carry[k] * now[k]
                        r.rows_b[k, j * 8:(j + 1) * 8, :] = half_sum(w * rates[k])
                        drate[k] = drate[k] + sz * w
                    r.acc_b[i, of_state(t), :] = sum_b
                    r.acc_c[i, of_state(t), :] = sum_c
                for k in range(tiles):
                    r.dact[g, :, tile(i, k)] = row_sums(r.rows_a, k)
                    r.dsz[g, :, tile(i, k)] = row_sums(r.rows_b, k)
                return tuple(carry), tuple(now), tuple(drate)

            none = tuple(jnp.zeros((states, LANES), f32) for _ in range(tiles))
            final = tuple(r.hist[l, of_state(tokens), tile(i, k)] for k in range(tiles))
            _, _, drate = lax.fori_loop(0, tokens // GROUP, group, (none, final, none))
            for k in range(tiles):
                r.grads_o[0, GA:GA + states, tile(i, k)] = drate[k] * (rates[k] * LN2)
            du = flat(r.dact[:, :, c])
            dv = (flat(r.dsz[:, :, c]) * LN2 + du * a) * r.sig[l, :, c]
            r.dact[:, :, c] = grouped(du * r.step[l, :, c] + dp * r.small[l, DS:DS + 1, c])
            r.dtg[:, c] = dv.astype(bf16)
            r.grads_o[0, GT:GT + 1, c] = jnp.sum(dv, axis=0, keepdims=True)
            return 0

        lax.fori_loop(0, steps_wide, scan, 0)
        lane = lax.broadcasted_iota(jnp.int32, (states, LANES), 1)
        db = jnp.zeros((states, LANES), f32)
        dc = jnp.zeros((states, LANES), f32)
        for t in range(tokens):
            here = slice(t * states, (t + 1) * states)
            db = jnp.where(lane == t, jnp.sum(chunks(r.acc_b, here), axis=1, keepdims=True), db)
            dc = jnp.where(lane == t, jnp.sum(chunks(r.acc_c, here), axis=1, keepdims=True), dc)
        r.pg_t[0:rank, :] = nt(r.xd_w[l, low_rows:low_rows + rank, :], r.dtg[...]).astype(bf16)
        r.pg_t[rank:rank + states, :] = db[:, 0:tokens].astype(bf16)
        r.pg_t[rank + states:low_rows, :] = dc[:, 0:tokens].astype(bf16)

        def conv_back(i, _):
            c = wide(i)
            r.grads_o[0, GX:GX + low_rows, c] = nn(r.pg_t[...], r.act[l, :, c])
            r.grads_o[0, GD:GD + rank, c] = nn(r.low_t[l], r.dtg[:, c])
            da = tn(r.pg_t[...], r.xd_w[l, 0:low_rows, c]) + flat(r.dact[:, :, c])
            total = r.conv[l, :, c]
            s = sigmoid(total)
            dv = da * (s * (1.0 + total * (1.0 - s)))
            v = r.inner[l, :, c]
            r.grads_o[0, GB:GB + 1, c] = jnp.sum(dv, axis=0, keepdims=True)
            r.grads_o[0, GC + taps - 1:GC + taps, c] = jnp.sum(dv * v, axis=0, keepdims=True)
            dinner = r.small[l, CW + taps - 1:CW + taps, c] * dv
            for k in range(1, taps):
                kept = jnp.where(keep(r, k), dv, 0.0)
                r.grads_o[0, GC + taps - 1 - k:GC + taps - k, c] = jnp.sum(
                    kept * pltpu.roll(v, k, 0), axis=0, keepdims=True
                )
                dinner = dinner + r.small[l, CW + taps - 1 - k:CW + taps - k, c] * pltpu.roll(kept, tokens - k, 0)
            r.fi[:, wide(i, width)] = dinner.astype(bf16)
            return 0

        lax.fori_loop(0, steps_wide, conv_back, 0)
        dn = nt(r.fi[:, width:width + 2 * e], r.in_w[l])
        x = r.resid[l]
        norm = lax.rsqrt(jnp.mean(x * x, axis=1, keepdims=True) + EPSILON)
        xr = x * norm
        r.grads_o[0, GG:GG + 1, 0:width] = jnp.sum(dn * xr, axis=0, keepdims=True)
        dxr = dn * r.small[l, GN:GN + 1, 0:width]
        grad_in = r.upstream[...] + norm * (dxr - xr * jnp.mean(dxr * xr, axis=1, keepdims=True))
        return grad_in

    def fetch(me, l, own, recv, dst, sem):
        @pl.when(me == l)
        def _():
            pltpu.make_async_copy(own, dst, sem).start()

        @pl.when(me != l)
        def _():
            pltpu.make_async_copy(recv, dst, sem).start()

    def forward_kernel(
        sec, lengths, mine, theirs, small_own, small_recv,
        in_own, in_recv, xd_own, xd_recv, out_own, out_recv, *refs,
    ):
        me = sec[0]
        n = len(STATE)
        first = SimpleNamespace(**dict(zip(STATE, refs[:n])))
        out_o, own_o, other_o, in_fac, grads, up_o = refs[n:n + 6]
        sems, in_sems, *rest = refs[n + 6:]
        last = SimpleNamespace(**dict(zip(STATE, rest[:n])))
        scratch = dict(zip(SCRATCH, rest[n:]))
        for l, r in enumerate((first, last)):
            r.__dict__.update(scratch)
            r.offs = first.offs
            weights = ((xd_own, xd_recv, r.xd_w), (out_own, out_recv, r.out_w))
            for i in range(2 * steps_wide):
                here = pl.ds((i % 2) * e + (i // 2) * WIDE, WIDE)
                fetch(me, l, in_own.at[:, here], in_recv.at[:, here], r.in_w.at[0, :, here], in_sems.at[l, i])
            for k, (own, recv, dst) in enumerate(weights):
                fetch(me, l, own, recv, dst.at[0], sems.at[l, k + 1])

            def arrived(_, k, l=l, weights=weights):
                own, _, dst = weights[k - 1]
                pltpu.make_async_copy(own, dst.at[0], sems.at[l, k]).wait()

            def arrived_in(i, l=l, r=r):
                for k in range(2):
                    here = wide(i, k * e)
                    pltpu.make_async_copy(in_own.at[:, here], r.in_w.at[0, :, here], in_sems.at[l, 2 * i + k]).wait()

            r.arrived_in = arrived_in
            r.arrived = arrived
            r.hist[0, 0:states, :] = jnp.zeros((states, e), f32)
        fill_offsets(first.offs, lengths)
        last.fi = in_fac
        for core in range(2):
            @pl.when(me == core)
            def _():
                own, other = (mine, theirs) if core == 0 else (theirs, mine)
                first.resid[0] = own[...].astype(f32)
                last.outg[...] = other[...]
                last.upstream[...] = other[...].astype(f32)
                for l, r in enumerate((first, last)):
                    r.small[0] = small_own[...] if l == core else small_recv[...]

        last.resid[0] = forward(0, first).astype(bf16).astype(f32)
        out_o[...] = forward(0, last)
        up = backward(0, last).astype(bf16)
        up_o[...] = up
        in_fac[:, 0:width] = last.nrm[0]
        grads[...] = last.grads_o[0].astype(bf16)
        for core in range(2):
            @pl.when(me == core)
            def _():
                for l, to in enumerate((own_o, other_o) if core == 0 else (other_o, own_o)):
                    to[:, 0:e] = (first, last)[l].gat[0]
                    to[:, e:] = up if l == 0 else last.outg[...]

    def backward_kernel(sec, up_in, out_in, in1, grads1, *refs):
        n = len(STATE)
        r = SimpleNamespace(**dict(zip(STATE, refs[:n])))
        own, own_small, send, own_end, send_end, in_fac, grads, gin, *rest = refs[n:]
        r.__dict__.update(zip(SCRATCH, rest))
        r.fi = in_fac
        r.outg[...] = up_in[...]
        r.upstream[...] = up_in[...].astype(f32)
        gin[...] = backward(0, r)
        in_fac[:, 0:width] = r.nrm[0]
        grads[...] = r.grads_o[0].astype(bf16)
        columns, block = in_fac.shape[1], grads.shape[0] // PLANE
        for core in range(2):
            @pl.when(sec[0] == core)
            def _():
                layers = ((in_fac, grads), (in1, grads1))
                mine, theirs = layers[core], layers[1 - core]
                own[...] = mine[0][...]
                own_small[...] = mine[1][...]
                own_end[...], send_end[...] = (gin[...], out_in[...]) if core == 0 else (out_in[...], gin[...])
                send[:, 0:columns] = theirs[0][...]
                for q in range(PLANE):
                    send[0:block, columns + q * e:columns + (q + 1) * e] = theirs[1][q * block:(q + 1) * block, :]

    grad_rows = (GG + 1 + 63) // 64 * 64
    return forward_kernel, backward_kernel, grad_rows


STATE = (
    "in_w", "xd_w", "out_w", "small", "offs", "resid", "nrm", "gat", "inner", "gate", "conv", "act",
    "size", "step", "sig", "yscan", "uin", "low_t", "bb", "cb", "rate", "hist",
)
SCRATCH = (
    "grads_o", "dyscan", "dact", "dsz", "dtg", "acc_b", "acc_c", "pg_t", "upstream", "outg", "rows_a", "rows_b",
)


def run_layers(section, lengths, mine, theirs, small_own, small_recv, weights, states, taps, rank):
    tokens, width = mine.shape
    in_w, _, xd_w, _, out_w, _ = weights
    e = out_w.shape[0]
    V = pltpu.VMEM
    forward, backward, grad_rows = make_layers(tokens, width, e, states, taps, rank)
    by_token = lambda kind=f32: V((1, tokens, e), kind)
    by_row = lambda *lead: V(lead + (tokens // GROUP, GROUP, e), f32)
    by_state = lambda *lead: V(lead + (tokens * states, LANES), f32)
    sums = lambda: V((WIDE // LANES, GROUP * 8, LANES), f32)
    state = (
        V((1,) + in_w.shape, bf16), V((1,) + xd_w.shape, bf16), V((1,) + out_w.shape, bf16),
        V((1,) + small_own.shape, f32), V((tokens, LANES), jnp.int32), V((1, tokens, width), f32),
        V((1, tokens, width), bf16), by_token(bf16), by_token(), by_token(), by_token(), by_token(bf16),
        by_row(1), by_token(), by_token(), by_row(1), by_row(1), V((1, rank, tokens), bf16),
        by_state(1), by_state(1), V((1, states, e), f32), V((1, (tokens + 1) * states, e), f32),
    )
    scratch = (
        V((1, grad_rows, e), f32), by_row(), by_row(), by_row(), V((tokens, e), bf16), by_state(e // WIDE), by_state(e // WIDE),
        V((rank + 2 * states, tokens), bf16), V((tokens, width), f32), V((tokens, width), bf16), sums(), sums(),
    )
    n = len(STATE)
    work = pl.CostEstimate(flops=1 << 30, bytes_accessed=30 * MIB, transcendentals=0)
    factors, grads = shaped((tokens, width + 2 * e), bf16), shaped((grad_rows, e), bf16)
    of_out = shaped((tokens, width + e), bf16)
    outs = (V((tokens, width), f32),) + tuple(V(a.shape, bf16) for a in (of_out, of_out, factors, grads, shaped((tokens, width), bf16)))
    here = lambda a, space: pltpu.with_memory_space_constraint(a, space)
    own_hbm = [here(a, pltpu.HBM) if k % 2 == 0 else a for k, a in enumerate(weights)]
    got = pl.pallas_call(
        forward, out_shape=state + outs,
        in_specs=[SMEM, SMEM] + [VMEM] * 4 + [ANYWHERE] * 6, out_specs=(VMEM,) * (n + len(outs)),
        scratch_shapes=[pltpu.SemaphoreType.DMA((2, 3)), pltpu.SemaphoreType.DMA((2, 2 * (e // WIDE))), *state, *scratch],
        compiler_params=pltpu.CompilerParams(vmem_limit_bytes=28 * MIB), name="forward_both", cost_estimate=work,
    )(section, lengths, mine, here(theirs, pltpu.VMEM), small_own, here(small_recv, pltpu.VMEM), *own_hbm)
    held = [here(a, pltpu.VMEM) for a in got[:n]]
    out, own_o, other_o, in1, grads1, up = got[n:]

    def rest(run):
        end = shaped((tokens, width), f32)
        outs = (factors, grads, shaped((tokens, factors.shape[1] + PLANE * e), bf16), end, end)
        inner_scratch = (V(factors.shape, bf16), V(grads.shape, bf16), V(end.shape, f32)) + scratch
        args = (section, up, out, in1, grads1, *held)
        return run(backward, outs, args, "backward_first", scratch=inner_scratch, limit=16, cost=work)

    return own_o, other_o, rest


def swap_chips(array, mask):
    chips = lax.axis_size("dp")
    return lax.ppermute(array, "dp", [(i, i ^ mask) for i in range(chips)])


ORDER = (
    "pack_out", "layer_0", "across", "M0", "pack_low", "A0", "F0", "M1", "pack_high",
    "P0", "A1", "M2", "Q0", "F1", "P1", "A2", "F2", "Q1",
    "P2", "Q2", "W0", "far", "W1", "ends", "W2",
)


class Chain:
    def __init__(self, after):
        self.after = after

    def __call__(self, kernel, outs, args, name, deps=(), **options):
        if self.after is not None:
            after = self.after
            if after.dtype == f32 and after.size > MIB:
                after = pltpu.with_memory_space_constraint(after, pltpu.HBM)
            deps = (after, *deps)
        got = call(kernel, outs, args, name, deps=deps, **options)
        self.after = jax.tree.leaves(got)[-1]
        return got


def pack(run, place, sides, parts, width, rows_more, name):
    tokens = place.tokens
    half = width // 2
    rows = sum(tokens if kind == "half" else 2 * tokens for kind, *_ in parts)
    given = list(sides)
    if rows_more:
        small_rows, own_small, column_small = rows_more
        rows += 2 * small_rows
        given.append(own_small)

    def kernel(at, *refs):
        first, second = refs[:2]
        outs = refs[len(given):]
        for mask in range(PLANE):
            q = at[0] ^ mask
            out = outs[mask]
            base = 0
            for kind, column, *stride in parts:
                for k, side in enumerate((first, second)):
                    if kind == "whole":
                        out[base + k * tokens:base + (k + 1) * tokens, :] = side[:, column:column + width]
                    else:
                        cols = pl.ds(pl.multiple_of(column + q * stride[0], LANES), half)
                        out[base:base + tokens, k * half:(k + 1) * half] = side[:, cols]
                base += tokens if kind == "half" else 2 * tokens
            if rows_more:
                block = pl.ds(pl.multiple_of(q * small_rows, 16), small_rows)
                for k in range(2):
                    cols = slice(k * width, (k + 1) * width)
                    there = pl.ds(pl.multiple_of(column_small + q * 2 * width + k * width, LANES), width)
                    total = refs[2][block, cols].astype(f32) + second[0:small_rows, there].astype(f32)
                    out[base:base + small_rows, :] = total.astype(bf16)
                    base += small_rows

    return run(kernel, (shaped((rows, width), bf16),) * PLANE, (place.array, *given), name)


def place_ends(run, place, own, came):
    tokens, width = own.shape

    def kernel(at, own, came, out):
        for core in range(2):
            @pl.when(at[3] == core)
            def _():
                out[core * tokens:(core + 1) * tokens, :] = own[...]
                out[(1 - core) * tokens:(2 - core) * tokens, :] = came[...]

    return run(kernel, shaped((2 * tokens, width), f32), (place.array, own, came), "place_ends")


def other_layers(run, place, parts, send, width):
    tokens, half = place.tokens, width // 2

    def kernel(at, *refs):
        out = refs[PLANE + 1]
        for k, ref in enumerate(refs[:PLANE]):
            out[k * tokens:(k + 1) * tokens, :] = ref[tokens:2 * tokens, :]
            at_row = (PLANE + k // 2) * tokens
            out[at_row:at_row + tokens, (k % 2) * half:(k % 2 + 1) * half] = ref[2 * tokens:3 * tokens, half:width]

    outs = (shaped((PLANE * tokens * 3 // 2, width), bf16), shaped(send.shape, bf16))
    run.after, send = pl.pallas_call(
        kernel, out_shape=outs, in_specs=[SMEM] + [VMEM] * PLANE + [ANYWHERE], out_specs=(VMEM, ANYWHERE),
        input_output_aliases={PLANE + 1: 1}, name="other_layers",
        compiler_params=pltpu.CompilerParams(vmem_limit_bytes=8 * MIB),
    )(place.array, *parts, send)
    return run.after, send


def store_sums(at, total, keep, send):
    b0 = at[1]
    for j in range(2):
        keep[j] = total[j, b0]
        send[j] = total[j, 1 - b0].astype(bf16)


def product_out(run, place, parts, came, width):
    tokens, half = place.tokens, width // 2
    many = 2 * PLANE * tokens
    shape = (2, half // 4, width)

    def kernel(at, *refs):
        came, keep, send, left, right, total = refs[PLANE:]
        for k, ref in enumerate(refs[:PLANE]):
            right[k * tokens:(k + 1) * tokens, :] = ref[0:tokens, :]
            left[k * tokens:(k + 1) * tokens, :] = ref[2 * tokens:3 * tokens, 0:half]
            there = (PLANE + k) * tokens
            right[there:there + tokens, :] = came[k * tokens:(k + 1) * tokens, :]
            at_row = (PLANE + k // 2) * tokens
            left[there:there + tokens, :] = came[at_row:at_row + tokens, (k % 2) * half:(k % 2 + 1) * half]
        total[...] = tn(left[...], right[...]).reshape(2, *shape)
        store_sums(at, total, keep, send)

    V = pltpu.VMEM
    scratch = [V((many, half), bf16), V((many, width), bf16), V((2,) + shape, f32)]
    outs = (shaped(shape, f32), shaped(shape, bf16))
    return run(kernel, outs, (place.array, *parts, came), "product_out", scratch=scratch)


def product_in(run, place, tall, thin, base, small_rows, width, name):
    tokens, half = place.tokens, width // 2
    many = 2 * PLANE * tokens
    shard = width // 4
    shape = (2, shard + small_rows, half)
    args = (place.array, *tall) + (() if thin is tall else tuple(thin))

    def kernel(at, *refs):
        ins, (keep, send, left, right, total) = refs[:-5], refs[-5:]
        for k in range(PLANE):
            side = ins[-PLANE + k]
            left[2 * k * tokens:2 * (k + 1) * tokens, :] = ins[k][0:2 * tokens, :]
            for j in range(2):
                here = slice((2 * k + j) * tokens, (2 * k + j + 1) * tokens)
                right[here, :] = side[base:base + tokens, j * half:(j + 1) * half]
        total[:, :, 0:shard, :] = tn(left[...], right[...]).reshape(2, 2, shard, half)
        if small_rows:
            end = base + tokens
            mixed = sum(ins[-PLANE + k][end:end + 2 * small_rows, :].astype(f32) for k in range(PLANE))
            for b1 in range(2):
                for b0 in range(2):
                    block = mixed[b1 * small_rows:(b1 + 1) * small_rows, b0 * half:(b0 + 1) * half]
                    total[b1, b0, shard:, :] = block
        store_sums(at, total, keep, send)

    V = pltpu.VMEM
    scratch = [V((many, width), bf16), V((many, half), bf16), V((2,) + shape, f32)]
    return run(kernel, (shaped(shape, f32), shaped(shape, bf16)), args, name, scratch=scratch)


def add_near(run, place, keep, came):
    def kernel(at, keep, came, mine, send):
        b1 = at[2]
        mine[...] = keep[b1] + came[b1].astype(f32)
        send[...] = (keep[1 - b1] + came[1 - b1].astype(f32)).astype(bf16)

    shape = keep.shape[1:]
    return run(kernel, (shaped(shape, f32), shaped(shape, bf16)), (place.array, keep, came), "add_near")


def add_far(run, place, mine, came):
    def kernel(at, mine, came, out):
        out[...] = (mine[...].astype(f32) + came[...].astype(f32)).astype(bf16)

    total = run(kernel, shaped(mine.shape, bf16), (place.array, mine, came), "add_far")
    mask = 4 * PLANE
    while mask < lax.axis_size("dp"):
        total = run(kernel, shaped(mine.shape, bf16), (place.array, total, swap_chips(total, mask)), "add_far")
        mask *= 2
    return total


def pair_up(run, place, own, came):
    def kernel(at, own, came, out):
        b1 = at[2]
        out[b1] = own[...]
        out[1 - b1] = came[...]

    return run(kernel, shaped((2,) + own.shape, bf16), (place.array, own, came), "pair_up")


def quarter_of(run, place, own, came, far=None):
    rows, cols = own.shape[1:]

    def kernel(at, own, came, *rest):
        b0 = at[1]
        out = rest[0] if far is None else rest[2]
        for j in range(2):
            out[j, b0] = own[j]
            out[j, 1 - b0] = came[j]
        if far is not None:
            by_x, by_y, out, to_x, to_y = rest
            for to, ref, cut in ((to_x, by_y, far[2]), (to_y, by_x, far[3])):
                for j in range(2):
                    for i in range(2):
                        to[(2 * j + i) * rows:(2 * j + i + 1) * rows, :] = out[j, i]
                at_row = 4 * rows
                for piece in cut(ref):
                    for column in range(0, piece.shape[1], cols):
                        to[at_row:at_row + piece.shape[0], :] = piece[:, column:column + cols]
                        at_row += piece.shape[0]

    outs = shaped((2, 2, rows, cols), bf16)
    args = (place.array, own, came)
    if far is not None:
        sent = shaped((4 * rows + far[4] // cols, cols), bf16)
        outs, args = (outs, sent, sent), args + tuple(far[:2])
    return run(kernel, outs, args, "quarter_of")


def far_halves(run, place, by_x, by_y, rows):
    cols = by_x.shape[1]

    def kernel(at, by_x, by_y, low, high):
        low[...] = by_y[0:2 * rows, :]
        high[...] = by_x[2 * rows:4 * rows, :]

    return run(kernel, (shaped((2 * rows, cols), bf16),) * 2, (place.array, by_x, by_y), "far_halves")


def spread(run, place, arrays, find, columns, shape, by_rows, slot, slots, base, small, name):
    rows, cols = columns
    shard = rows // 4

    def kernel(at, *refs):
        ins, rest = refs[:len(arrays)], refs[len(arrays):]
        rest = rest[1 if base is not None else 0:]
        out, outs = rest[0], rest[1:]
        step = pl.program_id(0)
        for k in range(PLANE):
            @pl.when(step == k)
            def _(k=k):
                for z in range(4):
                    value = find(ins, k, z).astype(f32)
                    out[z * shard:(z + 1) * shard, :] = value[0:shard]
                    if small:
                        block = pl.ds(pl.multiple_of((at[0] ^ k) * small[0], 8), small[0])
                        outs[-1][block, z * cols:(z + 1) * cols] = value[shard:]

        if small:
            @pl.when(step == PLANE - 1)
            def _():
                at_row = 0
                for out_s in outs[:-1]:
                    n = out_s.shape[0]
                    out_s[...] = outs[-1][at_row:at_row + n, 0:out_s.shape[1]]
                    at_row += n

    if by_rows:
        index = lambda step, at: (at[0] ^ step, 0)
    else:
        index = lambda step, at: (0, (at[0] ^ step) * slots + slot)
    args = list(arrays)
    in_specs = [pl.BlockSpec(a.shape, lambda step, at, n=len(a.shape): (0,) * n) for a in args]
    aliases = {}
    if base is not None:
        args.append(base)
        in_specs.append(ANYWHERE)
        aliases = {len(args): 0}
    given = len(args)
    if base is None:
        big = run.after.size > MIB // 8
        args.append(pltpu.with_memory_space_constraint(run.after, pltpu.HBM) if big else run.after)
        in_specs.append(ANYWHERE)
    outs, out_specs, scratch = [pltpu.HBM(shape, f32)], [pl.BlockSpec((rows, cols), index)], []
    if small:
        for n in small[1]:
            outs.append(shaped(n, f32))
            out_specs.append(pl.BlockSpec(n, lambda step, at: (0, 0)))
        scratch = [pltpu.VMEM((PLANE * small[0], 4 * cols), f32)]
    got = pl.pallas_call(
        with_deps(kernel, len(args) - given, 1 + given), out_shape=tuple(outs),
        grid_spec=pltpu.PrefetchScalarGridSpec(
            num_scalar_prefetch=1, grid=(PLANE,), in_specs=in_specs, out_specs=tuple(out_specs), scratch_shapes=scratch,
        ),
        input_output_aliases=aliases,
        compiler_params=pltpu.CompilerParams(vmem_limit_bytes=24 * MIB), name=name,
    )(place.array, *args)
    run.after = got[-1]
    return got


def per_device(
    ends_in, lengths, norm_gain, in_weight, conv_weight, conv_bias, xproj_weight,
    dtproj_weight, dt_bias, a_log, d_skip, out_weight,
):
    section = lax.axis_index("section")
    first = section == 0
    width, e = norm_gain.shape[1], conv_bias.shape[1]
    states, taps, rank = a_log.shape[1], conv_weight.shape[1], dtproj_weight.shape[1]
    tokens = ends_in.shape[1] // 2
    micro = lengths.shape[0]

    def across(array, pairs=((0, 1), (1, 0))):
        return lax.ppermute(array, "section", pairs)

    in_recv = across(in_weight[0])
    halves = ends_in[0].reshape(2, tokens, width)
    mine = lax.dynamic_index_in_dim(halves, section, 0, keepdims=False)
    theirs = across(lax.dynamic_index_in_dim(halves, 1 - section, 0, keepdims=False))
    small_own = pack_params(a_log[0], conv_weight[0], conv_bias, dt_bias, d_skip, norm_gain)
    small_recv = across(small_own)
    xd_own = jnp.concatenate([xproj_weight[0].T, dtproj_weight[0]], axis=0)
    xd_recv = across(xd_own)
    out_recv = across(out_weight[0])
    my_lengths = lax.dynamic_slice_in_dim(lengths, section * (micro // 2), micro // 2, 0)
    weights = (in_weight[0], in_recv, xd_own, xd_recv, out_weight[0], out_recv)
    chip = lax.axis_index("dp")
    coords = jnp.stack([chip % PLANE, chip // PLANE % 2, chip // (2 * PLANE) % 2, section]).astype(jnp.int32)
    place = SimpleNamespace(array=coords, tokens=tokens)

    own_o, other_o, backward_first = run_layers(
        section.astype(jnp.int32).reshape(1), my_lengths, mine, theirs, small_own, small_recv, weights, states, taps, rank
    )

    def around(parts):
        return [parts[0]] + [swap_chips(parts[m], m) for m in range(1, PLANE)]

    part = e // PLANE
    run = Chain(None)
    h = SimpleNamespace()

    def pack_out():
        h.out_parts = around(pack(run, place, (own_o, other_o), (("whole", e), ("half", 0, part)), width, None, "pack_out"))

    def layer_0():
        h.own, h.own_small, h.send, h.own_end, h.send_end = backward_first(run)
        h.small_rows = h.own_small.shape[0] // PLANE

    def out_across():
        out_other, send = other_layers(run, place, h.out_parts, h.send, width)
        h.out_other, h.other = across(out_other), across(send)

    def pack_low():
        parts = (("whole", 0), ("half", width, 2 * part))
        h.low_parts = around(pack(run, place, (h.own, h.other), parts, width, None, "pack_low"))

    def pack_high():
        small_at = (h.small_rows, h.own_small, h.own.shape[1])
        parts = (("half", width + part, 2 * part),)
        h.high_parts = around(pack(run, place, (h.own, h.other), parts, width, small_at, "pack_high"))

    def multiply(k):
        def step():
            if k == 0:
                h.sums0 = product_out(run, place, h.out_parts, h.out_other, width)
            elif k == 1:
                h.sums1 = product_in(run, place, h.low_parts, h.low_parts, 2 * tokens, 0, width, "product_low")
            else:
                h.sums2 = product_in(run, place, h.low_parts, h.high_parts, 0, h.small_rows, width, "product_high")

        return step

    def near_sum(k):
        def step():
            keep, send = getattr(h, f"sums{k}")
            setattr(h, f"near{k}", add_near(run, place, keep, swap_chips(send, PLANE)))

        return step

    def far_sum(k):
        def step():
            mine, send = getattr(h, f"near{k}")
            setattr(h, f"total{k}", add_far(run, place, mine, swap_chips(send, 2 * PLANE)))

        return step

    def pair(k):
        def step():
            total = getattr(h, f"total{k}")
            setattr(h, f"pair{k}", pair_up(run, place, total, swap_chips(total, 2 * PLANE)))

        return step

    def quarter_out():
        h.out_q = quarter_of(run, place, h.pair0, swap_chips(h.pair0, PLANE))
        h.rows_out = h.out_q.shape[2]
        h.out_x, h.out_y = swap_chips(h.out_q, 1), swap_chips(h.out_q, 2)

    def quarter_low():
        far = (h.out_x, h.out_y, lambda ref: [ref[0, 0], ref[0, 1]], lambda ref: [ref[1, 0], ref[1, 1]], h.out_q.size // 2)
        h.low_q, to_x, to_y = quarter_of(run, place, h.pair1, swap_chips(h.pair1, PLANE), far=far)
        h.rows_low = h.low_q.shape[2]
        h.low_x, h.low_y = swap_chips(to_x, 1), swap_chips(to_y, 2)

    def quarter_high():
        n = 2 * h.rows_low
        far = (h.low_x, h.low_y, lambda ref: [ref[0:n, :]], lambda ref: [ref[n:2 * n, :]], h.low_q.size // 2)
        h.high_q, to_x, to_y = quarter_of(run, place, h.pair2, swap_chips(h.pair2, PLANE), far=far)
        h.rows_high = h.high_q.shape[2]
        h.high_x, h.high_y = swap_chips(to_x, 1), swap_chips(to_y, 2)

    def last_far():
        low_half, high_half = far_halves(run, place, h.high_x, h.high_y, h.rows_high)
        h.far_low, h.far_high = swap_chips(low_half, 1), swap_chips(high_half, 2)

    def ends_step():
        after = run.after
        h.ends = place_ends(run, place, h.own_end, across(h.send_end))[None]
        run.after = after

    def find_out(refs, step, z):
        if step < 3:
            return refs[step][z // 2, z % 2]
        ref = refs[3 + z // 2]
        at_row = 4 * h.rows_low + (z % 2) * 2 * h.rows_out
        return jnp.concatenate([ref[at_row:at_row + h.rows_out, :], ref[at_row + h.rows_out:at_row + 2 * h.rows_out, :]], axis=1)

    def find_low(refs, step, z):
        if step == 0:
            return refs[0][z // 2, z % 2]
        if step < 3:
            return refs[step][z * h.rows_low:(z + 1) * h.rows_low, :]
        at_row = 4 * h.rows_high + (z % 2) * h.rows_low
        return refs[3 + z // 2][at_row:at_row + h.rows_low, :]

    def find_high(refs, step, z):
        if step == 0:
            return refs[0][z // 2, z % 2]
        at_row = (z if step < 3 else z % 2) * h.rows_high
        return refs[step if step < 3 else 3 + z // 2][at_row:at_row + h.rows_high, :]

    def write_out():
        arrays = (h.out_q, h.out_x, h.out_y, h.low_x, h.low_y)
        h.grad_out, = spread(run, place, arrays, find_out, (part, width), (e, width), True, 0, 1, None, None, "spread_out")

    def write_low():
        arrays = (h.low_q, h.low_x, h.low_y, h.high_x, h.high_y)
        h.grad_low, = spread(
            run, place, arrays, find_low, (width, part), (width, 2 * e), False, 0, 2, None, None, "spread_low"
        )

    def write_high():
        one = (1, e)
        low_rows = rank + 2 * states
        shapes = [(low_rows, e), (rank, e), (states, e), (taps, e), one, one, one, (1, width)]
        arrays = (h.high_q, h.high_x, h.high_y, h.far_low, h.far_high)
        h.last = spread(
            run, place, arrays, find_high, (width, part), (width, 2 * e), False, 1, 2, h.grad_low, (h.small_rows, shapes),
            "spread_high",
        )

    steps = {
        "pack_out": pack_out, "layer_0": layer_0, "across": out_across, "pack_low": pack_low,
        "pack_high": pack_high, "Q0": quarter_out, "Q1": quarter_low, "Q2": quarter_high, "far": last_far,
        "ends": ends_step, "W0": write_out, "W1": write_low, "W2": write_high,
    }
    for k in range(3):
        steps.update({f"M{k}": multiply(k), f"A{k}": near_sum(k), f"F{k}": far_sum(k), f"P{k}": pair(k)})
    for name in ORDER:
        steps[name]()
    ends, grad_out = h.ends, h.grad_out
    grad_in, xproj, dtproj, alog, conv_w, conv_b, dt_b, dskip, gain = h.last
    return (
        ends, gain, grad_in[None], conv_w[None], conv_b, xproj.T[None], dtproj[None], dt_b, alog[None], dskip,
        grad_out[None],
    )


def solution(mesh):
    in_specs = (
        P("section", "dp", None), P("dp", None), P("section", None), P("section", None, None),
        P("section", None, None), P("section", None), P("section", None, None), P("section", None, None),
        P("section", None), P("section", None, None), P("section", None), P("section", None, None),
    )
    out_specs = (
        P("section", "dp", None), P("section", None), P("section", None, None), P("section", None, None),
        P("section", None), P("section", None, None), P("section", None, None), P("section", None),
        P("section", None, None), P("section", None), P("section", None, None),
    )
    return jax.shard_map(per_device, mesh=mesh, in_specs=in_specs, out_specs=out_specs, check_vma=False)
```

```python
from types import SimpleNamespace

import jax
import jax.numpy as jnp
from jax import lax
from jax.experimental import pallas as pl
from jax.experimental.pallas import tpu as pltpu
from jax.sharding import PartitionSpec as P

EPSILON = 1e-05
LOG2E = 1.4426950408889634
LN2 = 0.6931471805599453
CUT = 1e6
LANES = 128
WIDE = 512
GROUP = 8
PLANE = 4
MIB = 1024 * 1024

bf16, f32 = jnp.bfloat16, jnp.float32
VMEM = pl.BlockSpec(memory_space=pltpu.VMEM)
SMEM = pl.BlockSpec(memory_space=pltpu.SMEM)
ANYWHERE = pl.BlockSpec(memory_space=pl.ANY)


def shaped(shape, kind):
    return jax.ShapeDtypeStruct(shape, kind)


def nn(a, b):
    return jnp.dot(a, b, preferred_element_type=f32)


def nt(a, b):
    return lax.dot_general(a, b, (((1,), (1,)), ((), ())), preferred_element_type=f32)


def tn(a, b):
    return lax.dot_general(a, b, (((0,), (0,)), ((), ())), preferred_element_type=f32)


def sigmoid(v):
    return 1.0 / (1.0 + jnp.exp(-v))


def with_deps(kernel, n_deps, at):
    def wrapped(*refs):
        return kernel(*refs[:at], *refs[at + n_deps:])

    return wrapped


def call(kernel, outs, args, name, smem=1, deps=(), scratch=(), limit=16, cost=None):
    specs = [SMEM] * smem + [VMEM] * (len(args) - smem) + [ANYWHERE] * len(deps)
    return pl.pallas_call(
        with_deps(kernel, len(deps), len(args)), out_shape=outs, in_specs=specs,
        out_specs=jax.tree.map(lambda _: VMEM, outs), scratch_shapes=list(scratch), name=name,
        cost_estimate=cost or pl.CostEstimate(flops=1, bytes_accessed=1, transcendentals=0),
        compiler_params=pltpu.CompilerParams(vmem_limit_bytes=limit * MIB),
    )(*args, *deps)


def pack_params(a_log, conv_weight, conv_bias, dt_bias, d_skip, norm_gain):
    rows = sum(a.shape[-2] for a in (a_log, conv_weight, conv_bias, dt_bias, d_skip, norm_gain))
    e, width = d_skip.shape[1], norm_gain.shape[1]

    def kernel(*refs):
        out = refs[-1]
        at_row = 0
        for ref in refs[:-1]:
            n, columns = ref.shape
            out[at_row:at_row + n, 0:columns] = ref[...]
            at_row += n
        out[at_row - 1:at_row, width:] = jnp.zeros((1, e - width), f32)

    args = (a_log, conv_weight, conv_bias, dt_bias, d_skip, norm_gain)
    return call(kernel, shaped((rows, e), f32), args, "pack_params", smem=0)


def make_layers(tokens, width, e, states, taps, rank):
    steps_wide = e // WIDE
    tiles = WIDE // LANES
    low_rows = rank + 2 * states
    AL, CW, CB, DB, DS, GN = 0, states, states + taps, states + taps + 1, states + taps + 2, states + taps + 3
    GX, GD = 0, low_rows
    GA = GD + rank
    GC = GA + states
    GB, GT, GS, GG = GC + taps, GC + taps + 1, GC + taps + 2, GC + taps + 3

    def wide(i, base=0):
        return pl.ds(pl.multiple_of(i * WIDE + base, LANES), WIDE)

    def tile(i, k):
        return pl.ds(pl.multiple_of(i * WIDE + k * LANES, LANES), LANES)

    def of_state(t):
        return pl.ds(pl.multiple_of(t * states, states), states)

    def grouped(value):
        return value.reshape(tokens // GROUP, GROUP, value.shape[1])

    def flat(value):
        return value.reshape(tokens, value.shape[2])

    def half_sum(value):
        return sum(value[n * 8:(n + 1) * 8] for n in range(states // 8))

    def row_sums(rows, k):
        return sum(rows[k, pl.ds(n, GROUP, stride=8), :] for n in range(8))

    def chunks(sums, here):
        return sum(sums[i, here, :] for i in range(steps_wide))

    def keep(r, k):
        return jnp.concatenate([r.offs[...]] * tiles, axis=1) >= k

    def fill_offsets(offs, lengths):
        micro = lengths.shape[0]
        count = tokens // micro
        row = lax.broadcasted_iota(jnp.int32, (tokens, LANES), 0)
        begin = jnp.zeros_like(row)
        for m in range(micro):
            a = lengths[m, 0] + m * count
            b = a + lengths[m, 1]
            begin = jnp.where(row >= m * count, m * count, begin)
            begin = jnp.where(row >= a, a, begin)
            begin = jnp.where(row >= b, b, begin)
        offs[...] = row - begin

    def fill_rate(r, l):
        r.rate[l] = -jnp.exp(r.small[l, AL:AL + states, :]) * LOG2E

    def forward(l, r):
        x = r.resid[l]
        norm = lax.rsqrt(jnp.mean(x * x, axis=1, keepdims=True) + EPSILON)
        r.nrm[l] = (x * norm * r.small[l, GN:GN + 1, 0:width]).astype(bf16)

        def project(i, _):
            c = wide(i)
            r.arrived_in(i)
            v = nn(r.nrm[l], r.in_w[l, :, c])
            r.inner[l, :, c] = v
            r.gate[l, :, c] = nn(r.nrm[l], r.in_w[l, :, wide(i, e)])
            total = r.small[l, CB:CB + 1, c] + r.small[l, CW + taps - 1:CW + taps, c] * v
            for k in range(1, taps):
                before = jnp.where(keep(r, k), pltpu.roll(v, k, 0), 0.0)
                total = total + r.small[l, CW + taps - 1 - k:CW + taps - k, c] * before
            r.conv[l, :, c] = total
            r.act[l, :, c] = (total * sigmoid(total)).astype(bf16)
            return 0

        lax.fori_loop(0, steps_wide, project, 0)
        r.arrived(l, 1)
        a = r.act[l]
        low = nt(a, r.xd_w[l, 0:rank, :]).astype(bf16)
        proj_t = nt(r.xd_w[l, 0:low_rows, :], a)
        r.low_t[l] = proj_t[0:rank].astype(bf16)
        for t in range(tokens):
            here = slice(t * states, (t + 1) * states)
            r.bb[l, here, :] = jnp.broadcast_to(proj_t[rank:rank + states, t:t + 1], (states, LANES))
            r.cb[l, here, :] = jnp.broadcast_to(proj_t[rank + states:, t:t + 1], (states, LANES))
        fill_rate(r, l)

        def scan(i, _):
            c = wide(i)
            v = nn(low, r.xd_w[l, low_rows:low_rows + rank, c]) + r.small[l, DB:DB + 1, c]
            shrunk = jnp.exp(-jnp.abs(v))
            s = jnp.maximum(v, 0.0) + jnp.log1p(shrunk)
            inverse = 1.0 / (1.0 + shrunk)
            r.sig[l, :, c] = jnp.where(v >= 0, inverse, shrunk * inverse)
            r.step[l, :, c] = s
            r.uin[l, :, :, c] = grouped(s * r.act[l, :, c].astype(f32))
            r.size[l, :, :, c] = grouped(jnp.where(keep(r, 1), s, CUT))
            rates = [r.rate[l, :, tile(i, k)] for k in range(tiles)]

            def group(g, h):
                h = list(h)
                for j in range(GROUP):
                    t = g * GROUP + j
                    bt, ct = r.bb[l, of_state(t), :], r.cb[l, of_state(t), :]
                    for k in range(tiles):
                        f = jnp.exp2(r.size[l, g, j:j + 1, tile(i, k)] * rates[k])
                        h[k] = f * h[k] + bt * r.uin[l, g, j:j + 1, tile(i, k)]
                        r.hist[l, of_state(t + 1), tile(i, k)] = h[k]
                        r.rows_a[k, j * 8:(j + 1) * 8, :] = half_sum(ct * h[k])
                for k in range(tiles):
                    r.yscan[l, g, :, tile(i, k)] = row_sums(r.rows_a, k)
                return tuple(h)

            none = tuple(jnp.zeros((states, LANES), f32) for _ in range(tiles))
            lax.fori_loop(0, tokens // GROUP, group, none)
            z = r.gate[l, :, c]
            p = flat(r.yscan[l, :, :, c]) + r.small[l, DS:DS + 1, c] * r.act[l, :, c].astype(f32)
            r.gat[l, :, c] = (p * (z * sigmoid(z))).astype(bf16)
            return 0

        lax.fori_loop(0, steps_wide, scan, 0)
        r.arrived(l, 2)
        result = x + nn(r.gat[l], r.out_w[l])
        return result

    def backward(l, r):
        r.outg[...] = r.upstream[...].astype(bf16)
        rest = r.grads_o.shape[1] - GG
        r.grads_o[0, GG:, :] = jnp.zeros((rest, e), f32)

        def scan(i, _):
            c = wide(i)
            from_out = nt(r.outg[...], r.out_w[l, c, :])
            a = r.act[l, :, c].astype(f32)
            z = r.gate[l, :, c]
            s = sigmoid(z)
            p = flat(r.yscan[l, :, :, c]) + r.small[l, DS:DS + 1, c] * a
            dp = from_out * (z * s)
            r.dyscan[:, :, c] = grouped(dp)
            r.fi[:, wide(i, width + e)] = (from_out * p * (s * (1.0 + z * (1.0 - s)))).astype(bf16)
            r.grads_o[0, GS:GS + 1, c] = jnp.sum(dp * a, axis=0, keepdims=True)
            rates = [r.rate[l, :, tile(i, k)] for k in range(tiles)]

            def group(backwards, carried):
                carry, now, drate = (list(v) for v in carried)
                g = tokens // GROUP - 1 - backwards
                for j in reversed(range(GROUP)):
                    t = g * GROUP + j
                    bt, ct = r.bb[l, of_state(t), :], r.cb[l, of_state(t), :]
                    sum_b = sum_c = None
                    for k in range(tiles):
                        sz = r.size[l, g, j:j + 1, tile(i, k)]
                        dy = r.dyscan[g, j:j + 1, tile(i, k)]
                        grad = carry[k] + ct * dy
                        part_b = grad * r.uin[l, g, j:j + 1, tile(i, k)]
                        part_c = now[k] * dy
                        sum_b = part_b if sum_b is None else sum_b + part_b
                        sum_c = part_c if sum_c is None else sum_c + part_c
                        r.rows_a[k, j * 8:(j + 1) * 8, :] = half_sum(bt * grad)
                        carry[k] = jnp.exp2(sz * rates[k]) * grad
                        now[k] = r.hist[l, of_state(t), tile(i, k)]
                        w = carry[k] * now[k]
                        r.rows_b[k, j * 8:(j + 1) * 8, :] = half_sum(w * rates[k])
                        drate[k] = drate[k] + sz * w
                    r.acc_b[i, of_state(t), :] = sum_b
                    r.acc_c[i, of_state(t), :] = sum_c
                for k in range(tiles):
                    r.dact[g, :, tile(i, k)] = row_sums(r.rows_a, k)
                    r.dsz[g, :, tile(i, k)] = row_sums(r.rows_b, k)
                return tuple(carry), tuple(now), tuple(drate)

            none = tuple(jnp.zeros((states, LANES), f32) for _ in range(tiles))
            final = tuple(r.hist[l, of_state(tokens), tile(i, k)] for k in range(tiles))
            _, _, drate = lax.fori_loop(0, tokens // GROUP, group, (none, final, none))
            for k in range(tiles):
                r.grads_o[0, GA:GA + states, tile(i, k)] = drate[k] * (rates[k] * LN2)
            du = flat(r.dact[:, :, c])
            dv = (flat(r.dsz[:, :, c]) * LN2 + du * a) * r.sig[l, :, c]
            r.dact[:, :, c] = grouped(du * r.step[l, :, c] + dp * r.small[l, DS:DS + 1, c])
            r.dtg[:, c] = dv.astype(bf16)
            r.grads_o[0, GT:GT + 1, c] = jnp.sum(dv, axis=0, keepdims=True)
            return 0

        lax.fori_loop(0, steps_wide, scan, 0)
        lane = lax.broadcasted_iota(jnp.int32, (states, LANES), 1)
        db = jnp.zeros((states, LANES), f32)
        dc = jnp.zeros((states, LANES), f32)
        for t in range(tokens):
            here = slice(t * states, (t + 1) * states)
            db = jnp.where(lane == t, jnp.sum(chunks(r.acc_b, here), axis=1, keepdims=True), db)
            dc = jnp.where(lane == t, jnp.sum(chunks(r.acc_c, here), axis=1, keepdims=True), dc)
        r.pg_t[0:rank, :] = nt(r.xd_w[l, low_rows:low_rows + rank, :], r.dtg[...]).astype(bf16)
        r.pg_t[rank:rank + states, :] = db[:, 0:tokens].astype(bf16)
        r.pg_t[rank + states:low_rows, :] = dc[:, 0:tokens].astype(bf16)

        def conv_back(i, _):
            c = wide(i)
            r.grads_o[0, GX:GX + low_rows, c] = nn(r.pg_t[...], r.act[l, :, c])
            r.grads_o[0, GD:GD + rank, c] = nn(r.low_t[l], r.dtg[:, c])
            da = tn(r.pg_t[...], r.xd_w[l, 0:low_rows, c]) + flat(r.dact[:, :, c])
            total = r.conv[l, :, c]
            s = sigmoid(total)
            dv = da * (s * (1.0 + total * (1.0 - s)))
            v = r.inner[l, :, c]
            r.grads_o[0, GB:GB + 1, c] = jnp.sum(dv, axis=0, keepdims=True)
            r.grads_o[0, GC + taps - 1:GC + taps, c] = jnp.sum(dv * v, axis=0, keepdims=True)
            dinner = r.small[l, CW + taps - 1:CW + taps, c] * dv
            for k in range(1, taps):
                kept = jnp.where(keep(r, k), dv, 0.0)
                r.grads_o[0, GC + taps - 1 - k:GC + taps - k, c] = jnp.sum(
                    kept * pltpu.roll(v, k, 0), axis=0, keepdims=True
                )
                dinner = dinner + r.small[l, CW + taps - 1 - k:CW + taps - k, c] * pltpu.roll(kept, tokens - k, 0)
            r.fi[:, wide(i, width)] = dinner.astype(bf16)
            return 0

        lax.fori_loop(0, steps_wide, conv_back, 0)
        dn = nt(r.fi[:, width:width + 2 * e], r.in_w[l])
        x = r.resid[l]
        norm = lax.rsqrt(jnp.mean(x * x, axis=1, keepdims=True) + EPSILON)
        xr = x * norm
        r.grads_o[0, GG:GG + 1, 0:width] = jnp.sum(dn * xr, axis=0, keepdims=True)
        dxr = dn * r.small[l, GN:GN + 1, 0:width]
        grad_in = r.upstream[...] + norm * (dxr - xr * jnp.mean(dxr * xr, axis=1, keepdims=True))
        return grad_in

    def fetch(me, l, own, recv, dst, sem):
        @pl.when(me == l)
        def _():
            pltpu.make_async_copy(own, dst, sem).start()

        @pl.when(me != l)
        def _():
            pltpu.make_async_copy(recv, dst, sem).start()

    def forward_kernel(
        sec, lengths, mine, theirs, small_own, small_recv,
        in_own, in_recv, xd_own, xd_recv, out_own, out_recv, *refs,
    ):
        me = sec[3]
        n = len(STATE)
        first = SimpleNamespace(**dict(zip(STATE, refs[:n])))
        out_o, *sends, in_fac, grads, up_o = refs[n:n + 4 + PLANE]
        sems, in_sems, *rest = refs[n + 4 + PLANE:]
        last = SimpleNamespace(**dict(zip(STATE, rest[:n])))
        scratch = dict(zip(SCRATCH, rest[n:]))
        for l, r in enumerate((first, last)):
            r.__dict__.update(scratch)
            r.offs = first.offs
            weights = ((xd_own, xd_recv, r.xd_w), (out_own, out_recv, r.out_w))
            for i in range(2 * steps_wide):
                here = pl.ds((i % 2) * e + (i // 2) * WIDE, WIDE)
                fetch(me, l, in_own.at[:, here], in_recv.at[:, here], r.in_w.at[0, :, here], in_sems.at[l, i])
            for k, (own, recv, dst) in enumerate(weights):
                fetch(me, l, own, recv, dst.at[0], sems.at[l, k + 1])

            def arrived(_, k, l=l, weights=weights):
                own, _, dst = weights[k - 1]
                pltpu.make_async_copy(own, dst.at[0], sems.at[l, k]).wait()

            def arrived_in(i, l=l, r=r):
                for k in range(2):
                    here = wide(i, k * e)
                    pltpu.make_async_copy(in_own.at[:, here], r.in_w.at[0, :, here], in_sems.at[l, 2 * i + k]).wait()

            r.arrived_in = arrived_in
            r.arrived = arrived
            r.hist[0, 0:states, :] = jnp.zeros((states, e), f32)
        fill_offsets(first.offs, lengths)
        last.fi = in_fac
        for core in range(2):
            @pl.when(me == core)
            def _():
                own, other = (mine, theirs) if core == 0 else (theirs, mine)
                first.resid[0] = own[...].astype(f32)
                last.outg[...] = other[...]
                last.upstream[...] = other[...].astype(f32)
                for l, r in enumerate((first, last)):
                    r.small[0] = small_own[...] if l == core else small_recv[...]

        last.resid[0] = forward(0, first).astype(bf16).astype(f32)
        out_o[...] = forward(0, last)
        up = backward(0, last).astype(bf16)
        up_o[...] = up
        in_fac[:, 0:width] = last.nrm[0]
        grads[...] = last.grads_o[0].astype(bf16)
        for core in range(2):
            @pl.when(me == core)
            def _():
                layers = ((first.gat, up), (last.gat, last.outg[...]))[:: 1 if core == 0 else -1]
                part = e // PLANE
                for mask, send in enumerate(sends):
                    cols = pl.ds(pl.multiple_of((sec[0] ^ mask) * part, LANES), part)
                    for k, (gated, grad) in enumerate(layers):
                        send[k * tokens:(k + 1) * tokens, :] = grad
                        send[2 * tokens:3 * tokens, k * part:(k + 1) * part] = gated[0, :, cols]

    def backward_kernel(sec, up_in, out_in, in1, grads1, *refs):
        n = len(STATE)
        r = SimpleNamespace(**dict(zip(STATE, refs[:n])))
        own, own_small, send, own_end, send_end, in_fac, grads, gin, *rest = refs[n:]
        r.__dict__.update(zip(SCRATCH, rest))
        r.fi = in_fac
        r.outg[...] = up_in[...]
        r.upstream[...] = up_in[...].astype(f32)
        gin[...] = backward(0, r)
        in_fac[:, 0:width] = r.nrm[0]
        grads[...] = r.grads_o[0].astype(bf16)
        columns, block = in_fac.shape[1], grads.shape[0] // PLANE
        for core in range(2):
            @pl.when(sec[3] == core)
            def _():
                layers = ((in_fac, grads), (in1, grads1))
                mine, theirs = layers[core], layers[1 - core]
                own[...] = mine[0][...]
                own_small[...] = mine[1][...]
                own_end[...], send_end[...] = (gin[...], out_in[...]) if core == 0 else (out_in[...], gin[...])
                send[:, 0:columns] = theirs[0][...]
                for q in range(PLANE):
                    send[0:block, columns + q * e:columns + (q + 1) * e] = theirs[1][q * block:(q + 1) * block, :]

    grad_rows = (GG + 1 + 63) // 64 * 64
    return forward_kernel, backward_kernel, grad_rows


STATE = (
    "in_w", "xd_w", "out_w", "small", "offs", "resid", "nrm", "gat", "inner", "gate", "conv", "act",
    "size", "step", "sig", "yscan", "uin", "low_t", "bb", "cb", "rate", "hist",
)
SCRATCH = (
    "grads_o", "dyscan", "dact", "dsz", "dtg", "acc_b", "acc_c", "pg_t", "upstream", "outg", "rows_a", "rows_b",
)


def run_layers(section, lengths, mine, theirs, small_own, small_recv, weights, states, taps, rank):
    tokens, width = mine.shape
    in_w, _, xd_w, _, out_w, _ = weights
    e = out_w.shape[0]
    V = pltpu.VMEM
    forward, backward, grad_rows = make_layers(tokens, width, e, states, taps, rank)
    by_token = lambda kind=f32: V((1, tokens, e), kind)
    by_row = lambda *lead: V(lead + (tokens // GROUP, GROUP, e), f32)
    by_state = lambda *lead: V(lead + (tokens * states, LANES), f32)
    sums = lambda: V((WIDE // LANES, GROUP * 8, LANES), f32)
    state = (
        V((1,) + in_w.shape, bf16), V((1,) + xd_w.shape, bf16), V((1,) + out_w.shape, bf16),
        V((1,) + small_own.shape, f32), V((tokens, LANES), jnp.int32), V((1, tokens, width), f32),
        V((1, tokens, width), bf16), by_token(bf16), by_token(), by_token(), by_token(), by_token(bf16),
        by_row(1), by_token(), by_token(), by_row(1), by_row(1), V((1, rank, tokens), bf16),
        by_state(1), by_state(1), V((1, states, e), f32), V((1, (tokens + 1) * states, e), f32),
    )
    scratch = (
        V((1, grad_rows, e), f32), by_row(), by_row(), by_row(), V((tokens, e), bf16), by_state(e // WIDE), by_state(e // WIDE),
        V((rank + 2 * states, tokens), bf16), V((tokens, width), f32), V((tokens, width), bf16), sums(), sums(),
    )
    n = len(STATE)
    work = pl.CostEstimate(flops=1 << 30, bytes_accessed=30 * MIB, transcendentals=0)
    factors, grads = shaped((tokens, width + 2 * e), bf16), shaped((grad_rows, e), bf16)
    of_out = shaped((3 * tokens, width), bf16)
    outs = (V((tokens, width), f32),) + tuple(V(a.shape, bf16) for a in (*(of_out,) * PLANE, factors, grads, shaped((tokens, width), bf16)))
    here = lambda a, space: pltpu.with_memory_space_constraint(a, space)
    own_hbm = [here(a, pltpu.HBM) if k % 2 == 0 else a for k, a in enumerate(weights)]
    got = pl.pallas_call(
        forward, out_shape=state + outs,
        in_specs=[SMEM, SMEM] + [VMEM] * 4 + [ANYWHERE] * 6, out_specs=(VMEM,) * (n + len(outs)),
        scratch_shapes=[pltpu.SemaphoreType.DMA((2, 3)), pltpu.SemaphoreType.DMA((2, 2 * (e // WIDE))), *state, *scratch],
        compiler_params=pltpu.CompilerParams(vmem_limit_bytes=28 * MIB), name="forward_both", cost_estimate=work,
    )(section, lengths, mine, here(theirs, pltpu.VMEM), small_own, here(small_recv, pltpu.VMEM), *own_hbm)
    held = [here(a, pltpu.VMEM) for a in got[:n]]
    out, *sends, in1, grads1, up = got[n:]

    def rest(run):
        end = shaped((tokens, width), f32)
        outs = (factors, grads, shaped((tokens, factors.shape[1] + PLANE * e), bf16), end, end)
        inner_scratch = (V(factors.shape, bf16), V(grads.shape, bf16), V(end.shape, f32)) + scratch
        args = (section, up, out, in1, grads1, *held)
        return run(backward, outs, args, "backward_first", scratch=inner_scratch, limit=16, cost=work)

    return sends, rest


def swap_chips(array, mask):
    chips = lax.axis_size("dp")
    return lax.ppermute(array, "dp", [(i, i ^ mask) for i in range(chips)])


ORDER = (
    "pack_out", "layer_0", "across", "M0", "pack_low", "A0", "F0", "M1", "pack_high",
    "P0", "A1", "M2", "Q0", "F1", "P1", "A2", "F2", "Q1",
    "P2", "Q2", "ends", "W0", "far", "W1", "W2", "W3",
)


class Chain:
    def __init__(self, after):
        self.after = after

    def __call__(self, kernel, outs, args, name, deps=(), **options):
        if self.after is not None:
            after = self.after
            if after.dtype == f32 and after.size > MIB // 16:
                after = pltpu.with_memory_space_constraint(after, pltpu.HBM)
            deps = (after, *deps)
        got = call(kernel, outs, args, name, deps=deps, **options)
        self.after = jax.tree.leaves(got)[-1]
        return got


def pack(run, place, sides, parts, width, rows_more, name):
    tokens = place.tokens
    half = width // 2
    rows = sum(tokens if kind == "half" else 2 * tokens for kind, *_ in parts)
    given = list(sides)
    if rows_more:
        small_rows, own_small, column_small = rows_more
        rows += 2 * small_rows
        given.append(own_small)

    def kernel(at, *refs):
        first, second = refs[:2]
        outs = refs[len(given):]
        for mask in range(PLANE):
            q = at[0] ^ mask
            out = outs[mask]
            base = 0
            for kind, column, *stride in parts:
                for k, side in enumerate((first, second)):
                    if kind == "whole":
                        out[base + k * tokens:base + (k + 1) * tokens, :] = side[:, column:column + width]
                    else:
                        cols = pl.ds(pl.multiple_of(column + q * stride[0], LANES), half)
                        out[base:base + tokens, k * half:(k + 1) * half] = side[:, cols]
                base += tokens if kind == "half" else 2 * tokens
            if rows_more:
                block = pl.ds(pl.multiple_of(q * small_rows, 16), small_rows)
                for k in range(2):
                    cols = slice(k * width, (k + 1) * width)
                    there = pl.ds(pl.multiple_of(column_small + q * 2 * width + k * width, LANES), width)
                    total = refs[2][block, cols].astype(f32) + second[0:small_rows, there].astype(f32)
                    out[base:base + small_rows, :] = total.astype(bf16)
                    base += small_rows

    return run(kernel, (shaped((rows, width), bf16),) * PLANE, (place.array, *given), name)


def place_ends(run, place, own, came):
    tokens, width = own.shape

    def kernel(at, own, came, out):
        for core in range(2):
            @pl.when(at[3] == core)
            def _():
                out[core * tokens:(core + 1) * tokens, :] = own[...]
                out[(1 - core) * tokens:(2 - core) * tokens, :] = came[...]

    return run(kernel, shaped((2 * tokens, width), f32), (place.array, own, came), "place_ends")


def other_layers(run, place, parts, send, width):
    tokens, half = place.tokens, width // 2

    def kernel(at, *refs):
        out = refs[PLANE + 1]
        for k, ref in enumerate(refs[:PLANE]):
            out[k * tokens:(k + 1) * tokens, :] = ref[tokens:2 * tokens, :]
            at_row = (PLANE + k // 2) * tokens
            out[at_row:at_row + tokens, (k % 2) * half:(k % 2 + 1) * half] = ref[2 * tokens:3 * tokens, half:width]

    outs = (shaped((PLANE * tokens * 3 // 2, width), bf16), shaped(send.shape, bf16))
    run.after, send = pl.pallas_call(
        kernel, out_shape=outs, in_specs=[SMEM] + [VMEM] * PLANE + [ANYWHERE], out_specs=(VMEM, ANYWHERE),
        input_output_aliases={PLANE + 1: 1}, name="other_layers",
        compiler_params=pltpu.CompilerParams(vmem_limit_bytes=8 * MIB),
    )(place.array, *parts, send)
    return run.after, send


def store_sums(at, total, keep, send):
    b0 = at[1]
    for j in range(2):
        keep[j] = total[j, b0]
        send[j] = total[j, 1 - b0].astype(bf16)


def product_out(run, place, parts, came, width):
    tokens, half = place.tokens, width // 2
    many = 2 * PLANE * tokens
    shape = (2, half // 4, width)

    def kernel(at, *refs):
        came, keep, send, left, right, total = refs[PLANE:]
        for k, ref in enumerate(refs[:PLANE]):
            right[k * tokens:(k + 1) * tokens, :] = ref[0:tokens, :]
            left[k * tokens:(k + 1) * tokens, :] = ref[2 * tokens:3 * tokens, 0:half]
            there = (PLANE + k) * tokens
            right[there:there + tokens, :] = came[k * tokens:(k + 1) * tokens, :]
            at_row = (PLANE + k // 2) * tokens
            left[there:there + tokens, :] = came[at_row:at_row + tokens, (k % 2) * half:(k % 2 + 1) * half]
        total[...] = tn(left[...], right[...]).reshape(2, *shape)
        store_sums(at, total, keep, send)

    V = pltpu.VMEM
    scratch = [V((many, half), bf16), V((many, width), bf16), V((2,) + shape, f32)]
    outs = (shaped(shape, f32), shaped(shape, bf16))
    return run(kernel, outs, (place.array, *parts, came), "product_out", scratch=scratch)


def product_in(run, place, tall, thin, base, small_rows, width, name):
    tokens, half = place.tokens, width // 2
    many = 2 * PLANE * tokens
    shard = width // 4
    shape = (2, shard + small_rows, half)
    args = (place.array, *tall) + (() if thin is tall else tuple(thin))

    def kernel(at, *refs):
        ins, (keep, send, left, right, total) = refs[:-5], refs[-5:]
        for k in range(PLANE):
            side = ins[-PLANE + k]
            left[2 * k * tokens:2 * (k + 1) * tokens, :] = ins[k][0:2 * tokens, :]
            for j in range(2):
                here = slice((2 * k + j) * tokens, (2 * k + j + 1) * tokens)
                right[here, :] = side[base:base + tokens, j * half:(j + 1) * half]
        total[:, :, 0:shard, :] = tn(left[...], right[...]).reshape(2, 2, shard, half)
        if small_rows:
            end = base + tokens
            mixed = sum(ins[-PLANE + k][end:end + 2 * small_rows, :].astype(f32) for k in range(PLANE))
            for b1 in range(2):
                for b0 in range(2):
                    block = mixed[b1 * small_rows:(b1 + 1) * small_rows, b0 * half:(b0 + 1) * half]
                    total[b1, b0, shard:, :] = block
        store_sums(at, total, keep, send)

    V = pltpu.VMEM
    scratch = [V((many, width), bf16), V((many, half), bf16), V((2,) + shape, f32)]
    return run(kernel, (shaped(shape, f32), shaped(shape, bf16)), args, name, scratch=scratch)


def add_near(run, place, keep, came):
    def kernel(at, keep, came, mine, send):
        b1 = at[2]
        mine[...] = keep[b1] + came[b1].astype(f32)
        send[...] = (keep[1 - b1] + came[1 - b1].astype(f32)).astype(bf16)

    shape = keep.shape[1:]
    return run(kernel, (shaped(shape, f32), shaped(shape, bf16)), (place.array, keep, came), "add_near")


def add_far(run, place, mine, came):
    def kernel(at, mine, came, out):
        out[...] = (mine[...].astype(f32) + came[...].astype(f32)).astype(bf16)

    total = run(kernel, shaped(mine.shape, bf16), (place.array, mine, came), "add_far")
    mask = 4 * PLANE
    while mask < lax.axis_size("dp"):
        total = run(kernel, shaped(mine.shape, bf16), (place.array, total, swap_chips(total, mask)), "add_far")
        mask *= 2
    return total


def pair_up(run, place, own, came):
    def kernel(at, own, came, out):
        b1 = at[2]
        out[b1] = own[...]
        out[1 - b1] = came[...]

    return run(kernel, shaped((2,) + own.shape, bf16), (place.array, own, came), "pair_up")


def quarter_of(run, place, own, came, far=None):
    rows, cols = own.shape[1:]

    def kernel(at, own, came, *rest):
        b0 = at[1]
        out = rest[0] if far is None else rest[2]
        for j in range(2):
            out[j, b0] = own[j]
            out[j, 1 - b0] = came[j]
        if far is not None:
            by_x, by_y, out, to_x, to_y = rest
            for to, ref, cut in ((to_x, by_y, far[2]), (to_y, by_x, far[3])):
                for j in range(2):
                    for i in range(2):
                        to[(2 * j + i) * rows:(2 * j + i + 1) * rows, :] = out[j, i]
                at_row = 4 * rows
                for piece in cut(ref):
                    for column in range(0, piece.shape[1], cols):
                        to[at_row:at_row + piece.shape[0], :] = piece[:, column:column + cols]
                        at_row += piece.shape[0]

    outs = shaped((2, 2, rows, cols), bf16)
    args = (place.array, own, came)
    if far is not None:
        sent = shaped((4 * rows + far[4] // cols, cols), bf16)
        outs, args = (outs, sent, sent), args + tuple(far[:2])
    return run(kernel, outs, args, "quarter_of")


def far_halves(run, place, by_x, by_y, rows):
    cols = by_x.shape[1]

    def kernel(at, by_x, by_y, low, high):
        low[...] = by_y[0:2 * rows, :]
        high[...] = by_x[2 * rows:4 * rows, :]

    return run(kernel, (shaped((2 * rows, cols), bf16),) * 2, (place.array, by_x, by_y), "far_halves")


def spread(run, place, arrays, find, columns, shape, by_rows, slot, slots, base, small, name, masks=range(PLANE)):
    rows, cols = columns
    shard = rows // 4

    def kernel(at, *refs):
        ins, rest = refs[:len(arrays)], refs[len(arrays):]
        rest = rest[1 if base is not None else 0:]
        out, outs = rest[0], rest[1:]
        step = pl.program_id(0)
        for k in masks:
            @pl.when(step == k - masks[0])
            def _(k=k):
                for z in range(4):
                    out[z * shard:(z + 1) * shard, :] = find(ins, k, z)[0:shard, :].astype(f32)

        if small:
            for k in range(PLANE):
                block = pl.ds(pl.multiple_of((at[0] ^ k) * small[0], 8), small[0])
                for z in range(4):
                    outs[-1][block, z * cols:(z + 1) * cols] = find(ins, k, z)[shard:, :].astype(f32)
            at_row = 0
            for out_s in outs[:-1]:
                n = out_s.shape[0]
                out_s[...] = outs[-1][at_row:at_row + n, 0:out_s.shape[1]]
                at_row += n

    if by_rows:
        index = lambda step, at: (at[0] ^ (step + masks[0]), 0)
    else:
        index = lambda step, at: (0, (at[0] ^ (step + masks[0])) * slots + slot)
    args = list(arrays)
    in_specs = [pl.BlockSpec(a.shape, lambda step, at, n=len(a.shape): (0,) * n) for a in args]
    aliases = {}
    if base is not None:
        args.append(base)
        in_specs.append(ANYWHERE)
        aliases = {len(args): 0}
    given = len(args)
    if base is None:
        big = run.after.size > MIB // 16
        args.append(pltpu.with_memory_space_constraint(run.after, pltpu.HBM) if big else run.after)
        in_specs.append(ANYWHERE)
    outs, out_specs, scratch = [pltpu.HBM(shape, f32)], [pl.BlockSpec((rows, cols), index)], []
    if small:
        for n in small[1]:
            outs.append(shaped(n, f32))
            out_specs.append(pl.BlockSpec(n, lambda step, at: (0, 0)))
        scratch = [pltpu.VMEM((PLANE * small[0], 4 * cols), f32)]
    got = pl.pallas_call(
        with_deps(kernel, len(args) - given, 1 + given), out_shape=tuple(outs),
        grid_spec=pltpu.PrefetchScalarGridSpec(
            num_scalar_prefetch=1, grid=(len(masks),), in_specs=in_specs, out_specs=tuple(out_specs), scratch_shapes=scratch,
        ),
        input_output_aliases=aliases,
        compiler_params=pltpu.CompilerParams(vmem_limit_bytes=24 * MIB), name=name,
    )(place.array, *args)
    run.after = got[-1]
    return got


def per_device(
    ends_in, lengths, norm_gain, in_weight, conv_weight, conv_bias, xproj_weight,
    dtproj_weight, dt_bias, a_log, d_skip, out_weight,
):
    section = lax.axis_index("section")
    first = section == 0
    width, e = norm_gain.shape[1], conv_bias.shape[1]
    states, taps, rank = a_log.shape[1], conv_weight.shape[1], dtproj_weight.shape[1]
    tokens = ends_in.shape[1] // 2
    micro = lengths.shape[0]

    def across(array, pairs=((0, 1), (1, 0))):
        return lax.ppermute(array, "section", pairs)

    in_recv = across(in_weight[0])
    halves = ends_in[0].reshape(2, tokens, width)
    mine = lax.dynamic_index_in_dim(halves, section, 0, keepdims=False)
    theirs = across(lax.dynamic_index_in_dim(halves, 1 - section, 0, keepdims=False))
    small_own = pack_params(a_log[0], conv_weight[0], conv_bias, dt_bias, d_skip, norm_gain)
    small_recv = across(small_own)
    xd_own = jnp.concatenate([xproj_weight[0].T, dtproj_weight[0]], axis=0)
    xd_recv = across(xd_own)
    out_recv = across(out_weight[0])
    my_lengths = lax.dynamic_slice_in_dim(lengths, section * (micro // 2), micro // 2, 0)
    weights = (in_weight[0], in_recv, xd_own, xd_recv, out_weight[0], out_recv)
    chip = lax.axis_index("dp")
    coords = jnp.stack([chip % PLANE, chip // PLANE % 2, chip // (2 * PLANE) % 2, section]).astype(jnp.int32)
    place = SimpleNamespace(array=coords, tokens=tokens)

    sends, backward_first = run_layers(
        coords, my_lengths, mine, theirs, small_own, small_recv, weights, states, taps, rank
    )

    def around(parts):
        return [parts[0]] + [swap_chips(parts[m], m) for m in range(1, PLANE)]

    part = e // PLANE
    run = Chain(None)
    h = SimpleNamespace()

    def pack_out():
        h.out_parts = around(sends)

    def layer_0():
        h.own, h.own_small, h.send, h.own_end, h.send_end = backward_first(run)
        h.small_rows = h.own_small.shape[0] // PLANE

    def out_across():
        out_other, send = other_layers(run, place, h.out_parts, h.send, width)
        h.out_other, h.other = across(out_other), across(send)

    def pack_low():
        parts = (("whole", 0), ("half", width, 2 * part))
        h.low_parts = around(pack(run, place, (h.own, h.other), parts, width, None, "pack_low"))

    def pack_high():
        small_at = (h.small_rows, h.own_small, h.own.shape[1])
        parts = (("half", width + part, 2 * part),)
        h.high_parts = around(pack(run, place, (h.own, h.other), parts, width, small_at, "pack_high"))

    def multiply(k):
        def step():
            if k == 0:
                h.sums0 = product_out(run, place, h.out_parts, h.out_other, width)
            elif k == 1:
                h.sums1 = product_in(run, place, h.low_parts, h.low_parts, 2 * tokens, 0, width, "product_low")
            else:
                h.sums2 = product_in(run, place, h.low_parts, h.high_parts, 0, h.small_rows, width, "product_high")

        return step

    def near_sum(k):
        def step():
            keep, send = getattr(h, f"sums{k}")
            setattr(h, f"near{k}", add_near(run, place, keep, swap_chips(send, PLANE)))

        return step

    def far_sum(k):
        def step():
            mine, send = getattr(h, f"near{k}")
            setattr(h, f"total{k}", add_far(run, place, mine, swap_chips(send, 2 * PLANE)))

        return step

    def pair(k):
        def step():
            total = getattr(h, f"total{k}")
            setattr(h, f"pair{k}", pair_up(run, place, total, swap_chips(total, 2 * PLANE)))

        return step

    def quarter_out():
        h.out_q = quarter_of(run, place, h.pair0, swap_chips(h.pair0, PLANE))
        h.rows_out = h.out_q.shape[2]
        h.out_x, h.out_y = swap_chips(h.out_q, 1), swap_chips(h.out_q, 2)

    def quarter_low():
        far = (h.out_x, h.out_y, lambda ref: [ref[0, 0], ref[0, 1]], lambda ref: [ref[1, 0], ref[1, 1]], h.out_q.size // 2)
        h.low_q, to_x, to_y = quarter_of(run, place, h.pair1, swap_chips(h.pair1, PLANE), far=far)
        h.rows_low = h.low_q.shape[2]
        h.low_x, h.low_y = swap_chips(to_x, 1), swap_chips(to_y, 2)

    def quarter_high():
        n = 2 * h.rows_low
        far = (h.low_x, h.low_y, lambda ref: [ref[0:n, :]], lambda ref: [ref[n:2 * n, :]], h.low_q.size // 2)
        h.high_q, to_x, to_y = quarter_of(run, place, h.pair2, swap_chips(h.pair2, PLANE), far=far)
        h.rows_high = h.high_q.shape[2]
        h.high_x, h.high_y = swap_chips(to_x, 1), swap_chips(to_y, 2)

    def last_far():
        low_half, high_half = far_halves(run, place, h.high_x, h.high_y, h.rows_high)
        h.far_low, h.far_high = swap_chips(low_half, 1), swap_chips(high_half, 2)

    def ends_step():
        h.ends = place_ends(run, place, h.own_end, across(h.send_end))[None]

    def find_out(refs, step, z):
        if step < 3:
            return refs[step][z // 2, z % 2]
        ref = refs[3 + z // 2]
        at_row = 4 * h.rows_low + (z % 2) * 2 * h.rows_out
        return jnp.concatenate([ref[at_row:at_row + h.rows_out, :], ref[at_row + h.rows_out:at_row + 2 * h.rows_out, :]], axis=1)

    def find_low(refs, step, z):
        if step == 0:
            return refs[0][z // 2, z % 2]
        if step < 3:
            return refs[step][z * h.rows_low:(z + 1) * h.rows_low, :]
        at_row = 4 * h.rows_high + (z % 2) * h.rows_low
        return refs[3 + z // 2][at_row:at_row + h.rows_low, :]

    def find_high(refs, step, z):
        if step == 0:
            return refs[0][z // 2, z % 2]
        at_row = (z if step < 3 else z % 2) * h.rows_high
        return refs[step if step < 3 else 3 + z // 2][at_row:at_row + h.rows_high, :]

    def write_out():
        arrays = (h.out_q, h.out_x, h.out_y, h.low_x, h.low_y)
        h.grad_out, = spread(run, place, arrays, find_out, (part, width), (e, width), True, 0, 1, None, None, "spread_out")

    def write_low():
        arrays = (h.low_q, h.low_x, h.low_y, h.high_x, h.high_y)
        h.grad_low, = spread(
            run, place, arrays, find_low, (width, part), (width, 2 * e), False, 0, 2, None, None, "spread_low"
        )

    def write_high():
        arrays = (h.high_q, h.high_x, h.high_y)
        h.grad_most, = spread(
            run, place, arrays, find_high, (width, part), (width, 2 * e), False, 1, 2, h.grad_low, None, "spread_high",
            range(PLANE - 1),
        )

    def write_rest():
        one = (1, e)
        low_rows = rank + 2 * states
        shapes = [(low_rows, e), (rank, e), (states, e), (taps, e), one, one, one, (1, width)]
        arrays = (h.high_q, h.high_x, h.high_y, h.far_low, h.far_high)
        h.last = spread(
            run, place, arrays, find_high, (width, part), (width, 2 * e), False, 1, 2, h.grad_most, (h.small_rows, shapes),
            "spread_rest", range(PLANE - 1, PLANE),
        )

    steps = {
        "pack_out": pack_out, "layer_0": layer_0, "across": out_across, "pack_low": pack_low,
        "pack_high": pack_high, "Q0": quarter_out, "Q1": quarter_low, "Q2": quarter_high, "far": last_far,
        "ends": ends_step, "W0": write_out, "W1": write_low, "W2": write_high, "W3": write_rest,
    }
    for k in range(3):
        steps.update({f"M{k}": multiply(k), f"A{k}": near_sum(k), f"F{k}": far_sum(k), f"P{k}": pair(k)})
    for name in ORDER:
        steps[name]()
    ends, grad_out = h.ends, h.grad_out
    grad_in, xproj, dtproj, alog, conv_w, conv_b, dt_b, dskip, gain = h.last
    return (
        ends, gain, grad_in[None], conv_w[None], conv_b, xproj.T[None], dtproj[None], dt_b, alog[None], dskip,
        grad_out[None],
    )


def solution(mesh):
    in_specs = (
        P("section", "dp", None), P("dp", None), P("section", None), P("section", None, None),
        P("section", None, None), P("section", None), P("section", None, None), P("section", None, None),
        P("section", None), P("section", None, None), P("section", None), P("section", None, None),
    )
    out_specs = (
        P("section", "dp", None), P("section", None), P("section", None, None), P("section", None, None),
        P("section", None), P("section", None, None), P("section", None, None), P("section", None),
        P("section", None, None), P("section", None), P("section", None, None),
    )
    return jax.shard_map(per_device, mesh=mesh, in_specs=in_specs, out_specs=out_specs, check_vma=False)
```

```python
from types import SimpleNamespace

import jax
import jax.numpy as jnp
from jax import lax
from jax.experimental import pallas as pl
from jax.experimental.pallas import tpu as pltpu
from jax.sharding import PartitionSpec as P

EPSILON = 1e-05
LOG2E = 1.4426950408889634
LN2 = 0.6931471805599453
CUT = 1e6
LANES = 128
WIDE = 512
GROUP = 8
PLANE = 4
MIB = 1024 * 1024

bf16, f32 = jnp.bfloat16, jnp.float32
VMEM = pl.BlockSpec(memory_space=pltpu.VMEM)
SMEM = pl.BlockSpec(memory_space=pltpu.SMEM)
ANYWHERE = pl.BlockSpec(memory_space=pl.ANY)


def shaped(shape, kind):
    return jax.ShapeDtypeStruct(shape, kind)


def nn(a, b):
    return jnp.dot(a, b, preferred_element_type=f32)


def nt(a, b):
    return lax.dot_general(a, b, (((1,), (1,)), ((), ())), preferred_element_type=f32)


def tn(a, b):
    return lax.dot_general(a, b, (((0,), (0,)), ((), ())), preferred_element_type=f32)


def sigmoid(v):
    return 1.0 / (1.0 + jnp.exp(-v))


def with_deps(kernel, n_deps, at):
    def wrapped(*refs):
        return kernel(*refs[:at], *refs[at + n_deps:])

    return wrapped


def call(kernel, outs, args, name, smem=1, deps=(), scratch=(), limit=16, cost=None):
    specs = [SMEM] * smem + [VMEM] * (len(args) - smem) + [ANYWHERE] * len(deps)
    return pl.pallas_call(
        with_deps(kernel, len(deps), len(args)), out_shape=outs, in_specs=specs,
        out_specs=jax.tree.map(lambda _: VMEM, outs), scratch_shapes=list(scratch), name=name,
        cost_estimate=cost or pl.CostEstimate(flops=1, bytes_accessed=1, transcendentals=0),
        compiler_params=pltpu.CompilerParams(vmem_limit_bytes=limit * MIB),
    )(*args, *deps)


def pack_params(a_log, conv_weight, conv_bias, dt_bias, d_skip, norm_gain):
    rows = sum(a.shape[-2] for a in (a_log, conv_weight, conv_bias, dt_bias, d_skip, norm_gain))
    e, width = d_skip.shape[1], norm_gain.shape[1]

    def kernel(*refs):
        out = refs[-1]
        at_row = 0
        for ref in refs[:-1]:
            n, columns = ref.shape
            out[at_row:at_row + n, 0:columns] = ref[...]
            at_row += n
        out[at_row - 1:at_row, width:] = jnp.zeros((1, e - width), f32)

    args = (a_log, conv_weight, conv_bias, dt_bias, d_skip, norm_gain)
    return call(kernel, shaped((rows, e), f32), args, "pack_params", smem=0)


def make_layers(tokens, width, e, states, taps, rank):
    steps_wide = e // WIDE
    tiles = WIDE // LANES
    low_rows = rank + 2 * states
    AL, CW, CB, DB, DS, GN = 0, states, states + taps, states + taps + 1, states + taps + 2, states + taps + 3
    GX, GD = 0, low_rows
    GA = GD + rank
    GC = GA + states
    GB, GT, GS, GG = GC + taps, GC + taps + 1, GC + taps + 2, GC + taps + 3

    def wide(i, base=0):
        return pl.ds(pl.multiple_of(i * WIDE + base, LANES), WIDE)

    def tile(i, k):
        return pl.ds(pl.multiple_of(i * WIDE + k * LANES, LANES), LANES)

    def of_state(t):
        return pl.ds(pl.multiple_of(t * states, states), states)

    def grouped(value):
        return value.reshape(tokens // GROUP, GROUP, value.shape[1])

    def flat(value):
        return value.reshape(tokens, value.shape[2])

    def half_sum(value):
        return sum(value[n * 8:(n + 1) * 8] for n in range(states // 8))

    def row_sums(rows, k):
        return sum(rows[k, pl.ds(n, GROUP, stride=8), :] for n in range(8))

    def chunks(sums, here):
        return sum(sums[i, here, :] for i in range(steps_wide))

    def keep(r, k):
        return jnp.concatenate([r.offs[...]] * tiles, axis=1) >= k

    def fill_offsets(offs, lengths):
        micro = lengths.shape[0]
        count = tokens // micro
        row = lax.broadcasted_iota(jnp.int32, (tokens, LANES), 0)
        begin = jnp.zeros_like(row)
        for m in range(micro):
            a = lengths[m, 0] + m * count
            b = a + lengths[m, 1]
            begin = jnp.where(row >= m * count, m * count, begin)
            begin = jnp.where(row >= a, a, begin)
            begin = jnp.where(row >= b, b, begin)
        offs[...] = row - begin

    def fill_rate(r, l):
        r.rate[l] = -jnp.exp(r.small[l, AL:AL + states, :]) * LOG2E

    def forward(l, r):
        x = r.resid[l]
        norm = lax.rsqrt(jnp.mean(x * x, axis=1, keepdims=True) + EPSILON)
        r.nrm[l] = (x * norm * r.small[l, GN:GN + 1, 0:width]).astype(bf16)

        def project(i, _):
            c = wide(i)
            r.arrived_in(i)
            v = nn(r.nrm[l], r.in_w[l, :, c])
            r.inner[l, :, c] = v
            r.gate[l, :, c] = nn(r.nrm[l], r.in_w[l, :, wide(i, e)])
            total = r.small[l, CB:CB + 1, c] + r.small[l, CW + taps - 1:CW + taps, c] * v
            for k in range(1, taps):
                before = jnp.where(keep(r, k), pltpu.roll(v, k, 0), 0.0)
                total = total + r.small[l, CW + taps - 1 - k:CW + taps - k, c] * before
            r.conv[l, :, c] = total
            r.act[l, :, c] = (total * sigmoid(total)).astype(bf16)
            return 0

        lax.fori_loop(0, steps_wide, project, 0)
        r.arrived(l, 1)
        a = r.act[l]
        low = nt(a, r.xd_w[l, 0:rank, :]).astype(bf16)
        proj_t = nt(r.xd_w[l, 0:low_rows, :], a)
        r.low_t[l] = proj_t[0:rank].astype(bf16)
        for t in range(tokens):
            here = slice(t * states, (t + 1) * states)
            r.bb[l, here, :] = jnp.broadcast_to(proj_t[rank:rank + states, t:t + 1], (states, LANES))
            r.cb[l, here, :] = jnp.broadcast_to(proj_t[rank + states:, t:t + 1], (states, LANES))
        fill_rate(r, l)

        def scan(i, _):
            c = wide(i)
            v = nn(low, r.xd_w[l, low_rows:low_rows + rank, c]) + r.small[l, DB:DB + 1, c]
            shrunk = jnp.exp(-jnp.abs(v))
            s = jnp.maximum(v, 0.0) + jnp.log1p(shrunk)
            inverse = 1.0 / (1.0 + shrunk)
            r.sig[l, :, c] = jnp.where(v >= 0, inverse, shrunk * inverse)
            r.step[l, :, c] = s
            r.uin[l, :, :, c] = grouped(s * r.act[l, :, c].astype(f32))
            r.size[l, :, :, c] = grouped(jnp.where(keep(r, 1), s, CUT))
            rates = [r.rate[l, :, tile(i, k)] for k in range(tiles)]

            def group(g, h):
                h = list(h)
                for j in range(GROUP):
                    t = g * GROUP + j
                    bt, ct = r.bb[l, of_state(t), :], r.cb[l, of_state(t), :]
                    for k in range(tiles):
                        f = jnp.exp2(r.size[l, g, j:j + 1, tile(i, k)] * rates[k])
                        h[k] = f * h[k] + bt * r.uin[l, g, j:j + 1, tile(i, k)]
                        r.hist[l, of_state(t + 1), tile(i, k)] = h[k]
                        r.rows_a[k, j * 8:(j + 1) * 8, :] = half_sum(ct * h[k])
                for k in range(tiles):
                    r.yscan[l, g, :, tile(i, k)] = row_sums(r.rows_a, k)
                return tuple(h)

            none = tuple(jnp.zeros((states, LANES), f32) for _ in range(tiles))
            lax.fori_loop(0, tokens // GROUP, group, none)
            z = r.gate[l, :, c]
            p = flat(r.yscan[l, :, :, c]) + r.small[l, DS:DS + 1, c] * r.act[l, :, c].astype(f32)
            r.gat[l, :, c] = (p * (z * sigmoid(z))).astype(bf16)
            return 0

        lax.fori_loop(0, steps_wide, scan, 0)
        r.arrived(l, 2)
        result = x + nn(r.gat[l], r.out_w[l])
        return result

    def backward(l, r):
        r.outg[...] = r.upstream[...].astype(bf16)
        rest = r.grads_o.shape[1] - GG
        r.grads_o[0, GG:, :] = jnp.zeros((rest, e), f32)

        def scan(i, _):
            c = wide(i)
            from_out = nt(r.outg[...], r.out_w[l, c, :])
            a = r.act[l, :, c].astype(f32)
            z = r.gate[l, :, c]
            s = sigmoid(z)
            p = flat(r.yscan[l, :, :, c]) + r.small[l, DS:DS + 1, c] * a
            dp = from_out * (z * s)
            r.dyscan[:, :, c] = grouped(dp)
            r.fi[:, wide(i, width + e)] = (from_out * p * (s * (1.0 + z * (1.0 - s)))).astype(bf16)
            r.grads_o[0, GS:GS + 1, c] = jnp.sum(dp * a, axis=0, keepdims=True)
            rates = [r.rate[l, :, tile(i, k)] for k in range(tiles)]

            def group(backwards, carried):
                carry, now, drate = (list(v) for v in carried)
                g = tokens // GROUP - 1 - backwards
                for j in reversed(range(GROUP)):
                    t = g * GROUP + j
                    bt, ct = r.bb[l, of_state(t), :], r.cb[l, of_state(t), :]
                    sum_b = sum_c = None
                    for k in range(tiles):
                        sz = r.size[l, g, j:j + 1, tile(i, k)]
                        dy = r.dyscan[g, j:j + 1, tile(i, k)]
                        grad = carry[k] + ct * dy
                        part_b = grad * r.uin[l, g, j:j + 1, tile(i, k)]
                        part_c = now[k] * dy
                        sum_b = part_b if sum_b is None else sum_b + part_b
                        sum_c = part_c if sum_c is None else sum_c + part_c
                        r.rows_a[k, j * 8:(j + 1) * 8, :] = half_sum(bt * grad)
                        carry[k] = jnp.exp2(sz * rates[k]) * grad
                        now[k] = r.hist[l, of_state(t), tile(i, k)]
                        w = carry[k] * now[k]
                        r.rows_b[k, j * 8:(j + 1) * 8, :] = half_sum(w * rates[k])
                        drate[k] = drate[k] + sz * w
                    r.acc_b[i, of_state(t), :] = sum_b
                    r.acc_c[i, of_state(t), :] = sum_c
                for k in range(tiles):
                    r.dact[g, :, tile(i, k)] = row_sums(r.rows_a, k)
                    r.dsz[g, :, tile(i, k)] = row_sums(r.rows_b, k)
                return tuple(carry), tuple(now), tuple(drate)

            none = tuple(jnp.zeros((states, LANES), f32) for _ in range(tiles))
            final = tuple(r.hist[l, of_state(tokens), tile(i, k)] for k in range(tiles))
            _, _, drate = lax.fori_loop(0, tokens // GROUP, group, (none, final, none))
            for k in range(tiles):
                r.grads_o[0, GA:GA + states, tile(i, k)] = drate[k] * (rates[k] * LN2)
            du = flat(r.dact[:, :, c])
            dv = (flat(r.dsz[:, :, c]) * LN2 + du * a) * r.sig[l, :, c]
            r.dact[:, :, c] = grouped(du * r.step[l, :, c] + dp * r.small[l, DS:DS + 1, c])
            r.dtg[:, c] = dv.astype(bf16)
            r.grads_o[0, GT:GT + 1, c] = jnp.sum(dv, axis=0, keepdims=True)
            return 0

        lax.fori_loop(0, steps_wide, scan, 0)
        lane = lax.broadcasted_iota(jnp.int32, (states, LANES), 1)
        db = jnp.zeros((states, LANES), f32)
        dc = jnp.zeros((states, LANES), f32)
        for t in range(tokens):
            here = slice(t * states, (t + 1) * states)
            db = jnp.where(lane == t, jnp.sum(chunks(r.acc_b, here), axis=1, keepdims=True), db)
            dc = jnp.where(lane == t, jnp.sum(chunks(r.acc_c, here), axis=1, keepdims=True), dc)
        r.pg_t[0:rank, :] = nt(r.xd_w[l, low_rows:low_rows + rank, :], r.dtg[...]).astype(bf16)
        r.pg_t[rank:rank + states, :] = db[:, 0:tokens].astype(bf16)
        r.pg_t[rank + states:low_rows, :] = dc[:, 0:tokens].astype(bf16)

        def conv_back(i, _):
            c = wide(i)
            r.grads_o[0, GX:GX + low_rows, c] = nn(r.pg_t[...], r.act[l, :, c])
            r.grads_o[0, GD:GD + rank, c] = nn(r.low_t[l], r.dtg[:, c])
            da = tn(r.pg_t[...], r.xd_w[l, 0:low_rows, c]) + flat(r.dact[:, :, c])
            total = r.conv[l, :, c]
            s = sigmoid(total)
            dv = da * (s * (1.0 + total * (1.0 - s)))
            v = r.inner[l, :, c]
            r.grads_o[0, GB:GB + 1, c] = jnp.sum(dv, axis=0, keepdims=True)
            r.grads_o[0, GC + taps - 1:GC + taps, c] = jnp.sum(dv * v, axis=0, keepdims=True)
            dinner = r.small[l, CW + taps - 1:CW + taps, c] * dv
            for k in range(1, taps):
                kept = jnp.where(keep(r, k), dv, 0.0)
                r.grads_o[0, GC + taps - 1 - k:GC + taps - k, c] = jnp.sum(
                    kept * pltpu.roll(v, k, 0), axis=0, keepdims=True
                )
                dinner = dinner + r.small[l, CW + taps - 1 - k:CW + taps - k, c] * pltpu.roll(kept, tokens - k, 0)
            r.fi[:, wide(i, width)] = dinner.astype(bf16)
            return 0

        lax.fori_loop(0, steps_wide, conv_back, 0)
        dn = nt(r.fi[:, width:width + 2 * e], r.in_w[l])
        x = r.resid[l]
        norm = lax.rsqrt(jnp.mean(x * x, axis=1, keepdims=True) + EPSILON)
        xr = x * norm
        r.grads_o[0, GG:GG + 1, 0:width] = jnp.sum(dn * xr, axis=0, keepdims=True)
        dxr = dn * r.small[l, GN:GN + 1, 0:width]
        grad_in = r.upstream[...] + norm * (dxr - xr * jnp.mean(dxr * xr, axis=1, keepdims=True))
        return grad_in

    def fetch(me, l, own, recv, dst, sem):
        @pl.when(me == l)
        def _():
            pltpu.make_async_copy(own, dst, sem).start()

        @pl.when(me != l)
        def _():
            pltpu.make_async_copy(recv, dst, sem).start()

    def forward_kernel(
        sec, lengths, mine, theirs, small_own, small_recv,
        in_own, in_recv, xd_own, xd_recv, out_own, out_recv, *refs,
    ):
        me = sec[3]
        n = len(STATE)
        first = SimpleNamespace(**dict(zip(STATE, refs[:n])))
        out_o, *sends, in_fac, grads, up_o = refs[n:n + 4 + PLANE]
        sems, in_sems, *rest = refs[n + 4 + PLANE:]
        last = SimpleNamespace(**dict(zip(STATE, rest[:n])))
        scratch = dict(zip(SCRATCH, rest[n:]))
        for l, r in enumerate((first, last)):
            r.__dict__.update(scratch)
            r.offs = first.offs
            weights = ((xd_own, xd_recv, r.xd_w), (out_own, out_recv, r.out_w))
            for i in range(2 * steps_wide):
                here = pl.ds((i % 2) * e + (i // 2) * WIDE, WIDE)
                fetch(me, l, in_own.at[:, here], in_recv.at[:, here], r.in_w.at[0, :, here], in_sems.at[l, i])
            for k, (own, recv, dst) in enumerate(weights):
                fetch(me, l, own, recv, dst.at[0], sems.at[l, k + 1])

            def arrived(_, k, l=l, weights=weights):
                own, _, dst = weights[k - 1]
                pltpu.make_async_copy(own, dst.at[0], sems.at[l, k]).wait()

            def arrived_in(i, l=l, r=r):
                for k in range(2):
                    here = wide(i, k * e)
                    pltpu.make_async_copy(in_own.at[:, here], r.in_w.at[0, :, here], in_sems.at[l, 2 * i + k]).wait()

            r.arrived_in = arrived_in
            r.arrived = arrived
            r.hist[0, 0:states, :] = jnp.zeros((states, e), f32)
        fill_offsets(first.offs, lengths)
        last.fi = in_fac
        for core in range(2):
            @pl.when(me == core)
            def _():
                own, other = (mine, theirs) if core == 0 else (theirs, mine)
                first.resid[0] = own[...].astype(f32)
                last.outg[...] = other[...]
                last.upstream[...] = other[...].astype(f32)
                for l, r in enumerate((first, last)):
                    r.small[0] = small_own[...] if l == core else small_recv[...]

        last.resid[0] = forward(0, first).astype(bf16).astype(f32)
        out_o[...] = forward(0, last)
        up = backward(0, last).astype(bf16)
        up_o[...] = up
        in_fac[:, 0:width] = last.nrm[0]
        grads[...] = last.grads_o[0].astype(bf16)
        for core in range(2):
            @pl.when(me == core)
            def _():
                layers = ((first.gat, up), (last.gat, last.outg[...]))[:: 1 if core == 0 else -1]
                part = e // PLANE
                for mask, send in enumerate(sends):
                    cols = pl.ds(pl.multiple_of((sec[0] ^ mask) * part, LANES), part)
                    for k, (gated, grad) in enumerate(layers):
                        send[k * tokens:(k + 1) * tokens, :] = grad
                        send[2 * tokens:3 * tokens, k * part:(k + 1) * part] = gated[0, :, cols]

    def backward_kernel(sec, up_in, out_in, in1, grads1, *refs):
        n = len(STATE)
        r = SimpleNamespace(**dict(zip(STATE, refs[:n])))
        own, own_small, send, own_end, send_end, in_fac, grads, gin, *rest = refs[n:]
        r.__dict__.update(zip(SCRATCH, rest))
        r.fi = in_fac
        r.outg[...] = up_in[...]
        r.upstream[...] = up_in[...].astype(f32)
        gin[...] = backward(0, r)
        in_fac[:, 0:width] = r.nrm[0]
        grads[...] = r.grads_o[0].astype(bf16)
        columns, block = in_fac.shape[1], grads.shape[0] // PLANE
        for core in range(2):
            @pl.when(sec[3] == core)
            def _():
                layers = ((in_fac, grads), (in1, grads1))
                mine, theirs = layers[core], layers[1 - core]
                own[...] = mine[0][...]
                own_small[...] = mine[1][...]
                own_end[...], send_end[...] = (gin[...], out_in[...]) if core == 0 else (out_in[...], gin[...])
                send[:, 0:columns] = theirs[0][...]
                for q in range(PLANE):
                    send[0:block, columns + q * e:columns + (q + 1) * e] = theirs[1][q * block:(q + 1) * block, :]

    grad_rows = (GG + 1 + 63) // 64 * 64
    return forward_kernel, backward_kernel, grad_rows


STATE = (
    "in_w", "xd_w", "out_w", "small", "offs", "resid", "nrm", "gat", "inner", "gate", "conv", "act",
    "size", "step", "sig", "yscan", "uin", "low_t", "bb", "cb", "rate", "hist",
)
SCRATCH = (
    "grads_o", "dyscan", "dact", "dsz", "dtg", "acc_b", "acc_c", "pg_t", "upstream", "outg", "rows_a", "rows_b",
)


def run_layers(section, lengths, mine, theirs, small_own, small_recv, weights, states, taps, rank):
    tokens, width = mine.shape
    in_w, _, xd_w, _, out_w, _ = weights
    e = out_w.shape[0]
    V = pltpu.VMEM
    forward, backward, grad_rows = make_layers(tokens, width, e, states, taps, rank)
    by_token = lambda kind=f32: V((1, tokens, e), kind)
    by_row = lambda *lead: V(lead + (tokens // GROUP, GROUP, e), f32)
    by_state = lambda *lead: V(lead + (tokens * states, LANES), f32)
    sums = lambda: V((WIDE // LANES, GROUP * 8, LANES), f32)
    state = (
        V((1,) + in_w.shape, bf16), V((1,) + xd_w.shape, bf16), V((1,) + out_w.shape, bf16),
        V((1,) + small_own.shape, f32), V((tokens, LANES), jnp.int32), V((1, tokens, width), f32),
        V((1, tokens, width), bf16), by_token(bf16), by_token(), by_token(), by_token(), by_token(bf16),
        by_row(1), by_token(), by_token(), by_row(1), by_row(1), V((1, rank, tokens), bf16),
        by_state(1), by_state(1), V((1, states, e), f32), V((1, (tokens + 1) * states, e), f32),
    )
    scratch = (
        V((1, grad_rows, e), f32), by_row(), by_row(), by_row(), V((tokens, e), bf16), by_state(e // WIDE), by_state(e // WIDE),
        V((rank + 2 * states, tokens), bf16), V((tokens, width), f32), V((tokens, width), bf16), sums(), sums(),
    )
    n = len(STATE)
    work = pl.CostEstimate(flops=1 << 30, bytes_accessed=30 * MIB, transcendentals=0)
    factors, grads = shaped((tokens, width + 2 * e), bf16), shaped((grad_rows, e), bf16)
    of_out = shaped((3 * tokens, width), bf16)
    outs = (V((tokens, width), f32),) + tuple(V(a.shape, bf16) for a in (*(of_out,) * PLANE, factors, grads, shaped((tokens, width), bf16)))
    here = lambda a, space: pltpu.with_memory_space_constraint(a, space)
    own_hbm = [here(a, pltpu.HBM) if k % 2 == 0 else a for k, a in enumerate(weights)]
    got = pl.pallas_call(
        forward, out_shape=state + outs,
        in_specs=[SMEM, SMEM] + [VMEM] * 4 + [ANYWHERE] * 6, out_specs=(VMEM,) * (n + len(outs)),
        scratch_shapes=[pltpu.SemaphoreType.DMA((2, 3)), pltpu.SemaphoreType.DMA((2, 2 * (e // WIDE))), *state, *scratch],
        compiler_params=pltpu.CompilerParams(vmem_limit_bytes=28 * MIB), name="forward_both", cost_estimate=work,
    )(section, lengths, mine, here(theirs, pltpu.VMEM), small_own, here(small_recv, pltpu.VMEM), *own_hbm)
    held = [here(a, pltpu.VMEM) for a in got[:n]]
    out, *sends, in1, grads1, up = got[n:]

    def rest(run):
        end = shaped((tokens, width), f32)
        outs = (factors, grads, shaped((tokens, factors.shape[1] + PLANE * e), bf16), end, end)
        inner_scratch = (V(factors.shape, bf16), V(grads.shape, bf16), V(end.shape, f32)) + scratch
        args = (section, up, out, in1, grads1, *held)
        return run(backward, outs, args, "backward_first", scratch=inner_scratch, limit=16, cost=work)

    return sends, rest


def swap_chips(array, mask):
    chips = lax.axis_size("dp")
    return lax.ppermute(array, "dp", [(i, i ^ mask) for i in range(chips)])


ORDER = (
    "pack_out", "layer_0", "across", "M0", "pack_low", "A0", "F0", "M1", "pack_high",
    "P0", "A1", "M2", "Q0", "F1", "P1", "A2", "F2", "Q1",
    "P2", "Q2", "ends", "W0", "far", "W1", "W2", "W3",
)


class Chain:
    def __init__(self, after):
        self.after = after

    def __call__(self, kernel, outs, args, name, deps=(), **options):
        if self.after is not None:
            after = self.after
            if after.dtype == f32 and after.size > MIB // 16:
                after = pltpu.with_memory_space_constraint(after, pltpu.HBM)
            deps = (after, *deps)
        got = call(kernel, outs, args, name, deps=deps, **options)
        self.after = jax.tree.leaves(got)[-1]
        return got


def pack(run, place, sides, parts, width, rows_more, name):
    tokens = place.tokens
    half = width // 2
    rows = sum(tokens if kind == "half" else 2 * tokens for kind, *_ in parts)
    given = list(sides)
    if rows_more:
        small_rows, own_small, column_small = rows_more
        rows += 2 * small_rows
        given.append(own_small)

    def kernel(at, *refs):
        first, second = refs[:2]
        outs = refs[len(given):]
        for mask in range(PLANE):
            q = at[0] ^ mask
            out = outs[mask]
            base = 0
            for kind, column, *stride in parts:
                for k, side in enumerate((first, second)):
                    if kind == "whole":
                        out[base + k * tokens:base + (k + 1) * tokens, :] = side[:, column:column + width]
                    else:
                        cols = pl.ds(pl.multiple_of(column + q * stride[0], LANES), half)
                        out[base:base + tokens, k * half:(k + 1) * half] = side[:, cols]
                base += tokens if kind == "half" else 2 * tokens
            if rows_more:
                block = pl.ds(pl.multiple_of(q * small_rows, 16), small_rows)
                for k in range(2):
                    cols = slice(k * width, (k + 1) * width)
                    there = pl.ds(pl.multiple_of(column_small + q * 2 * width + k * width, LANES), width)
                    total = refs[2][block, cols].astype(f32) + second[0:small_rows, there].astype(f32)
                    out[base:base + small_rows, :] = total.astype(bf16)
                    base += small_rows

    return run(kernel, (shaped((rows, width), bf16),) * PLANE, (place.array, *given), name)


def place_ends(run, place, own, came):
    tokens, width = own.shape

    def kernel(at, own, came, out):
        for core in range(2):
            @pl.when(at[3] == core)
            def _():
                out[core * tokens:(core + 1) * tokens, :] = own[...]
                out[(1 - core) * tokens:(2 - core) * tokens, :] = came[...]

    return run(kernel, shaped((2 * tokens, width), f32), (place.array, own, came), "place_ends")


def other_layers(run, place, parts, width):
    tokens, half = place.tokens, width // 2

    def kernel(at, *refs):
        out = refs[-1]
        for k, ref in enumerate(refs[:-1]):
            out[k * tokens:(k + 1) * tokens, :] = ref[tokens:2 * tokens, :]
            at_row = (PLANE + k // 2) * tokens
            out[at_row:at_row + tokens, (k % 2) * half:(k % 2 + 1) * half] = ref[2 * tokens:3 * tokens, half:width]

    return run(kernel, shaped((PLANE * tokens * 3 // 2, width), bf16), (place.array, *parts), "other_layers")


def store_sums(at, total, keep, send):
    b0 = at[1]
    for j in range(2):
        keep[j] = total[j, b0]
        send[j] = total[j, 1 - b0].astype(bf16)


def product_out(run, place, parts, came, across, width):
    tokens, half = place.tokens, width // 2
    many = 2 * PLANE * tokens
    shape = (2, half // 4, width)

    def kernel(at, *refs):
        came, (keep, send, _, left, right, total) = refs[PLANE], refs[-6:]
        for k, ref in enumerate(refs[:PLANE]):
            right[k * tokens:(k + 1) * tokens, :] = ref[0:tokens, :]
            left[k * tokens:(k + 1) * tokens, :] = ref[2 * tokens:3 * tokens, 0:half]
            there = (PLANE + k) * tokens
            right[there:there + tokens, :] = came[k * tokens:(k + 1) * tokens, :]
            at_row = (PLANE + k // 2) * tokens
            left[there:there + tokens, :] = came[at_row:at_row + tokens, (k % 2) * half:(k % 2 + 1) * half]
        total[...] = tn(left[...], right[...]).reshape(2, *shape)
        store_sums(at, total, keep, send)

    V = pltpu.VMEM
    keep, run.after, across = pl.pallas_call(
        kernel, out_shape=(shaped(shape, f32), shaped(shape, bf16), shaped(across.shape, bf16)),
        in_specs=[SMEM] + [VMEM] * (PLANE + 1) + [ANYWHERE] * 2, out_specs=(VMEM, VMEM, ANYWHERE),
        scratch_shapes=[V((many, half), bf16), V((many, width), bf16), V((2,) + shape, f32)],
        input_output_aliases={PLANE + 2: 2}, name="product_out",
        cost_estimate=pl.CostEstimate(flops=1, bytes_accessed=1, transcendentals=0),
        compiler_params=pltpu.CompilerParams(vmem_limit_bytes=16 * MIB),
    )(place.array, *parts, came, across, run.after)
    return keep, run.after, across


def product_in(run, place, tall, thin, base, small_rows, width, name):
    tokens, half = place.tokens, width // 2
    many = 2 * PLANE * tokens
    shard = width // 4
    shape = (2, shard + small_rows, half)
    args = (place.array, *tall) + (() if thin is tall else tuple(thin))

    def kernel(at, *refs):
        ins, (keep, send, left, right, total) = refs[:-5], refs[-5:]
        for k in range(PLANE):
            side = ins[-PLANE + k]
            left[2 * k * tokens:2 * (k + 1) * tokens, :] = ins[k][0:2 * tokens, :]
            for j in range(2):
                here = slice((2 * k + j) * tokens, (2 * k + j + 1) * tokens)
                right[here, :] = side[base:base + tokens, j * half:(j + 1) * half]
        total[:, :, 0:shard, :] = tn(left[...], right[...]).reshape(2, 2, shard, half)
        if small_rows:
            end = base + tokens
            mixed = sum(ins[-PLANE + k][end:end + 2 * small_rows, :].astype(f32) for k in range(PLANE))
            for b1 in range(2):
                for b0 in range(2):
                    block = mixed[b1 * small_rows:(b1 + 1) * small_rows, b0 * half:(b0 + 1) * half]
                    total[b1, b0, shard:, :] = block
        store_sums(at, total, keep, send)

    V = pltpu.VMEM
    scratch = [V((many, width), bf16), V((many, half), bf16), V((2,) + shape, f32)]
    return run(kernel, (shaped(shape, f32), shaped(shape, bf16)), args, name, scratch=scratch)


def add_near(run, place, keep, came):
    def kernel(at, keep, came, mine, send):
        b1 = at[2]
        mine[...] = keep[b1] + came[b1].astype(f32)
        send[...] = (keep[1 - b1] + came[1 - b1].astype(f32)).astype(bf16)

    shape = keep.shape[1:]
    return run(kernel, (shaped(shape, f32), shaped(shape, bf16)), (place.array, keep, came), "add_near")


def add_far(run, place, mine, came):
    def kernel(at, mine, came, out):
        out[...] = (mine[...].astype(f32) + came[...].astype(f32)).astype(bf16)

    total = run(kernel, shaped(mine.shape, bf16), (place.array, mine, came), "add_far")
    mask = 4 * PLANE
    while mask < lax.axis_size("dp"):
        total = run(kernel, shaped(mine.shape, bf16), (place.array, total, swap_chips(total, mask)), "add_far")
        mask *= 2
    return total


def pair_up(run, place, own, came):
    def kernel(at, own, came, out):
        b1 = at[2]
        out[b1] = own[...]
        out[1 - b1] = came[...]

    return run(kernel, shaped((2,) + own.shape, bf16), (place.array, own, came), "pair_up")


def quarter_of(run, place, own, came, far=None):
    rows, cols = own.shape[1:]

    def kernel(at, own, came, *rest):
        b0 = at[1]
        out = rest[0] if far is None else rest[2]
        for j in range(2):
            out[j, b0] = own[j]
            out[j, 1 - b0] = came[j]
        if far is not None:
            by_x, by_y, out, to_x, to_y = rest
            for to, ref, cut in ((to_x, by_y, far[2]), (to_y, by_x, far[3])):
                for j in range(2):
                    for i in range(2):
                        to[(2 * j + i) * rows:(2 * j + i + 1) * rows, :] = out[j, i]
                at_row = 4 * rows
                for piece in cut(ref):
                    for column in range(0, piece.shape[1], cols):
                        to[at_row:at_row + piece.shape[0], :] = piece[:, column:column + cols]
                        at_row += piece.shape[0]

    outs = shaped((2, 2, rows, cols), bf16)
    args = (place.array, own, came)
    if far is not None:
        sent = shaped((4 * rows + far[4] // cols, cols), bf16)
        outs, args = (outs, sent, sent), args + tuple(far[:2])
    return run(kernel, outs, args, "quarter_of")


def far_halves(run, place, by_x, by_y, rows):
    cols = by_x.shape[1]

    def kernel(at, by_x, by_y, low, high):
        low[...] = by_y[0:2 * rows, :]
        high[...] = by_x[2 * rows:4 * rows, :]

    return run(kernel, (shaped((2 * rows, cols), bf16),) * 2, (place.array, by_x, by_y), "far_halves")


def spread(run, place, arrays, find, columns, shape, by_rows, slot, slots, base, small, name, masks=range(PLANE)):
    rows, cols = columns
    shard = rows // 4

    def kernel(at, *refs):
        ins, rest = refs[:len(arrays)], refs[len(arrays):]
        rest = rest[1 if base is not None else 0:]
        out, outs = rest[0], rest[1:]
        step = pl.program_id(0)
        for k in masks:
            @pl.when(step == k - masks[0])
            def _(k=k):
                for z in range(4):
                    out[z * shard:(z + 1) * shard, :] = find(ins, k, z)[0:shard, :].astype(f32)

        if small:
            for k in range(PLANE):
                block = pl.ds(pl.multiple_of((at[0] ^ k) * small[0], 8), small[0])
                for z in range(4):
                    outs[-1][block, z * cols:(z + 1) * cols] = find(ins, k, z)[shard:, :].astype(f32)
            at_row = 0
            for out_s in outs[:-1]:
                n = out_s.shape[0]
                out_s[...] = outs[-1][at_row:at_row + n, 0:out_s.shape[1]]
                at_row += n

    if by_rows:
        index = lambda step, at: (at[0] ^ (step + masks[0]), 0)
    else:
        index = lambda step, at: (0, (at[0] ^ (step + masks[0])) * slots + slot)
    args = list(arrays)
    in_specs = [pl.BlockSpec(a.shape, lambda step, at, n=len(a.shape): (0,) * n) for a in args]
    aliases = {}
    if base is not None:
        args.append(base)
        in_specs.append(ANYWHERE)
        aliases = {len(args): 0}
    given = len(args)
    if base is None:
        big = run.after.size > MIB // 16
        args.append(pltpu.with_memory_space_constraint(run.after, pltpu.HBM) if big else run.after)
        in_specs.append(ANYWHERE)
    outs, out_specs, scratch = [pltpu.HBM(shape, f32)], [pl.BlockSpec((rows, cols), index)], []
    if small:
        for n in small[1]:
            outs.append(shaped(n, f32))
            out_specs.append(pl.BlockSpec(n, lambda step, at: (0, 0)))
        scratch = [pltpu.VMEM((PLANE * small[0], 4 * cols), f32)]
    got = pl.pallas_call(
        with_deps(kernel, len(args) - given, 1 + given), out_shape=tuple(outs),
        grid_spec=pltpu.PrefetchScalarGridSpec(
            num_scalar_prefetch=1, grid=(len(masks),), in_specs=in_specs, out_specs=tuple(out_specs), scratch_shapes=scratch,
        ),
        input_output_aliases=aliases,
        compiler_params=pltpu.CompilerParams(vmem_limit_bytes=24 * MIB), name=name,
    )(place.array, *args)
    run.after = got[-1]
    return got


def per_device(
    ends_in, lengths, norm_gain, in_weight, conv_weight, conv_bias, xproj_weight,
    dtproj_weight, dt_bias, a_log, d_skip, out_weight,
):
    section = lax.axis_index("section")
    first = section == 0
    width, e = norm_gain.shape[1], conv_bias.shape[1]
    states, taps, rank = a_log.shape[1], conv_weight.shape[1], dtproj_weight.shape[1]
    tokens = ends_in.shape[1] // 2
    micro = lengths.shape[0]

    def across(array, pairs=((0, 1), (1, 0))):
        return lax.ppermute(array, "section", pairs)

    in_recv = across(in_weight[0])
    halves = ends_in[0].reshape(2, tokens, width)
    mine = lax.dynamic_index_in_dim(halves, section, 0, keepdims=False)
    theirs = across(lax.dynamic_index_in_dim(halves, 1 - section, 0, keepdims=False))
    small_own = pack_params(a_log[0], conv_weight[0], conv_bias, dt_bias, d_skip, norm_gain)
    small_recv = across(small_own)
    xd_own = jnp.concatenate([xproj_weight[0].T, dtproj_weight[0]], axis=0)
    xd_recv = across(xd_own)
    out_recv = across(out_weight[0])
    my_lengths = lax.dynamic_slice_in_dim(lengths, section * (micro // 2), micro // 2, 0)
    weights = (in_weight[0], in_recv, xd_own, xd_recv, out_weight[0], out_recv)
    chip = lax.axis_index("dp")
    coords = jnp.stack([chip % PLANE, chip // PLANE % 2, chip // (2 * PLANE) % 2, section]).astype(jnp.int32)
    place = SimpleNamespace(array=coords, tokens=tokens)

    sends, backward_first = run_layers(
        coords, my_lengths, mine, theirs, small_own, small_recv, weights, states, taps, rank
    )

    def around(parts):
        return [parts[0]] + [swap_chips(parts[m], m) for m in range(1, PLANE)]

    part = e // PLANE
    run = Chain(None)
    h = SimpleNamespace()

    def pack_out():
        h.out_parts = around(sends)

    def layer_0():
        h.own, h.own_small, h.send, h.own_end, h.send_end = backward_first(run)
        h.small_rows = h.own_small.shape[0] // PLANE

    def out_across():
        h.out_other = across(other_layers(run, place, h.out_parts, width))

    def pack_low():
        parts = (("whole", 0), ("half", width, 2 * part))
        h.low_parts = around(pack(run, place, (h.own, h.other), parts, width, None, "pack_low"))

    def pack_high():
        small_at = (h.small_rows, h.own_small, h.own.shape[1])
        parts = (("half", width + part, 2 * part),)
        h.high_parts = around(pack(run, place, (h.own, h.other), parts, width, small_at, "pack_high"))

    def multiply(k):
        def step():
            if k == 0:
                *h.sums0, send = product_out(run, place, h.out_parts, h.out_other, h.send, width)
                h.other = across(send)
            elif k == 1:
                h.sums1 = product_in(run, place, h.low_parts, h.low_parts, 2 * tokens, 0, width, "product_low")
            else:
                h.sums2 = product_in(run, place, h.low_parts, h.high_parts, 0, h.small_rows, width, "product_high")

        return step

    def near_sum(k):
        def step():
            keep, send = getattr(h, f"sums{k}")
            setattr(h, f"near{k}", add_near(run, place, keep, swap_chips(send, PLANE)))

        return step

    def far_sum(k):
        def step():
            mine, send = getattr(h, f"near{k}")
            setattr(h, f"total{k}", add_far(run, place, mine, swap_chips(send, 2 * PLANE)))

        return step

    def pair(k):
        def step():
            total = getattr(h, f"total{k}")
            setattr(h, f"pair{k}", pair_up(run, place, total, swap_chips(total, 2 * PLANE)))

        return step

    def quarter_out():
        h.out_q = quarter_of(run, place, h.pair0, swap_chips(h.pair0, PLANE))
        h.rows_out = h.out_q.shape[2]
        h.out_x, h.out_y = swap_chips(h.out_q, 1), swap_chips(h.out_q, 2)

    def quarter_low():
        far = (h.out_x, h.out_y, lambda ref: [ref[0, 0], ref[0, 1]], lambda ref: [ref[1, 0], ref[1, 1]], h.out_q.size // 2)
        h.low_q, to_x, to_y = quarter_of(run, place, h.pair1, swap_chips(h.pair1, PLANE), far=far)
        h.rows_low = h.low_q.shape[2]
        h.low_x, h.low_y = swap_chips(to_x, 1), swap_chips(to_y, 2)

    def quarter_high():
        n = 2 * h.rows_low
        far = (h.low_x, h.low_y, lambda ref: [ref[0:n, :]], lambda ref: [ref[n:2 * n, :]], h.low_q.size // 2)
        h.high_q, to_x, to_y = quarter_of(run, place, h.pair2, swap_chips(h.pair2, PLANE), far=far)
        h.rows_high = h.high_q.shape[2]
        h.high_x, h.high_y = swap_chips(to_x, 1), swap_chips(to_y, 2)

    def last_far():
        low_half, high_half = far_halves(run, place, h.high_x, h.high_y, h.rows_high)
        h.far_low, h.far_high = swap_chips(low_half, 1), swap_chips(high_half, 2)

    def ends_step():
        h.ends = place_ends(run, place, h.own_end, across(h.send_end))[None]

    def find_out(refs, step, z):
        if step < 3:
            return refs[step][z // 2, z % 2]
        ref = refs[3 + z // 2]
        at_row = 4 * h.rows_low + (z % 2) * 2 * h.rows_out
        return jnp.concatenate([ref[at_row:at_row + h.rows_out, :], ref[at_row + h.rows_out:at_row + 2 * h.rows_out, :]], axis=1)

    def find_low(refs, step, z):
        if step == 0:
            return refs[0][z // 2, z % 2]
        if step < 3:
            return refs[step][z * h.rows_low:(z + 1) * h.rows_low, :]
        at_row = 4 * h.rows_high + (z % 2) * h.rows_low
        return refs[3 + z // 2][at_row:at_row + h.rows_low, :]

    def find_high(refs, step, z):
        if step == 0:
            return refs[0][z // 2, z % 2]
        at_row = (z if step < 3 else z % 2) * h.rows_high
        return refs[step if step < 3 else 3 + z // 2][at_row:at_row + h.rows_high, :]

    def write_out():
        arrays = (h.out_q, h.out_x, h.out_y, h.low_x, h.low_y)
        h.grad_out, = spread(run, place, arrays, find_out, (part, width), (e, width), True, 0, 1, None, None, "spread_out")

    def write_low():
        arrays = (h.low_q, h.low_x, h.low_y, h.high_x, h.high_y)
        h.grad_low, = spread(
            run, place, arrays, find_low, (width, part), (width, 2 * e), False, 0, 2, None, None, "spread_low"
        )

    def write_high():
        arrays = (h.high_q, h.high_x, h.high_y)
        h.grad_most, = spread(
            run, place, arrays, find_high, (width, part), (width, 2 * e), False, 1, 2, h.grad_low, None, "spread_high",
            range(PLANE - 1),
        )

    def write_rest():
        one = (1, e)
        low_rows = rank + 2 * states
        shapes = [(low_rows, e), (rank, e), (states, e), (taps, e), one, one, one, (1, width)]
        arrays = (h.high_q, h.high_x, h.high_y, h.far_low, h.far_high)
        h.last = spread(
            run, place, arrays, find_high, (width, part), (width, 2 * e), False, 1, 2, h.grad_most, (h.small_rows, shapes),
            "spread_rest", range(PLANE - 1, PLANE),
        )

    steps = {
        "pack_out": pack_out, "layer_0": layer_0, "across": out_across, "pack_low": pack_low,
        "pack_high": pack_high, "Q0": quarter_out, "Q1": quarter_low, "Q2": quarter_high, "far": last_far,
        "ends": ends_step, "W0": write_out, "W1": write_low, "W2": write_high, "W3": write_rest,
    }
    for k in range(3):
        steps.update({f"M{k}": multiply(k), f"A{k}": near_sum(k), f"F{k}": far_sum(k), f"P{k}": pair(k)})
    for name in ORDER:
        steps[name]()
    ends, grad_out = h.ends, h.grad_out
    grad_in, xproj, dtproj, alog, conv_w, conv_b, dt_b, dskip, gain = h.last
    return (
        ends, gain, grad_in[None], conv_w[None], conv_b, xproj.T[None], dtproj[None], dt_b, alog[None], dskip,
        grad_out[None],
    )


def solution(mesh):
    in_specs = (
        P("section", "dp", None), P("dp", None), P("section", None), P("section", None, None),
        P("section", None, None), P("section", None), P("section", None, None), P("section", None, None),
        P("section", None), P("section", None, None), P("section", None), P("section", None, None),
    )
    out_specs = (
        P("section", "dp", None), P("section", None), P("section", None, None), P("section", None, None),
        P("section", None), P("section", None, None), P("section", None, None), P("section", None),
        P("section", None, None), P("section", None), P("section", None, None),
    )
    return jax.shard_map(per_device, mesh=mesh, in_specs=in_specs, out_specs=out_specs, check_vma=False)
```
